256 devices in a mesh: section: 8 (over y, x_lo), dp: 32 (over x_hi, z, core).
Axes of the slice: x: 4 (x_hi: 2, x_lo: 2; x = x_hi * 2 + x_lo), y: 4, z: 8, core: 2. Of those that a mesh axis runs over, the one named last changes fastest.
Arguments:
- embedded: bfloat16 [16384, 2048], P('dp'), may hold values from -6 to 6
- out_grad: bfloat16 [16384, 2048], P('dp'), may hold values from -0.046875 to 0.046875
- stored: bfloat16 [8, 2, 384, 64, 2048], P('section', None, 'dp'), as said below
- sample_ids: int32 [384], P('dp'), may hold values from 0 to 11, as said below
- lengths: int32 [384], P('dp'), may hold values from 1 to 64, as said below
- weight: bfloat16 [8, 2048, 2048], P('section', 'dp'), may hold values from -0.125 to 0.125
- gain: bfloat16 [8, 2048], P('section'), may hold values from 0.099609375 to 1.8984375
Outputs:
- boundary: bfloat16 [8, 16384, 2048], P('section', 'dp')
- weight_grad: float32 [8, 2048, 2048], P('section', 'dp')
The draws below stay inside these ranges and needn't reach their ends.
Inputs may be any that keep to these rules, and one draw needn't show every extreme that they name: stored[s, 1] equals stored[s + 1, 0] for every s below the last block. `sample_ids`: within each data group's 12 entries every slot 0 to 11 appears once. In each data group the first 4 lengths (long bucket) lie in 33 to 64 and the rest in 1 to 32; each group has a long sample of length 64 and a short one of length 32.
All inputs are finite; a program needn't handle non-finite values.
Results may differ from the reference program's by a relative error of at most 0.027.
Values may be sent and summed in bfloat16 or wider, within the bound.
No kernel may reach another device: no remote copies, remote signals or barrier semaphores. Data moves between devices by JAX's collectives and lax.ppermute only.
A program may use at most 128 MiB of HBM per device.

```python
import jax
import jax.numpy as jnp
from jax import lax

D = 2048
QB = 128
LEN_A = 64
SPM_A = 1
MICRO = 4
LEN_B = 32
SPM_B = 2
SAMP = 12
TOKENS = 16384
N_SECTION = 8
N_DP = 32


def draw_stored(key, part):
    key = jax.random.fold_in(key, 11)
    base = jax.random.normal(key, (N_SECTION + 1, N_DP * SAMP, LEN_A, D), jnp.float32).astype(jnp.bfloat16)
    return jnp.stack([base[:-1], base[1:]], axis=1)


def draw_sample_ids(key, part):
    key = jax.random.fold_in(key, 12)
    group_keys = jax.random.split(key, N_DP)

    def one_group(group_key):
        return jax.random.permutation(group_key, SAMP)
    return jax.vmap(one_group)(group_keys).reshape(-1).astype(jnp.int32)


def draw_lengths(key, part):
    key = jax.random.fold_in(key, 13)
    key_long, key_short, pick_long_key, pick_short_key = jax.random.split(key, 4)
    count_long = MICRO * SPM_A
    count_short = MICRO * SPM_B
    long_len = jax.random.randint(key_long, (N_DP, count_long), LEN_B + 1, LEN_A + 1)
    short_len = jax.random.randint(key_short, (N_DP, count_short), 1, LEN_B + 1)
    pick_long = jax.random.randint(pick_long_key, (N_DP, 1), 0, count_long)
    pick_short = jax.random.randint(pick_short_key, (N_DP, 1), 0, count_short)
    long_len = jnp.where(jnp.arange(count_long)[None, :] == pick_long, LEN_A, long_len)
    short_len = jnp.where(jnp.arange(count_short)[None, :] == pick_short, LEN_B, short_len)
    return jnp.concatenate([long_len, short_len], axis=1).reshape(-1).astype(jnp.int32)


def raised(drawn, stream_key, source, target, shards_of, factor):
    owner, partner = [(jnp.arange(drawn.shape[position]) // (drawn.shape[position] // shards_of)).reshape([-1 if axis == position else 1 for axis in range(drawn.ndim)]) for position in (source, target)]
    chosen = jax.random.permutation(stream_key, shards_of)[partner]
    strong = (owner == chosen) | (owner == (partner + shards_of // 2) % shards_of)
    return jnp.where(strong, factor * drawn, drawn)


def shard_levels(own_key, shape, pieces, least, largest):
    def one(dim, parts):
        heights = jax.random.uniform(jax.random.fold_in(jax.random.fold_in(own_key, 6), dim), (parts,), jnp.float32, least / len(pieces), largest / len(pieces))
        return jnp.repeat(jnp.exp(heights), shape[dim] // parts).reshape((-1,) + (1,) * (len(shape) - dim - 1))

    factor_of = one(*pieces[0])
    for cut in pieces[1:]:
        factor_of = factor_of * one(*cut)
    return factor_of


def gaussian(key, shape, scale, bound, cuts=(), kind=jnp.bfloat16):
    entries = jax.random.normal(key, shape, jnp.float32) * scale
    if len(cuts) > 0:
        entries = shard_levels(key, shape, cuts, -0.22, 0.18) * entries
    return jnp.clip(entries, min=-bound, max=bound).astype(kind)


def heavy_noise(key, shape, deviation, reach, pieces, heavy, kind=jnp.bfloat16):
    values = deviation * jax.random.normal(key, shape, jnp.float32)
    if pieces:
        values = values * shard_levels(key, shape, pieces, -0.22, 0.18)
    return jnp.clip(raised(values, jax.random.fold_in(key, 3), *heavy), -reach, reach).astype(kind)


def setup_inputs(seed: int = 0) -> dict:
    streams_of = jax.random.split(jax.random.key(seed), 8)
    embedded = heavy_noise(streams_of[0], (TOKENS, D), 1.0, 6.0, ((0, 32),), (0, 1, 32, 2.75))
    out_grad = gaussian(streams_of[1], (TOKENS, D), (TOKENS ** -0.5), 0.046875, ((0, 32),))
    stored = draw_stored(jax.random.fold_in(streams_of[7], 71), 0)
    sample_ids = draw_sample_ids(jax.random.fold_in(streams_of[7], 71), 0)
    lengths = draw_lengths(jax.random.fold_in(streams_of[7], 71), 0)
    weight = gaussian(streams_of[5], (N_SECTION, D, D), D ** -0.5, 0.125, ((0, 8), (1, 32)))
    gain = jnp.clip(1.0 + 0.18 * jax.random.normal(streams_of[6], (N_SECTION, D), jnp.float32), 0.099609375, 1.8984375).astype(jnp.bfloat16)
    return {"embedded": embedded, "out_grad": out_grad, "stored": stored, "sample_ids": sample_ids, "lengths": lengths, "weight": weight, "gain": gain}


eps_norm = 1e-06
eps_scale = 1e-06

def quantize(values, block_size):
    row_count, feature_count = values.shape
    grouped = values.reshape(row_count, feature_count // block_size, block_size)
    scaling = (lax.optimization_barrier(jnp.max(jnp.abs(grouped), axis=2)) / 127.0 + eps_scale).astype(jnp.bfloat16)
    encoded = (grouped / scaling.astype(jnp.float32)[:, :, None]).astype(jnp.bfloat16)
    return (encoded.reshape(row_count, feature_count), scaling)

def restore(encoded, scaling, block_size):
    row_count, feature_count = encoded.shape
    grouped = encoded.astype(jnp.float32).reshape(row_count, feature_count // block_size, block_size)
    return (grouped * scaling.astype(jnp.float32)[:, :, None]).reshape(row_count, feature_count)

def normalize(block_in, gain_row):
    values = block_in.astype(jnp.float32)
    inverse = lax.rsqrt(lax.optimization_barrier(jnp.mean(values * values, axis=1, keepdims=True)) + eps_norm)
    return (values, inverse, values * inverse * gain_row)

def slot_rows(slot_data, slot_ids):
    count_long = MICRO * SPM_A
    feature_count = slot_data.shape[2]
    long_part = jnp.take(slot_data, slot_ids[:count_long], axis=0).reshape(-1, feature_count)
    short_part = jnp.take(slot_data, slot_ids[count_long:], axis=0)[:, :LEN_B].reshape(-1, feature_count)
    return jnp.concatenate([long_part, short_part], axis=0)

def live_rows(sample_len):
    count_long = MICRO * SPM_A
    count_short = sample_len.shape[0] - count_long
    place_long = jnp.tile(jnp.arange(LEN_A, dtype=jnp.int32), count_long)
    place_short = jnp.tile(jnp.arange(LEN_B, dtype=jnp.int32), count_short)
    limit_long = jnp.repeat(sample_len[:count_long], LEN_A)
    limit_short = jnp.repeat(sample_len[count_long:], LEN_B)
    return jnp.concatenate([place_long < limit_long, place_short < limit_short])

def group_sum(normed, slope):
    feature_count = normed.shape[1]
    left_rows = normed.reshape(N_DP, -1, feature_count)
    right_rows = slope.reshape(N_DP, -1, feature_count)

    def add_group(running, operands):
        product = lax.dot_general(operands[0], operands[1], (((0,), (0,)), ((), ())), preferred_element_type=jnp.float32)
        rounded = lax.optimization_barrier(product.astype(jnp.bfloat16))
        return (running + rounded.astype(jnp.float32), None)
    running, _ = lax.scan(add_group, jnp.zeros((feature_count, feature_count), jnp.float32), (left_rows, right_rows))
    return running

def reference(embedded, out_grad, stored, sample_ids, lengths, weight, gain):
    feature_count = embedded.shape[1]
    slot_ids = sample_ids.reshape(N_DP, -1)
    sample_len = lengths.reshape(N_DP, -1)
    live = jax.vmap(live_rows)(sample_len).reshape(-1, 1)

    def gather_store(slot_all):
        slot_data = slot_all.reshape(N_DP, -1, LEN_A, feature_count)
        return jax.vmap(slot_rows)(slot_data, slot_ids).reshape(-1, feature_count)
    block_in = embedded
    inputs = []
    boundary = []
    for section_num in range(N_SECTION):
        values, inverse, normal = normalize(block_in, gain[section_num].astype(jnp.float32))
        normed = normal.astype(jnp.bfloat16)
        mixed = jnp.dot(normed, weight[section_num], preferred_element_type=jnp.float32)
        output = values + jax.nn.silu(mixed)
        inputs.append(block_in)
        if section_num < N_SECTION - 1:
            sender = gather_store(stored[section_num, 1]).astype(jnp.float32)
            delta = jnp.where(live, output - sender, 0.0)
            encoded, scaling = quantize(delta, QB)
            change = restore(encoded, scaling, QB)
            boundary.append((sender + change).astype(jnp.bfloat16))
            receiver = gather_store(stored[section_num + 1, 0]).astype(jnp.float32)
            block_in = (receiver + change).astype(jnp.bfloat16)
        else:
            boundary.append(output.astype(jnp.bfloat16))
    incoming = jnp.where(live, out_grad.astype(jnp.float32), 0.0)
    grads = [None] * N_SECTION
    for section_num in reversed(range(N_SECTION)):
        gain_row = gain[section_num].astype(jnp.float32)
        values, inverse, normal = normalize(inputs[section_num], gain_row)
        normed = normal.astype(jnp.bfloat16)
        mixed = jnp.dot(normed, weight[section_num], preferred_element_type=jnp.float32)
        gated = jax.nn.sigmoid(mixed)
        slope = (incoming * gated * (1.0 + mixed * (1.0 - gated))).astype(jnp.bfloat16)
        back = lax.dot_general(slope, weight[section_num], (((1,), (1,)), ((), ())), preferred_element_type=jnp.float32)
        weighted = back * gain_row
        centre = lax.optimization_barrier(jnp.mean(values * weighted, axis=1, keepdims=True))
        grad_in = incoming + inverse * weighted - values * inverse * inverse * inverse * centre
        grads[section_num] = group_sum(normed, slope)
        if section_num > 0:
            encoded, scaling = quantize(grad_in, QB)
            incoming = restore(encoded, scaling, QB)
    return (jnp.stack(boundary), jnp.stack(grads))
```

```python
import functools

import jax
import jax.numpy as jnp
from jax import lax
from jax.experimental import pallas as pl
from jax.experimental.pallas import tpu as pltpu
from jax.sharding import PartitionSpec as P

D = 2048
QTR = 32
N_MICRO = 4
ROWS = 128
N_SEC = 8
N_Z = 8
LAST = 10
TICKS = LAST + N_MICRO
EPS = 1e-6
BF = jnp.bfloat16
F32 = jnp.float32
BOTH = ("section", "dp")


def device(y, a, xh, z, c):
    return (2 * y + a) * 32 + 16 * xh + 2 * z + c


def pairs_of(target):
    out = []
    for y in range(4):
        for a in range(2):
            for xh in range(2):
                for z in range(N_Z):
                    for c in range(2):
                        to = target(y, a, xh, z, c)
                        if to is not None:
                            out.append((device(y, a, xh, z, c), device(*to)))
    return out


TURN = pairs_of(lambda y, a, xh, z, c: (y, c, xh, z, a))
TURN_FLIP = pairs_of(lambda y, a, xh, z, c: (y, 1 - c, xh, z, a))
TURN_FLIP_BACK = pairs_of(lambda y, a, xh, z, c: (y, c, xh, z, 1 - a))
CORES = pairs_of(lambda y, a, xh, z, c: (y, a, xh, z, 1 - c))
FAR_X = pairs_of(lambda y, a, xh, z, c: (y, a, 1 - xh, z, c))
UP_CORE = pairs_of(lambda y, a, xh, z, c: (y, a, xh, z, 1) if c == 0 else None)
UP_CHIP = pairs_of(lambda y, a, xh, z, c: (y + 1, a, xh, z, 0) if c == 1 and y < 3 else None)
DOWN_CORE = pairs_of(lambda y, a, xh, z, c: (y, a, xh, z, 0) if c == 1 else None)
DOWN_CHIP = pairs_of(lambda y, a, xh, z, c: (y - 1, a, xh, z, 1) if c == 0 and y > 0 else None)
Z_GROUPS = [[16 * xh + 2 * z + c for z in range(N_Z)] for xh in range(2) for c in range(2)]
X_GROUPS = [[16 * xh + 2 * z + c for xh in range(2)] for z in range(N_Z) for c in range(2)]

SHUFFLE = [(z * 2 + xh, xh * N_Z + z) for z in range(N_Z) for xh in range(2)]


def send(array, pairs):
    return lax.ppermute(array, BOTH, pairs)


def live_mask(tab, micro):
    row = lax.broadcasted_iota(jnp.int32, (ROWS, 1), 0)
    quarter = row // QTR
    limit = jnp.zeros((ROWS, 1), jnp.int32)
    for q in range(4):
        limit = jnp.where(quarter == q, tab[2 + micro * 4 + q], limit)
    return row - quarter * QTR < limit


def forward_kernel(
    tick, tab, first_ref, core_ref, chip_ref, held_ref, w_ref, gain_ref, sx, sm, sk,
    msg_ref, x_ref, mixed_ref, kept_ref, normed_ref,
):
    micro = tick - tab[1]
    block = tab[0]
    active = (micro >= 0) & (micro < N_MICRO)

    @pl.when(active & (block == 0))
    def _():
        x_ref[0] = first_ref[0]

    @pl.when(active & (block % 2 == 1))
    def _():
        x_ref[0] = core_ref[...]

    @pl.when(active & (block % 2 == 0) & (block > 0))
    def _():
        x_ref[0] = chip_ref[...]

    @pl.when(active)
    def _():
        values = x_ref[0].astype(F32)
        inverse = lax.rsqrt(jnp.mean(values * values, axis=1, keepdims=True) + EPS)
        normed = (values * inverse * gain_ref[...].astype(F32)).astype(BF)
        for to, at in SHUFFLE:
            normed_ref[:, to * 128 : to * 128 + 128] = normed[:, at * 128 : at * 128 + 128]
        mixed = jnp.dot(normed_ref[...], w_ref[...], preferred_element_type=F32)
        mixed_ref[0] = mixed
        output = x_ref[0].astype(F32) + mixed / (1.0 + jnp.exp(-mixed))
        keep = live_mask(tab, micro) | (block == N_SEC - 1)
        kept = jnp.where(keep, output, held_ref[0].astype(F32)).astype(BF)
        msg_ref[...] = kept
        kept_ref[0] = kept


def micro_block(tick, tab):
    return jnp.clip(tick - tab[1], 0, N_MICRO - 1)


def slot_block(tick, tab):
    micro = tick - tab[1]
    return jnp.where((micro >= 0) & (micro < N_MICRO), micro, N_MICRO)


ANY = pl.BlockSpec(memory_space=pl.ANY)
WHOLE = pl.BlockSpec((ROWS, D), lambda i, tab: (0, 0))
COST = pl.CostEstimate(flops=2 * ROWS * D * D, bytes_accessed=D * D * 2, transcendentals=ROWS * D)
PARAMS = pltpu.CompilerParams(vmem_limit_bytes=36 * 2**20)


def forward_tick(tick, tab, first, core, chip, held, weight, gain, stash):
    read = pl.BlockSpec((1, ROWS, D), lambda i, tab: (micro_block(tick, tab), 0, 0))
    slot = pl.BlockSpec((1, ROWS, D), lambda i, tab: (slot_block(tick, tab), 0, 0))
    return pl.pallas_call(
        functools.partial(forward_kernel, tick),
        grid_spec=pltpu.PrefetchScalarGridSpec(
            num_scalar_prefetch=1,
            grid=(1,),
            in_specs=[
                read, WHOLE, WHOLE, read,
                pl.BlockSpec((D, D), lambda i, tab: (0, 0)),
                pl.BlockSpec((1, D), lambda i, tab: (0, 0)),
                ANY, ANY, ANY,
            ],
            out_specs=[WHOLE, slot, slot, slot],
            scratch_shapes=[pltpu.VMEM((ROWS, D), BF)],
        ),
        out_shape=[jax.ShapeDtypeStruct((ROWS, D), BF)]
        + [jax.ShapeDtypeStruct(s.shape, s.dtype) for s in stash],
        input_output_aliases={7: 1, 8: 2, 9: 3},
        compiler_params=PARAMS,
        cost_estimate=COST,
        name=f"forward_{tick}",
    )(tab, first, core, chip, held, weight, gain, *stash)


def backward_kernel(
    tick, tab, given_ref, core_ref, chip_ref, w_ref, gain_ref, x_ref, mixed_ref, sn, ss,
    msg_ref, x_out, mixed_out, normed_ref, slope_ref, up_ref,
):
    micro = tick - (LAST - tab[1])
    block = tab[0]
    active = (micro >= 0) & (micro < N_MICRO)

    @pl.when(active & (block == N_SEC - 1))
    def _():
        given = given_ref[0].astype(F32)
        up_ref[...] = jnp.where(live_mask(tab, micro), given, 0.0).astype(BF)

    @pl.when(active & (block % 2 == 0))
    def _():
        up_ref[...] = core_ref[...]

    @pl.when(active & (block % 2 == 1) & (block < N_SEC - 1))
    def _():
        up_ref[...] = chip_ref[...]

    @pl.when(active)
    def _():
        mixed = mixed_ref[0]
        gated = 1.0 / (1.0 + jnp.exp(-mixed))
        up = up_ref[...].astype(F32)
        slope_ref[0] = (up * gated * (1.0 + mixed * (1.0 - gated))).astype(BF)
        values = x_ref[0].astype(F32)
        inverse = lax.rsqrt(jnp.mean(values * values, axis=1, keepdims=True) + EPS)
        normed = (values * inverse * gain_ref[...].astype(F32)).astype(BF)
        for to, at in SHUFFLE:
            normed_ref[0, :, to * 128 : to * 128 + 128] = normed[:, at * 128 : at * 128 + 128]

    @pl.when(active & (block > 0))
    def _():
        back = lax.dot_general(
            slope_ref[0], w_ref[...], (((1,), (1,)), ((), ())), preferred_element_type=F32
        )
        values = x_ref[0].astype(F32)
        inverse = lax.rsqrt(jnp.mean(values * values, axis=1, keepdims=True) + EPS)
        total = jnp.zeros((ROWS, 128), F32)
        weighted = []
        for to, at in SHUFFLE:
            part = back[:, to * 128 : to * 128 + 128] * gain_ref[:, at * 128 : at * 128 + 128].astype(F32)
            total = total + part * values[:, at * 128 : at * 128 + 128]
            weighted.append(part)
        centre = jnp.sum(total, axis=1, keepdims=True) * (1.0 / D)
        factor = inverse * inverse * inverse * centre
        for (to, at), part in zip(SHUFFLE, weighted):
            cols = slice(at * 128, at * 128 + 128)
            grad = up_ref[:, cols].astype(F32) + inverse * part - values[:, cols] * factor
            msg_ref[:, cols] = grad.astype(BF)


def backward_tick(tick, tab, given, core, chip, weight, gain, stash, sums):
    def micro_of(tab):
        return tick - (LAST - tab[1])

    def slot_of(tab):
        micro = micro_of(tab)
        return jnp.where((micro >= 0) & (micro < N_MICRO), micro, N_MICRO)

    read = pl.BlockSpec(
        (1, ROWS, D), lambda i, tab: (jnp.clip(micro_of(tab), 0, N_MICRO - 1), 0, 0)
    )
    slot = pl.BlockSpec((1, ROWS, D), lambda i, tab: (slot_of(tab), 0, 0))
    return pl.pallas_call(
        functools.partial(backward_kernel, tick),
        grid_spec=pltpu.PrefetchScalarGridSpec(
            num_scalar_prefetch=1,
            grid=(1,),
            in_specs=[
                read, WHOLE, WHOLE,
                pl.BlockSpec((D, D), lambda i, tab: (0, 0)),
                pl.BlockSpec((1, D), lambda i, tab: (0, 0)),
                read, read, ANY, ANY,
            ],
            out_specs=[WHOLE, ANY, ANY, slot, slot],
            scratch_shapes=[pltpu.VMEM((ROWS, D), BF)],
        ),
        out_shape=[jax.ShapeDtypeStruct((ROWS, D), BF)]
        + [jax.ShapeDtypeStruct(s.shape, s.dtype) for s in (*stash, *sums)],
        input_output_aliases={6: 1, 7: 2, 8: 3, 9: 4},
        compiler_params=PARAMS,
        cost_estimate=COST,
        name=f"backward_{tick}",
    )(tab, given, core, chip, weight, gain, *stash, *sums)


def held_rows(slots, ids):
    long_part = jnp.take(slots, ids[:4], axis=0).reshape(-1, D)
    short_part = jnp.take(slots[:, :QTR], ids[4:], axis=0).reshape(-1, D)
    return jnp.concatenate([long_part, short_part], axis=0)


def body(embedded, out_grad, stored, sample_ids, lengths, weight, gain):
    section = lax.axis_index("section")
    data = lax.axis_index("dp")
    y, a = section // 2, section % 2
    xh, c = data // 16, data % 2
    same = a == c
    block = 2 * y + c

    mine = send(weight[0], TURN)
    other = send(weight[0], TURN_FLIP)
    rows = jnp.where(
        a == 0, jnp.concatenate([mine, other], axis=0), jnp.concatenate([other, mine], axis=0)
    )
    rows = lax.all_gather(rows, "dp", axis=0, tiled=True, axis_index_groups=X_GROUPS)
    full = lax.all_gather(rows, "dp", axis=0, tiled=True, axis_index_groups=Z_GROUPS)

    ends = jnp.where(y == 0, embedded, out_grad)
    ends = jnp.where(same, ends, send(ends, CORES)).reshape(N_MICRO, ROWS, D)
    limits = jnp.where(same, lengths, send(lengths, CORES))
    gain_pair = jnp.where(same, gain, send(gain, TURN))
    held = send(held_rows(stored[0, 1], sample_ids), TURN).reshape(N_MICRO, ROWS, D)
    long_limits = jnp.stack([limits[:4], limits[:4] - QTR], axis=1).reshape(-1)
    tab = jnp.concatenate([jnp.stack([block, 3 * y + c]), long_limits, limits[4:]])

    blank = jnp.zeros((ROWS, D), BF)
    stash = [
        jnp.zeros((N_MICRO + 1, ROWS, D), BF),
        jnp.zeros((N_MICRO + 1, ROWS, D), F32),
        jnp.zeros((N_MICRO + 1, ROWS, D), BF),
    ]
    sums = [jnp.zeros((N_MICRO + 1, ROWS, D), BF), jnp.zeros((N_MICRO + 1, ROWS, D), BF)]
    up_core, up_chip = [blank], [blank, blank]
    down_core, down_chip = [blank], [blank, blank]
    kept = None
    for tick in range(LAST + TICKS):
        if tick < TICKS:
            msg, *stash = forward_tick(
                tick, tab, ends, up_core[tick], up_chip[tick], held, full, gain_pair, stash
            )
            if tick < TICKS - 1:
                up_core.append(send(msg, UP_CORE))
            if tick < TICKS - 2:
                up_chip.append(send(msg, UP_CHIP))
            if tick == TICKS - 1:
                kept = send(stash[2][:N_MICRO].reshape(-1, D), TURN)
                stash = stash[:2]
        if tick >= LAST:
            step = tick - LAST
            two = stash[:2]
            msg, two[0], two[1], *sums = backward_tick(
                step, tab, ends, down_core[step], down_chip[step], full, gain_pair, two, sums
            )
            stash = two + stash[2:]
            if step < TICKS - 1:
                down_core.append(send(msg, DOWN_CORE))
            if step < TICKS - 2:
                down_chip.append(send(msg, DOWN_CHIP))

    normed = sums[0][:N_MICRO].reshape(-1, D)
    slope = sums[1][:N_MICRO].reshape(-1, D)
    product = lax.dot_general(
        normed, slope, (((0,), (0,)), ((), ())), preferred_element_type=F32
    ).astype(BF)
    part = lax.psum_scatter(
        product, "dp", scatter_dimension=0, tiled=True, axis_index_groups=Z_GROUPS
    ).reshape(2, 128, D)
    own = lax.dynamic_index_in_dim(part, xh, 0, keepdims=False)
    far = send(lax.dynamic_index_in_dim(part, 1 - xh, 0, keepdims=False), FAR_X)
    both = (own.astype(F32) + far.astype(F32)).astype(BF).reshape(2, 64, D)
    first = send(lax.dynamic_index_in_dim(both, a, 0, keepdims=False), TURN)
    second = send(lax.dynamic_index_in_dim(both, 1 - a, 0, keepdims=False), TURN_FLIP_BACK)
    shard = first.astype(F32) + second.astype(F32)
    return (kept[None], shard[None])


def solution(mesh):
    in_specs = (
        P("dp", None),
        P("dp", None),
        P("section", None, "dp", None, None),
        P("dp"),
        P("dp"),
        P("section", "dp", None),
        P("section", None),
    )
    out_specs = (P("section", "dp", None), P("section", "dp", None))
    return jax.shard_map(body, mesh=mesh, in_specs=in_specs, out_specs=out_specs, check_vma=False)
```

```python
import functools

import jax
import jax.numpy as jnp
from jax import lax
from jax.experimental import pallas as pl
from jax.experimental.pallas import tpu as pltpu
from jax.sharding import PartitionSpec as P

D = 2048
QTR = 32
N_MICRO = 4
ROWS = 128
N_SEC = 8
N_Z = 8
LAST = 10
TICKS = LAST + N_MICRO
EPS = 1e-6
BF = jnp.bfloat16
F32 = jnp.float32
BOTH = ("section", "dp")


def device(y, a, xh, z, c):
    return (2 * y + a) * 32 + 16 * xh + 2 * z + c


def pairs_of(target):
    out = []
    for y in range(4):
        for a in range(2):
            for xh in range(2):
                for z in range(N_Z):
                    for c in range(2):
                        to = target(y, a, xh, z, c)
                        if to is not None:
                            out.append((device(y, a, xh, z, c), device(*to)))
    return out


TURN = pairs_of(lambda y, a, xh, z, c: (y, c, xh, z, a))
CORES = pairs_of(lambda y, a, xh, z, c: (y, a, xh, z, 1 - c))
UP_CORE = pairs_of(lambda y, a, xh, z, c: (y, a, xh, z, 1) if c == 0 else None)
UP_CHIP = pairs_of(lambda y, a, xh, z, c: (y + 1, a, xh, z, 0) if c == 1 and y < 3 else None)
DOWN_CORE = pairs_of(lambda y, a, xh, z, c: (y, a, xh, z, 0) if c == 1 else None)
DOWN_CHIP = pairs_of(lambda y, a, xh, z, c: (y - 1, a, xh, z, 1) if c == 0 and y > 0 else None)
RIGHT = pairs_of(lambda y, a, xh, z, c: (y, a, xh, (z + 1) % N_Z, c))
LEFT = pairs_of(lambda y, a, xh, z, c: (y, a, xh, (z - 1) % N_Z, c))
FLIPS = [(dx, dt) for dx in range(2) for dt in range(2)]
TO_ROLE = [pairs_of(lambda y, a, xh, z, c: (y, c ^ dt, xh ^ dx, z, a)) for dx, dt in FLIPS]
TO_PLACE = [pairs_of(lambda y, a, xh, z, c: (y, c, xh ^ dx, z, a ^ dt)) for dx, dt in FLIPS]

CHUNK = 256
HALF = 1024


def send(array, pairs):
    return lax.ppermute(array, BOTH, pairs)


ANY = pl.BlockSpec(memory_space=pl.ANY)
WHOLE = pl.BlockSpec((ROWS, D), lambda i, tab: (0, 0))
COST = pl.CostEstimate(flops=2 * ROWS * D * D, bytes_accessed=D * D * 2, transcendentals=ROWS * D)
PARAMS = pltpu.CompilerParams(vmem_limit_bytes=30 * 2**20)


def feature_columns(z, k, xh):
    return pl.ds(pl.multiple_of((xh * N_Z + lax.rem(z + k, N_Z)) * 128, 128), 128)


def arrange_kernel(place, p0, p1, p2, p3, left_ref, right_ref):
    for (dx, dt), part in zip(FLIPS, (p0, p1, p2, p3)):
        index = (place[0] ^ dx) * 2 + (place[1] ^ dt)
        rows = pl.ds(pl.multiple_of(index * 64, 64), 64)
        left_ref[rows, :] = part[:, :HALF]
        right_ref[rows, :] = part[:, HALF:]


def arrange(place, parts):
    half = jax.ShapeDtypeStruct((CHUNK, HALF), BF)
    return pl.pallas_call(
        arrange_kernel,
        grid_spec=pltpu.PrefetchScalarGridSpec(
            num_scalar_prefetch=1,
            grid=(1,),
            in_specs=[pl.BlockSpec((64, D), lambda i, place: (0, 0))] * 4,
            out_specs=[pl.BlockSpec((CHUNK, HALF), lambda i, place: (0, 0))] * 2,
        ),
        out_shape=[half, half],
        name="arrange",
    )(place, *parts)


def assemble_kernel(*refs):
    out = refs[-1]
    for k in range(N_Z):
        for h in range(2):
            out[k * CHUNK : (k + 1) * CHUNK, h * HALF : (h + 1) * HALF] = refs[2 * k + h][...]


def assemble(chunks):
    return pl.pallas_call(
        assemble_kernel,
        grid=(1,),
        in_specs=[pl.BlockSpec((CHUNK, HALF), lambda i: (0, 0))] * 16,
        out_specs=pl.BlockSpec((D, D), lambda i: (0, 0)),
        out_shape=jax.ShapeDtypeStruct((D, D), BF),
        compiler_params=PARAMS,
        name="assemble",
    )(*[half for chunk in chunks for half in chunk])


def gather_weight(place, shard):
    own = arrange(place, [send(shard, pairs) for pairs in TO_ROLE])
    chunks = [None] * N_Z
    chunks[0] = list(own)
    from_left, from_right = list(own), list(own)
    for step in range(1, 4):
        from_left = [send(half, RIGHT) for half in from_left]
        from_right = [send(half, LEFT) for half in from_right]
        chunks[N_Z - step], chunks[step] = from_left, from_right
    chunks[4] = [send(from_left[0], RIGHT), send(from_right[1], LEFT)]
    return assemble(chunks)


def product_kernel(has, n_ref, s_ref, *refs):
    rows = N_MICRO * ROWS
    total = lax.dot_general(
        n_ref[...].reshape(rows, CHUNK),
        s_ref[...].reshape(rows, HALF),
        (((0,), (0,)), ((), ())),
        preferred_element_type=F32,
    )
    for ref in refs[:has]:
        total = total + ref[...].astype(F32)
    refs[has][...] = total.astype(BF)


def product(sums, k, half, arrived):
    piece = pl.BlockSpec((CHUNK, HALF), lambda i: (0, 0))
    return pl.pallas_call(
        functools.partial(product_kernel, len(arrived)),
        grid=(1,),
        in_specs=[
            pl.BlockSpec((N_MICRO, ROWS, CHUNK), lambda i: (0, 0, k)),
            pl.BlockSpec((N_MICRO, ROWS, HALF), lambda i: (0, 0, half)),
        ]
        + [piece] * len(arrived),
        out_specs=piece,
        out_shape=jax.ShapeDtypeStruct((CHUNK, HALF), BF),
        compiler_params=PARAMS,
        cost_estimate=pl.CostEstimate(
            flops=2 * N_MICRO * ROWS * CHUNK * HALF, bytes_accessed=2**21, transcendentals=0
        ),
        name=f"product_{k}_{half}",
    )(*sums, *arrived)


def spread_kernel(place, left_ref, right_ref, o0, o1, o2, o3):
    for (dx, dt), out in zip(FLIPS, (o0, o1, o2, o3)):
        index = (place[0] ^ dx) * 2 + (place[1] ^ dt)
        rows = pl.ds(pl.multiple_of(index * 64, 64), 64)
        out[:, :HALF] = left_ref[rows, :]
        out[:, HALF:] = right_ref[rows, :]


def spread(place, halves):
    return pl.pallas_call(
        spread_kernel,
        grid_spec=pltpu.PrefetchScalarGridSpec(
            num_scalar_prefetch=1,
            grid=(1,),
            in_specs=[pl.BlockSpec((CHUNK, HALF), lambda i, place: (0, 0))] * 2,
            out_specs=[pl.BlockSpec((64, D), lambda i, place: (0, 0))] * 4,
        ),
        out_shape=[jax.ShapeDtypeStruct((64, D), BF)] * 4,
        name="spread",
    )(place, *halves)


def scatter_grad(place, sums):
    to_right = [send(product(sums, 4, 0, []), RIGHT), None]
    to_left = [None, send(product(sums, 4, 1, []), LEFT)]
    for step in range(3, 0, -1):
        for half in (1, 0):
            held = to_right[half]
            to_right[half] = send(product(sums, step, half, [] if held is None else [held]), RIGHT)
            held = to_left[1 - half]
            to_left[1 - half] = send(
                product(sums, N_Z - step, 1 - half, [] if held is None else [held]), LEFT
            )
    halves = [product(sums, 0, half, [to_right[half], to_left[half]]) for half in range(2)]
    parts = [send(part, pairs) for part, pairs in zip(spread(place, halves), TO_PLACE)]
    total = parts[0].astype(F32)
    for part in parts[1:]:
        total = total + part.astype(F32)
    return total


def live_mask(tab, micro):
    row = lax.broadcasted_iota(jnp.int32, (ROWS, 1), 0)
    quarter = row // QTR
    limit = jnp.zeros((ROWS, 1), jnp.int32)
    for q in range(4):
        limit = jnp.where(quarter == q, tab[3 + micro * 4 + q], limit)
    return row - quarter * QTR < limit


def forward_kernel(
    tick, tab, first_ref, core_ref, chip_ref, held_ref, w_ref, gain_ref, sx, sm, sk, sn,
    msg_ref, x_ref, mixed_ref, kept_ref, normed_ref, plain_ref,
):
    micro = tick - tab[1]
    block = tab[0]
    active = (micro >= 0) & (micro < N_MICRO)

    @pl.when(active & (block == 0))
    def _():
        x_ref[0] = first_ref[0]

    @pl.when(active & (block % 2 == 1))
    def _():
        x_ref[0] = core_ref[...]

    @pl.when(active & (block % 2 == 0) & (block > 0))
    def _():
        x_ref[0] = chip_ref[...]

    @pl.when(active)
    def _():
        values = x_ref[0].astype(F32)
        inverse = lax.rsqrt(jnp.mean(values * values, axis=1, keepdims=True) + EPS)
        plain_ref[...] = (values * inverse * gain_ref[...].astype(F32)).astype(BF)
        for k in range(N_Z):
            for xh in range(2):
                to = k * CHUNK + xh * 128
                normed_ref[0, :, to : to + 128] = plain_ref[:, feature_columns(tab[2], k, xh)]
        mixed = jnp.dot(normed_ref[0], w_ref[...], preferred_element_type=F32)
        mixed_ref[0] = mixed
        output = x_ref[0].astype(F32) + mixed / (1.0 + jnp.exp(-mixed))
        keep = live_mask(tab, micro) | (block == N_SEC - 1)
        kept = jnp.where(keep, output, held_ref[0].astype(F32)).astype(BF)
        msg_ref[...] = kept
        kept_ref[0] = kept


def micro_block(tick, tab):
    return jnp.clip(tick - tab[1], 0, N_MICRO - 1)


def slot_block(tick, tab):
    micro = tick - tab[1]
    return jnp.where((micro >= 0) & (micro < N_MICRO), micro, N_MICRO)


def forward_tick(tick, tab, first, core, chip, held, weight, gain, stash):
    read = pl.BlockSpec((1, ROWS, D), lambda i, tab: (micro_block(tick, tab), 0, 0))
    slot = pl.BlockSpec((1, ROWS, D), lambda i, tab: (slot_block(tick, tab), 0, 0))
    return pl.pallas_call(
        functools.partial(forward_kernel, tick),
        grid_spec=pltpu.PrefetchScalarGridSpec(
            num_scalar_prefetch=1,
            grid=(1,),
            in_specs=[
                read, WHOLE, WHOLE, read,
                pl.BlockSpec((D, D), lambda i, tab: (0, 0)),
                pl.BlockSpec((1, D), lambda i, tab: (0, 0)),
                ANY, ANY, ANY, ANY,
            ],
            out_specs=[WHOLE, slot, slot, slot, slot],
            scratch_shapes=[pltpu.VMEM((ROWS, D), BF)],
        ),
        out_shape=[jax.ShapeDtypeStruct((ROWS, D), BF)]
        + [jax.ShapeDtypeStruct(s.shape, s.dtype) for s in stash],
        input_output_aliases={7: 1, 8: 2, 9: 3, 10: 4},
        compiler_params=PARAMS,
        cost_estimate=COST,
        name=f"forward_{tick}",
    )(tab, first, core, chip, held, weight, gain, *stash)


def backward_kernel(
    tick, tab, given_ref, core_ref, chip_ref, w_ref, gain_ref, x_ref, mixed_ref, ss,
    msg_ref, x_out, mixed_out, slope_ref, up_ref,
):
    micro = tick - (LAST - tab[1])
    block = tab[0]
    active = (micro >= 0) & (micro < N_MICRO)

    @pl.when(active & (block == N_SEC - 1))
    def _():
        given = given_ref[0].astype(F32)
        up_ref[...] = jnp.where(live_mask(tab, micro), given, 0.0).astype(BF)

    @pl.when(active & (block % 2 == 0))
    def _():
        up_ref[...] = core_ref[...]

    @pl.when(active & (block % 2 == 1) & (block < N_SEC - 1))
    def _():
        up_ref[...] = chip_ref[...]

    @pl.when(active)
    def _():
        mixed = mixed_ref[0]
        gated = 1.0 / (1.0 + jnp.exp(-mixed))
        up = up_ref[...].astype(F32)
        slope_ref[0] = (up * gated * (1.0 + mixed * (1.0 - gated))).astype(BF)

    @pl.when(active & (block > 0))
    def _():
        back = lax.dot_general(
            slope_ref[0], w_ref[...], (((1,), (1,)), ((), ())), preferred_element_type=F32
        )
        values = x_ref[0].astype(F32)
        inverse = lax.rsqrt(jnp.mean(values * values, axis=1, keepdims=True) + EPS)
        total = jnp.zeros((ROWS, 128), F32)
        weighted = []
        for k in range(N_Z):
            for xh in range(2):
                cols = feature_columns(tab[2], k, xh)
                at = k * CHUNK + xh * 128
                part = back[:, at : at + 128] * gain_ref[:, cols].astype(F32)
                total = total + part * x_ref[0, :, cols].astype(F32)
                weighted.append((cols, part))
        centre = jnp.sum(total, axis=1, keepdims=True) * (1.0 / D)
        factor = inverse * inverse * inverse * centre
        for cols, part in weighted:
            grad = up_ref[:, cols].astype(F32) + inverse * part
            msg_ref[:, cols] = (grad - x_ref[0, :, cols].astype(F32) * factor).astype(BF)


def backward_tick(tick, tab, given, core, chip, weight, gain, stash, slopes):
    def micro_of(tab):
        return tick - (LAST - tab[1])

    def slot_of(tab):
        micro = micro_of(tab)
        return jnp.where((micro >= 0) & (micro < N_MICRO), micro, N_MICRO)

    read = pl.BlockSpec(
        (1, ROWS, D), lambda i, tab: (jnp.clip(micro_of(tab), 0, N_MICRO - 1), 0, 0)
    )
    slot = pl.BlockSpec((1, ROWS, D), lambda i, tab: (slot_of(tab), 0, 0))
    return pl.pallas_call(
        functools.partial(backward_kernel, tick),
        grid_spec=pltpu.PrefetchScalarGridSpec(
            num_scalar_prefetch=1,
            grid=(1,),
            in_specs=[
                read, WHOLE, WHOLE,
                pl.BlockSpec((D, D), lambda i, tab: (0, 0)),
                pl.BlockSpec((1, D), lambda i, tab: (0, 0)),
                read, read, ANY,
            ],
            out_specs=[WHOLE, ANY, ANY, slot],
            scratch_shapes=[pltpu.VMEM((ROWS, D), BF)],
        ),
        out_shape=[jax.ShapeDtypeStruct((ROWS, D), BF)]
        + [jax.ShapeDtypeStruct(s.shape, s.dtype) for s in (*stash, slopes)],
        input_output_aliases={6: 1, 7: 2, 8: 3},
        compiler_params=PARAMS,
        cost_estimate=COST,
        name=f"backward_{tick}",
    )(tab, given, core, chip, weight, gain, *stash, slopes)


def held_rows(slots, ids):
    long_part = jnp.take(slots, ids[:4], axis=0).reshape(-1, D)
    short_part = jnp.take(slots[:, :QTR], ids[4:], axis=0).reshape(-1, D)
    return jnp.concatenate([long_part, short_part], axis=0)


def body(embedded, out_grad, stored, sample_ids, lengths, weight, gain):
    section = lax.axis_index("section")
    data = lax.axis_index("dp")
    y, a = section // 2, section % 2
    xh, c = data // 16, data % 2
    z = (data // 2) % N_Z
    same = a == c
    block = 2 * y + c
    place = jnp.stack([xh, a, z])
    full = gather_weight(place, weight[0])

    ends = jnp.where(y == 0, embedded, out_grad)
    ends = jnp.where(same, ends, send(ends, CORES)).reshape(N_MICRO, ROWS, D)
    limits = jnp.where(same, lengths, send(lengths, CORES))
    gain_pair = send(gain, TURN)
    held = send(held_rows(stored[0, 1], sample_ids), TURN).reshape(N_MICRO, ROWS, D)
    long_limits = jnp.stack([limits[:4], limits[:4] - QTR], axis=1).reshape(-1)
    tab = jnp.concatenate([jnp.stack([block, 3 * y + c, z]), long_limits, limits[4:]])

    blank = jnp.zeros((ROWS, D), BF)
    stash = [
        jnp.zeros((N_MICRO + 1, ROWS, D), BF),
        jnp.zeros((N_MICRO + 1, ROWS, D), F32),
        jnp.zeros((N_MICRO + 1, ROWS, D), BF),
        jnp.zeros((N_MICRO + 1, ROWS, D), BF),
    ]
    slopes = jnp.zeros((N_MICRO + 1, ROWS, D), BF)
    up_core, up_chip = [blank], [blank, blank]
    down_core, down_chip = [blank], [blank, blank]
    kept = None
    for tick in range(LAST + TICKS):
        if tick < TICKS:
            msg, *stash = forward_tick(
                tick, tab, ends, up_core[tick], up_chip[tick], held, full, gain_pair, stash
            )
            if tick < TICKS - 1:
                up_core.append(send(msg, UP_CORE))
            if tick < TICKS - 2:
                up_chip.append(send(msg, UP_CHIP))
            if tick == TICKS - 1:
                kept = send(stash[2][:N_MICRO].reshape(-1, D), TURN)
        if tick >= LAST:
            step = tick - LAST
            msg, stash[0], stash[1], slopes = backward_tick(
                step, tab, ends, down_core[step], down_chip[step], full, gain_pair, stash[:2], slopes
            )
            if step < TICKS - 1:
                down_core.append(send(msg, DOWN_CORE))
            if step < TICKS - 2:
                down_chip.append(send(msg, DOWN_CHIP))

    shard = scatter_grad(place, (stash[3], slopes))
    return (kept[None], shard[None])


def solution(mesh):
    in_specs = (
        P("dp", None),
        P("dp", None),
        P("section", None, "dp", None, None),
        P("dp"),
        P("dp"),
        P("section", "dp", None),
        P("section", None),
    )
    out_specs = (P("section", "dp", None), P("section", "dp", None))
    return jax.shard_map(body, mesh=mesh, in_specs=in_specs, out_specs=out_specs, check_vma=False)
```

```python
import functools

import jax
import jax.numpy as jnp
from jax import lax
from jax.experimental import pallas as pl
from jax.experimental.pallas import tpu as pltpu
from jax.sharding import PartitionSpec as P

D = 2048
QTR = 32
N_MICRO = 4
ROWS = 128
N_SEC = 8
N_Z = 8
LAST = 10
TICKS = LAST + N_MICRO
EPS = 1e-6
BF = jnp.bfloat16
F32 = jnp.float32
BOTH = ("section", "dp")


def device(y, a, xh, z, c):
    return (2 * y + a) * 32 + 16 * xh + 2 * z + c


def pairs_of(target):
    out = []
    for y in range(4):
        for a in range(2):
            for xh in range(2):
                for z in range(N_Z):
                    for c in range(2):
                        to = target(y, a, xh, z, c)
                        if to is not None:
                            out.append((device(y, a, xh, z, c), device(*to)))
    return out


TURN = pairs_of(lambda y, a, xh, z, c: (y, c, xh, z, a))
CORES = pairs_of(lambda y, a, xh, z, c: (y, a, xh, z, 1 - c))
RIGHT = pairs_of(lambda y, a, xh, z, c: (y, a, xh, (z + 1) % N_Z, c))
LEFT = pairs_of(lambda y, a, xh, z, c: (y, a, xh, (z - 1) % N_Z, c))
UP_CORE = pairs_of(lambda y, a, xh, z, c: (y, a, xh, z, 1) if c == 0 else None)
UP_CHIP = pairs_of(lambda y, a, xh, z, c: (y + 1, a, xh, z, 0) if c == 1 and y < 3 else None)
DOWN_CORE = pairs_of(lambda y, a, xh, z, c: (y, a, xh, z, 0) if c == 1 else None)
DOWN_CHIP = pairs_of(lambda y, a, xh, z, c: (y - 1, a, xh, z, 1) if c == 0 and y > 0 else None)
FAR_X = pairs_of(lambda y, a, xh, z, c: (y, a, 1 - xh, z, c))
FAR_X_CORE = pairs_of(lambda y, a, xh, z, c: (y, a, 1 - xh, z, 1 - c))
TO_PLACE = [pairs_of(lambda y, a, xh, z, c: (y, c, xh, z, a ^ j)) for j in range(2)]


def beside(y, a, xh, z, step, core):
    x = (2 * xh + a + step) % 4
    return (y, x % 2, x // 2, z, core)


TO_CORE = pairs_of(lambda y, a, xh, z, c: (y, a, xh, z, a) if c != a else None)
TO_NEXT = pairs_of(lambda y, a, xh, z, c: beside(y, a, xh, z, 1, a) if c == 0 else None)
TO_PREVIOUS = pairs_of(lambda y, a, xh, z, c: beside(y, a, xh, z, -1, a) if c == 1 else None)

CHUNK = 256
HALF = 1024
QUARTER = 512
BATCHES = ((0, 7, 1), (6, 2), (5, 3, 4))
ORDER = sum(BATCHES, ())


def send(array, pairs):
    return lax.ppermute(array, BOTH, pairs)


ANY = pl.BlockSpec(memory_space=pl.ANY)
WHOLE = pl.BlockSpec((ROWS, D), lambda i, tab: (0, 0))
COST = pl.CostEstimate(flops=2 * ROWS * D * D, bytes_accessed=D * D * 2, transcendentals=ROWS * D)
PARAMS = pltpu.CompilerParams(vmem_limit_bytes=18 * 2**20)


def feature_columns(z, k, xh):
    return pl.ds(pl.multiple_of((xh * N_Z + lax.rem(z + k, N_Z)) * 128, 128), 128)


def whole(shape):
    return pl.BlockSpec(shape, lambda i, place: (0,) * len(shape))


def placed(kernel, name, place, arrays, outs):
    return pl.pallas_call(
        kernel,
        grid_spec=pltpu.PrefetchScalarGridSpec(
            num_scalar_prefetch=1,
            grid=(1,),
            in_specs=[whole(r.shape) for r in arrays],
            out_specs=[whole(shape) for shape, _ in outs],
        ),
        out_shape=[jax.ShapeDtypeStruct(shape, dtype) for shape, dtype in outs],
        compiler_params=pltpu.CompilerParams(vmem_limit_bytes=28 * 2**20),
        name=name,
    )(place, *arrays)


def half_columns(index):
    return pl.ds(pl.multiple_of(index * HALF, HALF), HALF)


def part_rows(index, rows):
    return pl.ds(pl.multiple_of(index * rows, rows), rows)


def divide_kernel(place, shard, mine, other):
    mine[...] = shard[:, half_columns(place[2])]
    other[...] = shard[:, half_columns(1 - place[2])]


def arrange_kernel(place, p00, p01, p10, p11, out):
    for dx, dt, part in ((0, 0, p00), (0, 1, p01), (1, 0, p10), (1, 1, p11)):
        out[part_rows((place[0] ^ dx) * 2 + (place[2] ^ dt), 64), :] = part[...]


def assemble_kernel(place, *refs):
    own, refs = refs[:9], refs[9:]
    out = refs[-1]
    core, following, previous = refs[:3], refs[3:6], refs[6:9]

    def fill(batches, columns):
        for ref, batch in zip(batches, BATCHES):
            for i, k in enumerate(batch):
                out[k * CHUNK : (k + 1) * CHUNK, columns] = ref[i * CHUNK : (i + 1) * CHUNK, :]

    for c in range(2):

        @pl.when((place[1] == place[2]) & (place[2] == c))
        def _():
            columns = slice(c * HALF, (c + 1) * HALF)
            for k in range(N_Z):
                if k != 4:
                    out[k * CHUNK : (k + 1) * CHUNK, columns] = own[k][...]
            out[4 * CHUNK : 4 * CHUNK + 128, columns] = own[4][...]
            out[4 * CHUNK + 128 : 5 * CHUNK, columns] = own[8][...]
            fill(core, slice((1 - c) * HALF, (2 - c) * HALF))

    @pl.when(place[1] != place[2])
    def _():
        fill(following, slice(0, HALF))
        fill(previous, slice(HALF, D))


def gather_weight(place, shard):
    quarter, chunk = ((64, HALF), BF), ((CHUNK, HALF), BF)
    mine, other = placed(divide_kernel, "divide", place, [shard], [quarter, quarter])
    parts = [mine, send(other, CORES), send(mine, FAR_X), send(other, FAR_X_CORE)]
    own = [None] * 9
    own[0] = placed(arrange_kernel, "arrange", place, parts, [chunk])[0]
    core, following, previous = [], [], []

    def pass_on(batch):
        pieces = [own[k] for k in batch if k != 4] + ([own[4], own[8]] if 4 in batch else [])
        rows = jnp.concatenate(pieces, axis=0)
        following.append(send(rows, TO_NEXT))
        previous.append(send(rows, TO_PREVIOUS))
        core.append(send(rows, TO_CORE))

    for step in range(1, 4):
        own[-step % N_Z] = send(own[(1 - step) % N_Z], RIGHT)
        own[step] = send(own[step - 1], LEFT)
        if step < 3:
            pass_on(BATCHES[step - 1])
    own[4] = send(own[5][:128], RIGHT)
    own[8] = send(own[3][128:], LEFT)
    pass_on(BATCHES[2])
    arrays = [*own, *core, *following, *previous]
    full = placed(assemble_kernel, "assemble", place, arrays, [((D, D), BF)])[0]
    return full, own[6]


def product_kernel(has, *refs):
    rows = N_MICRO * ROWS
    total = jnp.zeros((CHUNK, QUARTER), F32)
    for j in range(2):
        slope = jnp.concatenate([ref[...] for ref in refs[2 + 4 * j : 6 + 4 * j]], axis=0)
        total = total + lax.dot_general(
            refs[j][...].reshape(rows, CHUNK),
            slope,
            (((0,), (0,)), ((), ())),
            preferred_element_type=F32,
        )
    for ref in refs[10 : 10 + has]:
        total = total + ref[...].astype(F32)
    refs[-1][...] = total.astype(BF)


def product(sums, k, part, arrived):
    piece = pl.BlockSpec((CHUNK, QUARTER), lambda i: (0, 0))
    return pl.pallas_call(
        functools.partial(product_kernel, len(arrived)),
        grid=(1,),
        in_specs=[pl.BlockSpec((N_MICRO, ROWS, CHUNK), lambda i: (0, 0, k))] * 2
        + [pl.BlockSpec((ROWS, QUARTER), lambda i: (0, part))] * 8
        + [piece] * len(arrived),
        out_specs=piece,
        out_shape=jax.ShapeDtypeStruct((CHUNK, QUARTER), BF),
        compiler_params=PARAMS,
        cost_estimate=pl.CostEstimate(
            flops=4 * N_MICRO * ROWS * CHUNK * QUARTER, bytes_accessed=2**21, transcendentals=0
        ),
        name=f"product_{k}_{part}",
    )(*sums, *arrived)


def split_x_kernel(place, q0, q1, mine, other):
    for out, xh in ((mine, place[0]), (other, 1 - place[0])):
        rows = part_rows(xh, 128)
        out[:, :QUARTER] = q0[rows, :]
        out[:, QUARTER:] = q1[rows, :]


def split_core_kernel(place, mine, arrived, own, other, total):
    total[...] = mine[...].astype(F32) + arrived[...].astype(F32)
    own[...] = total[part_rows(place[2], 64), :]
    other[...] = total[part_rows(1 - place[2], 64), :].astype(BF)


def scatter_grad(place, sums, core):
    to_right = [send(product(sums, 4, 0, []), RIGHT), None]
    to_left = [None, send(product(sums, 4, 1, []), LEFT)]
    for step in range(3, 0, -1):
        for part in (1, 0):
            held = to_right[part]
            to_right[part] = send(product(sums, step, part, [] if held is None else [held]), RIGHT)
            held = to_left[1 - part]
            to_left[1 - part] = send(
                product(sums, N_Z - step, 1 - part, [] if held is None else [held]), LEFT
            )
    quarters = [product(sums, 0, part, [to_right[part], to_left[part]]) for part in range(2)]
    block = ((128, HALF), BF)
    mine, other = placed(split_x_kernel, "split_x", place, quarters, [block, block])
    arrived = send(other, FAR_X)
    own, other, _ = placed(
        split_core_kernel, "split_core", place, [mine, arrived],
        [((64, HALF), F32), ((64, HALF), BF), ((128, HALF), F32)],
    )
    arrived = send(other, CORES).astype(F32)
    return jnp.where(
        core == 0,
        jnp.concatenate([own, arrived], axis=1),
        jnp.concatenate([arrived, own], axis=1),
    )


def live_mask(tab, micro):
    row = lax.broadcasted_iota(jnp.int32, (ROWS, 1), 0)
    quarter = row // QTR
    limit = jnp.zeros((ROWS, 1), jnp.int32)
    for q in range(4):
        limit = jnp.where(quarter == q, tab[3 + micro * 4 + q], limit)
    return row - quarter * QTR < limit


def forward_kernel(
    tick, tab, first_ref, core_ref, chip_ref, held_ref, w_ref, gain_ref, sx, sm, sk, sn,
    msg_ref, x_ref, mixed_ref, kept_ref, normed_ref, plain_ref,
):
    micro = tick - tab[1]
    block = tab[0]
    active = (micro >= 0) & (micro < N_MICRO)

    @pl.when(active & (block == 0))
    def _():
        x_ref[0] = first_ref[0]

    @pl.when(active & (block % 2 == 1))
    def _():
        x_ref[0] = core_ref[...]

    @pl.when(active & (block % 2 == 0) & (block > 0))
    def _():
        x_ref[0] = chip_ref[...]

    @pl.when(active)
    def _():
        values = x_ref[0].astype(F32)
        inverse = lax.rsqrt(jnp.mean(values * values, axis=1, keepdims=True) + EPS)
        plain_ref[...] = (values * inverse * gain_ref[...].astype(F32)).astype(BF)
        for k in range(N_Z):
            for xh in range(2):
                to = k * CHUNK + xh * 128
                normed_ref[0, :, to : to + 128] = plain_ref[:, feature_columns(tab[2], k, xh)]
        mixed = jnp.dot(normed_ref[0], w_ref[...], preferred_element_type=F32)
        mixed_ref[0] = mixed
        output = x_ref[0].astype(F32) + mixed / (1.0 + jnp.exp(-mixed))
        keep = live_mask(tab, micro) | (block == N_SEC - 1)
        kept = jnp.where(keep, output, held_ref[0].astype(F32)).astype(BF)
        msg_ref[...] = kept
        kept_ref[0] = kept


def micro_block(tick, tab):
    return jnp.clip(tick - tab[1], 0, N_MICRO - 1)


def slot_block(tick, tab):
    micro = tick - tab[1]
    return jnp.where((micro >= 0) & (micro < N_MICRO), micro, N_MICRO)


def forward_tick(tick, tab, first, core, chip, held, weight, gain, stash):
    read = pl.BlockSpec((1, ROWS, D), lambda i, tab: (micro_block(tick, tab), 0, 0))
    slot = pl.BlockSpec((1, ROWS, D), lambda i, tab: (slot_block(tick, tab), 0, 0))
    return pl.pallas_call(
        functools.partial(forward_kernel, tick),
        grid_spec=pltpu.PrefetchScalarGridSpec(
            num_scalar_prefetch=1,
            grid=(1,),
            in_specs=[
                read, WHOLE, WHOLE, read,
                pl.BlockSpec((D, D), lambda i, tab: (0, 0)),
                pl.BlockSpec((1, D), lambda i, tab: (0, 0)),
                ANY, ANY, ANY, ANY,
            ],
            out_specs=[WHOLE, slot, slot, slot, slot],
            scratch_shapes=[pltpu.VMEM((ROWS, D), BF)],
        ),
        out_shape=[jax.ShapeDtypeStruct((ROWS, D), BF)]
        + [jax.ShapeDtypeStruct(s.shape, s.dtype) for s in stash],
        input_output_aliases={7: 1, 8: 2, 9: 3, 10: 4},
        compiler_params=PARAMS,
        cost_estimate=COST,
        name=f"forward_{tick}",
    )(tab, first, core, chip, held, weight, gain, *stash)


def backward_kernel(tick, tab, given_ref, core_ref, chip_ref, w_ref, gain_ref, x_ref, mixed_ref, *refs):
    early = tick < LAST
    sa, sb = refs[:2]
    msg_ref, x_out, mixed_out, sa_ref, sb_ref = refs[2:7]
    up_ref, slope_ref = refs[-2:]
    micro = tick - (LAST - tab[1])
    block = tab[0]
    active = (micro >= 0) & (micro < N_MICRO)

    @pl.when(active & (block == N_SEC - 1))
    def _():
        given = given_ref[0].astype(F32)
        up_ref[...] = jnp.where(live_mask(tab, micro), given, 0.0).astype(BF)

    @pl.when(active & (block % 2 == 0))
    def _():
        up_ref[...] = core_ref[...]

    @pl.when(active & (block % 2 == 1) & (block < N_SEC - 1))
    def _():
        up_ref[...] = chip_ref[...]

    @pl.when(active)
    def _():
        mixed = mixed_ref[0]
        gated = 1.0 / (1.0 + jnp.exp(-mixed))
        up = up_ref[...].astype(F32)
        slope_ref[...] = (up * gated * (1.0 + mixed * (1.0 - gated))).astype(BF)
        for j, out in enumerate((sa_ref, sb_ref)):
            out[0] = slope_ref[:, half_columns(tab[19] ^ j)]

    if not early:
        @pl.when(block == 0)
        def _():
            refs[7][...] = sa_ref[0]
            refs[8][...] = sb_ref[0]

        @pl.when(block != 0)
        def _():
            refs[7][...] = sa[0]
            refs[8][...] = sb[0]

    @pl.when(active & (block > 0))
    def _():
        back = lax.dot_general(
            slope_ref[...], w_ref[...], (((1,), (1,)), ((), ())), preferred_element_type=F32
        )
        values = x_ref[0].astype(F32)
        inverse = lax.rsqrt(jnp.mean(values * values, axis=1, keepdims=True) + EPS)
        total = jnp.zeros((ROWS, 128), F32)
        weighted = []
        for k in range(N_Z):
            for xh in range(2):
                cols = feature_columns(tab[2], k, xh)
                at = k * CHUNK + xh * 128
                part = back[:, at : at + 128] * gain_ref[:, cols].astype(F32)
                total = total + part * x_ref[0, :, cols].astype(F32)
                weighted.append((cols, part))
        centre = jnp.sum(total, axis=1, keepdims=True) * (1.0 / D)
        factor = inverse * inverse * inverse * centre
        for cols, part in weighted:
            grad = up_ref[:, cols].astype(F32) + inverse * part
            msg_ref[:, cols] = (grad - x_ref[0, :, cols].astype(F32) * factor).astype(BF)


def backward_tick(tick, tab, given, core, chip, weight, gain, stash, slopes):
    def micro_of(tab):
        return tick - (LAST - tab[1])

    def slot_of(tab):
        micro = micro_of(tab)
        return jnp.where((micro >= 0) & (micro < N_MICRO), micro, N_MICRO)

    read = pl.BlockSpec(
        (1, ROWS, D), lambda i, tab: (jnp.clip(micro_of(tab), 0, N_MICRO - 1), 0, 0)
    )
    slot = pl.BlockSpec((1, ROWS, HALF), lambda i, tab: (slot_of(tab), 0, 0))
    early = tick < LAST
    kept = ANY if early else pl.BlockSpec((1, ROWS, HALF), lambda i, tab: (tick - LAST, 0, 0))
    half = pl.BlockSpec((ROWS, HALF), lambda i, tab: (0, 0))
    out = pl.pallas_call(
        functools.partial(backward_kernel, tick),
        grid_spec=pltpu.PrefetchScalarGridSpec(
            num_scalar_prefetch=1,
            grid=(1,),
            in_specs=[
                read, WHOLE, WHOLE,
                pl.BlockSpec((D, D), lambda i, tab: (0, 0)),
                pl.BlockSpec((1, D), lambda i, tab: (0, 0)),
                read, read, kept, kept,
            ],
            out_specs=[WHOLE, ANY, ANY, slot, slot] + ([] if early else [half, half]),
            scratch_shapes=[pltpu.VMEM((ROWS, D), BF)] * 2,
        ),
        out_shape=[jax.ShapeDtypeStruct((ROWS, D), BF)]
        + [jax.ShapeDtypeStruct(s.shape, s.dtype) for s in (*stash, *slopes)]
        + ([] if early else [jax.ShapeDtypeStruct((ROWS, HALF), BF)] * 2),
        input_output_aliases={6: 1, 7: 2, 8: 3, 9: 4},
        compiler_params=PARAMS,
        cost_estimate=COST,
        name=f"backward_{tick}",
    )(tab, given, core, chip, weight, gain, *stash, *slopes)
    return out[0], out[1:3], out[3:5], out[5:]


def held_rows(slots, ids):
    long_part = jnp.take(slots, ids[:4], axis=0).reshape(-1, D)
    short_part = jnp.take(slots[:, :QTR], ids[4:], axis=0).reshape(-1, D)
    return jnp.concatenate([long_part, short_part], axis=0)


def body(embedded, out_grad, stored, sample_ids, lengths, weight, gain):
    section = lax.axis_index("section")
    data = lax.axis_index("dp")
    y, a = section // 2, section % 2
    xh, c = data // 16, data % 2
    z = (data // 2) % N_Z
    same = a == c
    block = 2 * y + c
    place = jnp.stack([xh, a, c])
    full, middle = gather_weight(place, weight[0])
    later = (middle[0, 0].astype(F32) * 0.0).astype(jnp.int32)
    y = y + later
    sample_ids = sample_ids + later

    ends = jnp.where(y == 0, embedded, out_grad)
    ends = jnp.where(same, ends, send(ends, CORES)).reshape(N_MICRO, ROWS, D)
    limits = jnp.where(same, lengths, send(lengths, CORES))
    gain_pair = send(gain, TURN)
    held = send(held_rows(stored[0, 1], sample_ids), TURN).reshape(N_MICRO, ROWS, D)
    long_limits = jnp.stack([limits[:4], limits[:4] - QTR], axis=1).reshape(-1)
    tab = jnp.concatenate([jnp.stack([block, 3 * y + c, z]), long_limits, limits[4:], a[None]])

    blank = jnp.zeros((ROWS, D), BF)
    stash = [
        jnp.zeros((N_MICRO + 1, ROWS, D), BF),
        jnp.zeros((N_MICRO + 1, ROWS, D), F32),
        jnp.zeros((N_MICRO + 1, ROWS, D), BF),
        jnp.zeros((N_MICRO + 1, ROWS, D), BF),
    ]
    slopes = [jnp.zeros((N_MICRO + 1, ROWS, HALF), BF) for _ in range(2)]
    normed, leaving = [], [[], []]
    up_core, up_chip = [blank], [blank, blank]
    down_core, down_chip = [blank], [blank, blank]
    kept = None
    for tick in range(LAST + TICKS):
        if tick < TICKS:
            msg, *stash = forward_tick(
                tick, tab, ends, up_core[tick], up_chip[tick], held, full, gain_pair, stash
            )
            if tick < TICKS - 1:
                up_core.append(send(msg, UP_CORE))
            if tick < TICKS - 2:
                up_chip.append(send(msg, UP_CHIP))
            if tick == TICKS - 1:
                normed = [send(stash[3][:N_MICRO], pairs) for pairs in TO_PLACE]
        if tick >= LAST:
            step = tick - LAST
            msg, stash[:2], slopes, halves = backward_tick(
                step, tab, ends, down_core[step], down_chip[step], full, gain_pair, stash[:2], slopes
            )
            if step < TICKS - 1:
                down_core.append(send(msg, DOWN_CORE))
            if step < TICKS - 2:
                down_chip.append(send(msg, DOWN_CHIP))
            for j, half in enumerate(halves):
                leaving[j].append(send(half, TO_PLACE[j]))

    after = (leaving[0][-1][0, 0].astype(F32) * 0.0).astype(jnp.int32)
    kept = lax.dynamic_slice(stash[2], (after, 0, 0), (N_MICRO, ROWS, D))
    kept = send(kept.reshape(-1, D), TURN)
    shard = scatter_grad(place, (*normed, *leaving[0], *leaving[1]), c)
    return (kept[None], shard[None])


def solution(mesh):
    in_specs = (
        P("dp", None),
        P("dp", None),
        P("section", None, "dp", None, None),
        P("dp"),
        P("dp"),
        P("section", "dp", None),
        P("section", None),
    )
    out_specs = (P("section", "dp", None), P("section", "dp", None))
    return jax.shard_map(body, mesh=mesh, in_specs=in_specs, out_specs=out_specs, check_vma=False)
```

```python
import functools

import jax
import jax.numpy as jnp
from jax import lax
from jax.experimental import pallas as pl
from jax.experimental.pallas import tpu as pltpu
from jax.sharding import PartitionSpec as P

D = 2048
QTR = 32
N_MICRO = 4
ROWS = 128
N_SEC = 8
N_Z = 8
LAST = 10
TICKS = LAST + N_MICRO
EPS = 1e-6
BF = jnp.bfloat16
F32 = jnp.float32
BOTH = ("section", "dp")


def device(y, a, xh, z, c):
    return (2 * y + a) * 32 + 16 * xh + 2 * z + c


def pairs_of(target):
    out = []
    for y in range(4):
        for a in range(2):
            for xh in range(2):
                for z in range(N_Z):
                    for c in range(2):
                        to = target(y, a, xh, z, c)
                        if to is not None:
                            out.append((device(y, a, xh, z, c), device(*to)))
    return out


TURN = pairs_of(lambda y, a, xh, z, c: (y, c, xh, z, a))
CORES = pairs_of(lambda y, a, xh, z, c: (y, a, xh, z, 1 - c))
RIGHT = pairs_of(lambda y, a, xh, z, c: (y, a, xh, (z + 1) % N_Z, c))
LEFT = pairs_of(lambda y, a, xh, z, c: (y, a, xh, (z - 1) % N_Z, c))
UP_CORE = pairs_of(lambda y, a, xh, z, c: (y, a, xh, z, 1) if c == 0 else None)
UP_CHIP = pairs_of(lambda y, a, xh, z, c: (y + 1, a, xh, z, 0) if c == 1 and y < 3 else None)
DOWN_CORE = pairs_of(lambda y, a, xh, z, c: (y, a, xh, z, 0) if c == 1 else None)
DOWN_CHIP = pairs_of(lambda y, a, xh, z, c: (y - 1, a, xh, z, 1) if c == 0 and y > 0 else None)
FAR_X = pairs_of(lambda y, a, xh, z, c: (y, a, 1 - xh, z, c))
FAR_X_CORE = pairs_of(lambda y, a, xh, z, c: (y, a, 1 - xh, z, 1 - c))
TO_PLACE = [pairs_of(lambda y, a, xh, z, c: (y, c, xh, z, a ^ j)) for j in range(2)]


def beside(y, a, xh, z, step, core):
    x = (2 * xh + a + step) % 4
    return (y, x % 2, x // 2, z, core)


TO_NEXT = pairs_of(
    lambda y, a, xh, z, c: beside(y, a, xh, z, 1, a) if c == 0 else (y, a, xh, z, 0) if a == 0 else None
)
TO_PREVIOUS = pairs_of(
    lambda y, a, xh, z, c: beside(y, a, xh, z, -1, a) if c == 1 else (y, a, xh, z, 1) if a == 1 else None
)

CHUNK = 256
HALF = 1024
QUARTER = 512
BATCHES = ((0, 7, 1), (6, 2), (5, 3), (4,))


def send(array, pairs):
    return lax.ppermute(array, BOTH, pairs)


ANY = pl.BlockSpec(memory_space=pl.ANY)
WHOLE = pl.BlockSpec((ROWS, D), lambda i, tab: (0, 0))
COST = pl.CostEstimate(flops=2 * ROWS * D * D, bytes_accessed=D * D * 2, transcendentals=ROWS * D)
PARAMS = pltpu.CompilerParams(vmem_limit_bytes=18 * 2**20)


def feature_columns(z, k, xh):
    return pl.ds(pl.multiple_of((xh * N_Z + lax.rem(z + k, N_Z)) * 128, 128), 128)


def whole(shape):
    return pl.BlockSpec(shape, lambda i, place: (0,) * len(shape))


def placed(kernel, name, place, arrays, outs):
    return pl.pallas_call(
        kernel,
        grid_spec=pltpu.PrefetchScalarGridSpec(
            num_scalar_prefetch=1,
            grid=(1,),
            in_specs=[whole(r.shape) for r in arrays],
            out_specs=[whole(shape) for shape, _ in outs],
        ),
        out_shape=[jax.ShapeDtypeStruct(shape, dtype) for shape, dtype in outs],
        compiler_params=pltpu.CompilerParams(vmem_limit_bytes=28 * 2**20),
        name=name,
    )(place, *arrays)


def half_columns(index):
    return pl.ds(pl.multiple_of(index * HALF, HALF), HALF)


def part_rows(index, rows):
    return pl.ds(pl.multiple_of(index * rows, rows), rows)


def divide_kernel(place, shard, mine, other):
    mine[...] = shard[:, half_columns(place[2])]
    other[...] = shard[:, half_columns(1 - place[2])]


def arrange_kernel(place, p00, p01, p10, p11, out):
    for dx, dt, part in ((0, 0, p00), (0, 1, p01), (1, 0, p10), (1, 1, p11)):
        out[part_rows((place[0] ^ dx) * 2 + (place[2] ^ dt), 64), :] = part[...]


def assemble_kernel(place, *refs):
    own, following, previous, out = refs[:9], refs[9:13], refs[13:17], refs[-2]
    same = place[1] == place[2]

    def fill(batches, half):
        columns = slice(half * HALF, (half + 1) * HALF)
        for ref, batch in zip(batches, BATCHES):
            for i, k in enumerate(batch):
                out[k * CHUNK : (k + 1) * CHUNK, columns] = ref[i * CHUNK : (i + 1) * CHUNK, :]

    for c, arrived in ((0, following), (1, previous)):

        @pl.when(same & (place[2] == c))
        def _():
            columns = slice(c * HALF, (c + 1) * HALF)
            for k in range(N_Z):
                if k != 4:
                    out[k * CHUNK : (k + 1) * CHUNK, columns] = own[k][...]
            out[4 * CHUNK : 4 * CHUNK + 128, columns] = own[4][...]
            out[4 * CHUNK + 128 : 5 * CHUNK, columns] = own[8][...]
            fill(arrived, 1 - c)

    @pl.when(jnp.logical_not(same))
    def _():
        fill(following, 0)
        fill(previous, 1)


def assemble(place, arrays, held, ready):
    return pl.pallas_call(
        assemble_kernel,
        grid_spec=pltpu.PrefetchScalarGridSpec(
            num_scalar_prefetch=1,
            grid=(1,),
            in_specs=[whole(r.shape) for r in arrays] + [ANY] * (1 + len(ready)),
            out_specs=[whole((D, D)), ANY],
        ),
        out_shape=[jax.ShapeDtypeStruct((D, D), BF), jax.ShapeDtypeStruct(held.shape, held.dtype)],
        input_output_aliases={len(arrays) + 1: 1},
        compiler_params=pltpu.CompilerParams(vmem_limit_bytes=28 * 2**20),
        name="assemble",
    )(place, *arrays, held, *ready)


def gather_weight(place, shard):
    quarter, chunk = ((64, HALF), BF), ((CHUNK, HALF), BF)
    mine, other = placed(divide_kernel, "divide", place, [shard], [quarter, quarter])
    parts = [mine, send(other, CORES), send(mine, FAR_X), send(other, FAR_X_CORE)]
    own = [None] * 9
    own[0] = placed(arrange_kernel, "arrange", place, parts, [chunk])[0]
    following, previous = [], []

    def pass_on(pieces):
        rows = jnp.concatenate(pieces, axis=0)
        following.append(send(rows, TO_NEXT))
        previous.append(send(rows, TO_PREVIOUS))

    for step in range(1, 4):
        own[-step % N_Z] = send(own[(1 - step) % N_Z], RIGHT)
        own[step] = send(own[step - 1], LEFT)
        pass_on([own[k] for k in BATCHES[step - 1]])
    own[4] = send(own[5][:128], RIGHT)
    own[8] = send(own[3][128:], LEFT)
    pass_on([own[4], own[8]])
    return [*own, *following, *previous], own[6]


def sample_of(group):
    early = group < 8
    return jnp.where(early, group // 2, group - 4), jnp.where(early, lax.rem(group, 2), 0)


def held_block(side):
    def index(group, ids, *rest):
        sample, half = sample_of(group)
        return (side * 12 + ids[sample], half, 0, 0)

    return pl.BlockSpec((1, 1, QTR, D), index)


def held_rows(ids, stored):
    def kernel(ids, held_ref, out_ref):
        out_ref[...] = held_ref[0, 0]

    return pl.pallas_call(
        kernel,
        grid_spec=pltpu.PrefetchScalarGridSpec(
            num_scalar_prefetch=1,
            grid=(16,),
            in_specs=[held_block(0)],
            out_specs=pl.BlockSpec((QTR, D), lambda g, ids: (g, 0)),
        ),
        out_shape=jax.ShapeDtypeStruct((N_MICRO * ROWS, D), BF),
        compiler_params=PARAMS,
        name="held_rows",
    )(ids, stored)


def boundary_rows(ids, limits, kept, stored):
    def kernel(ids, limits, kept_ref, held_ref, out_ref):
        sample, half = sample_of(pl.program_id(0))
        row = lax.broadcasted_iota(jnp.int32, (QTR, 1), 0) + half * QTR
        live = (row < limits[sample]) | (limits[12] == 1)
        value = jnp.where(live, kept_ref[...].astype(F32), held_ref[0, 0].astype(F32))
        out_ref[...] = value.astype(BF)

    rows = pl.BlockSpec((QTR, D), lambda g, *tables: (g, 0))
    return pl.pallas_call(
        kernel,
        grid_spec=pltpu.PrefetchScalarGridSpec(
            num_scalar_prefetch=2, grid=(16,), in_specs=[rows, held_block(1)], out_specs=rows
        ),
        out_shape=jax.ShapeDtypeStruct((N_MICRO * ROWS, D), BF),
        compiler_params=PARAMS,
        name="boundary_rows",
    )(ids, limits, kept, stored)


def product_kernel(has, *refs):
    rows = N_MICRO * ROWS
    total = jnp.zeros((CHUNK, QUARTER), F32)
    for j in range(2):
        slope = jnp.concatenate([ref[...] for ref in refs[2 + 4 * j : 6 + 4 * j]], axis=0)
        total = total + lax.dot_general(
            refs[j][...].reshape(rows, CHUNK),
            slope,
            (((0,), (0,)), ((), ())),
            preferred_element_type=F32,
        )
    for ref in refs[10 : 10 + has]:
        total = total + ref[...].astype(F32)
    refs[-1][...] = total.astype(BF)


def product(sums, k, part, arrived):
    piece = pl.BlockSpec((CHUNK, QUARTER), lambda i: (0, 0))
    return pl.pallas_call(
        functools.partial(product_kernel, len(arrived)),
        grid=(1,),
        in_specs=[pl.BlockSpec((N_MICRO, ROWS, CHUNK), lambda i: (0, 0, k))] * 2
        + [pl.BlockSpec((ROWS, QUARTER), lambda i: (0, part))] * 8
        + [piece] * len(arrived),
        out_specs=piece,
        out_shape=jax.ShapeDtypeStruct((CHUNK, QUARTER), BF),
        compiler_params=PARAMS,
        cost_estimate=pl.CostEstimate(
            flops=4 * N_MICRO * ROWS * CHUNK * QUARTER, bytes_accessed=2**21, transcendentals=0
        ),
        name=f"product_{k}_{part}",
    )(*sums, *arrived)


def split_x_kernel(place, q0, q1, mine, other):
    for out, xh in ((mine, place[0]), (other, 1 - place[0])):
        rows = part_rows(xh, 128)
        out[:, :QUARTER] = q0[rows, :]
        out[:, QUARTER:] = q1[rows, :]


def split_core_kernel(place, mine, arrived, own, other, total):
    total[...] = mine[...].astype(F32) + arrived[...].astype(F32)
    own[...] = total[part_rows(place[2], 64), :]
    other[...] = total[part_rows(1 - place[2], 64), :].astype(BF)


def scatter_grad(place, sums, core):
    to_right = [send(product(sums, 4, 0, []), RIGHT), None]
    to_left = [None, send(product(sums, 4, 1, []), LEFT)]
    for step in range(3, 0, -1):
        for part in (1, 0):
            held = to_right[part]
            to_right[part] = send(product(sums, step, part, [] if held is None else [held]), RIGHT)
            held = to_left[1 - part]
            to_left[1 - part] = send(
                product(sums, N_Z - step, 1 - part, [] if held is None else [held]), LEFT
            )
    quarters = [product(sums, 0, part, [to_right[part], to_left[part]]) for part in range(2)]
    block = ((128, HALF), BF)
    mine, other = placed(split_x_kernel, "split_x", place, quarters, [block, block])
    arrived = send(other, FAR_X)
    own, other, _ = placed(
        split_core_kernel, "split_core", place, [mine, arrived],
        [((64, HALF), F32), ((64, HALF), BF), ((128, HALF), F32)],
    )
    arrived = send(other, CORES).astype(F32)
    return jnp.where(
        core == 0,
        jnp.concatenate([own, arrived], axis=1),
        jnp.concatenate([arrived, own], axis=1),
    )


def live_mask(tab, micro):
    row = lax.broadcasted_iota(jnp.int32, (ROWS, 1), 0)
    if micro < 2:
        limit = jnp.where(row < 64, tab[4 + 2 * micro], tab[5 + 2 * micro])
        return row % 64 < limit
    limit = jnp.zeros((ROWS, 1), jnp.int32)
    for q in range(4):
        limit = jnp.where(row // QTR == q, tab[4 * micro + q], limit)
    return row % QTR < limit


def slot_block(micro):
    return jnp.where((micro >= 0) & (micro < N_MICRO), micro, N_MICRO)


def forward_kernel(tick, names, tab, *refs):
    ref = dict(zip(names, refs))
    micro = tick - tab[1]
    block = tab[0]
    active = (micro >= 0) & (micro < N_MICRO)
    x_ref, normed_ref, plain_ref = ref["x"], ref["normed"], refs[-1]

    if "first" in ref:

        @pl.when(active & (block == 0) & (tab[3] == 0))
        def _():
            x_ref[0] = ref["first"][...]

        @pl.when(active & (block == 0) & (tab[3] == 1))
        def _():
            x_ref[0] = ref["first_other"][...]

    if "core" in ref:

        @pl.when(active & (block % 2 == 1))
        def _():
            x_ref[0] = ref["core"][...]

    if "chip" in ref:

        @pl.when(active & (block % 2 == 0) & (block > 0))
        def _():
            x_ref[0] = ref["chip"][...]

    if "held" in ref:

        @pl.when(block == N_SEC - 1)
        def _():
            live = live_mask(tab, tick - LAST)
            x = jnp.where(live, x_ref[0].astype(F32), ref["held"][...].astype(F32))
            x_ref[0] = x.astype(BF)

    @pl.when(active)
    def _():
        values = x_ref[0].astype(F32)
        inverse = lax.rsqrt(jnp.mean(values * values, axis=1, keepdims=True) + EPS)
        plain_ref[...] = (values * inverse * ref["gain"][...].astype(F32)).astype(BF)
        for k in range(N_Z):
            for xh in range(2):
                to = k * CHUNK + xh * 128
                normed_ref[0, :, to : to + 128] = plain_ref[:, feature_columns(tab[2], k, xh)]
        mixed = jnp.dot(normed_ref[0], ref["weight"][...], preferred_element_type=F32)
        ref["mixed"][0] = mixed
        output = (x_ref[0].astype(F32) + mixed / (1.0 + jnp.exp(-mixed))).astype(BF)
        ref["msg"][...] = output
        ref["kept"][0] = output


STASH = {"x": BF, "mixed": F32, "kept": BF, "normed": BF}


def forward_tick(tick, tab, blocks, weight, gain, stash, wait_for):
    slot = pl.BlockSpec((1, ROWS, D), lambda i, tab: (slot_block(tick - tab[1]), 0, 0))
    names = [*blocks, "weight", "gain"]
    arrays = [array for array, _ in blocks.values()] + [weight, gain]
    specs = [pl.BlockSpec((ROWS, D), lambda i, tab, at=at: (at, 0)) for _, at in blocks.values()]
    specs += [whole((D, D)), whole((1, D))]
    old = [] if stash is None else list(stash)
    aliases = {1 + len(arrays) + i: 1 + i for i in range(len(old))}
    names += [None] * (len(old) + len(wait_for)) + ["msg", *STASH]
    return pl.pallas_call(
        functools.partial(forward_kernel, tick, names),
        grid_spec=pltpu.PrefetchScalarGridSpec(
            num_scalar_prefetch=1,
            grid=(1,),
            in_specs=specs + [ANY] * (len(old) + len(wait_for)),
            out_specs=[WHOLE] + [slot] * 4,
            scratch_shapes=[pltpu.VMEM((ROWS, D), BF)],
        ),
        out_shape=[jax.ShapeDtypeStruct((ROWS, D), BF)]
        + [jax.ShapeDtypeStruct((N_MICRO + 1, ROWS, D), kind) for kind in STASH.values()],
        input_output_aliases=aliases,
        compiler_params=PARAMS,
        cost_estimate=COST,
        name=f"forward_{tick}",
    )(tab, *arrays, *old, *wait_for)


def backward_kernel(tick, names, tab, *refs):
    ref = dict(zip(names, refs))
    up_ref, slope_ref = refs[-2:]
    x_ref, msg_ref = ref["x"], ref["msg"]
    micro = tick - (LAST - tab[1])
    block = tab[0]
    active = (micro >= 0) & (micro < N_MICRO)

    if "given" in ref:
        for a, name in ((1, "given"), (0, "given_other")):

            @pl.when(active & (block == N_SEC - 1) & (tab[3] == a))
            def _():
                given = ref[name][...].astype(F32)
                up_ref[...] = jnp.where(live_mask(tab, tick), given, 0.0).astype(BF)

    if "core" in ref:

        @pl.when(active & (block % 2 == 0))
        def _():
            up_ref[...] = ref["core"][...]

    if "chip" in ref:

        @pl.when(active & (block % 2 == 1) & (block < N_SEC - 1))
        def _():
            up_ref[...] = ref["chip"][...]

    @pl.when(active)
    def _():
        mixed = ref["mixed"][0]
        gated = 1.0 / (1.0 + jnp.exp(-mixed))
        up = up_ref[...].astype(F32)
        slope_ref[...] = (up * gated * (1.0 + mixed * (1.0 - gated))).astype(BF)
        for j, name in enumerate(("slope_0", "slope_1")):
            ref[name][0] = slope_ref[:, half_columns(tab[3] ^ j)]

    if tick >= LAST:
        for source, condition in (("slope", block == 0), ("old", block != 0)):

            @pl.when(condition)
            def _():
                for j in "01":
                    ref["leave_" + j][...] = ref[source + "_" + j][0]

    @pl.when(active & (block > 0))
    def _():
        back = lax.dot_general(
            slope_ref[...], ref["weight"][...], (((1,), (1,)), ((), ())), preferred_element_type=F32
        )
        values = x_ref[0].astype(F32)
        inverse = lax.rsqrt(jnp.mean(values * values, axis=1, keepdims=True) + EPS)
        total = jnp.zeros((ROWS, 128), F32)
        weighted = []
        for k in range(N_Z):
            for xh in range(2):
                cols = feature_columns(tab[2], k, xh)
                at = k * CHUNK + xh * 128
                part = back[:, at : at + 128] * ref["gain"][:, cols].astype(F32)
                total = total + part * x_ref[0, :, cols].astype(F32)
                weighted.append((cols, part))
        centre = jnp.sum(total, axis=1, keepdims=True) * (1.0 / D)
        factor = inverse * inverse * inverse * centre
        for cols, part in weighted:
            grad = up_ref[:, cols].astype(F32) + inverse * part
            msg_ref[:, cols] = (grad - x_ref[0, :, cols].astype(F32) * factor).astype(BF)


def backward_tick(tick, tab, blocks, weight, gain, stash, slopes, wait_for):
    def micro_of(tab):
        return tick - (LAST - tab[1])

    read = pl.BlockSpec(
        (1, ROWS, D), lambda i, tab: (jnp.clip(micro_of(tab), 0, N_MICRO - 1), 0, 0)
    )
    slot = pl.BlockSpec((1, ROWS, HALF), lambda i, tab: (slot_block(micro_of(tab)), 0, 0))
    late = tick >= LAST
    names = [*blocks, "weight", "gain", "x", "mixed"]
    arrays = [array for array, _ in blocks.values()] + [weight, gain, *stash]
    specs = [pl.BlockSpec((ROWS, D), lambda i, tab, at=at: (at, 0)) for _, at in blocks.values()]
    specs += [whole((D, D)), whole((1, D)), read, read]
    aliases = {len(arrays) - 1: 1, len(arrays): 2}
    if slopes is not None:
        aliases |= {len(arrays) + 1: 3, len(arrays) + 2: 4}
        arrays += slopes
        names += ["old_0", "old_1"]
        specs += [
            pl.BlockSpec((1, ROWS, HALF), lambda i, tab: (tick - LAST, 0, 0)) if late else ANY
        ] * 2
    names += [None] * len(wait_for) + ["msg", None, None, "slope_0", "slope_1"]
    names += ["leave_0", "leave_1"] if late else []
    half = jax.ShapeDtypeStruct((ROWS, HALF), BF)
    kept = jax.ShapeDtypeStruct((N_MICRO + 1, ROWS, HALF), BF)
    out = pl.pallas_call(
        functools.partial(backward_kernel, tick, names),
        grid_spec=pltpu.PrefetchScalarGridSpec(
            num_scalar_prefetch=1,
            grid=(1,),
            in_specs=specs + [ANY] * len(wait_for),
            out_specs=[WHOLE, ANY, ANY, slot, slot] + [whole((ROWS, HALF))] * (2 * late),
            scratch_shapes=[pltpu.VMEM((ROWS, D), BF)] * 2,
        ),
        out_shape=[jax.ShapeDtypeStruct((ROWS, D), BF)]
        + [jax.ShapeDtypeStruct(s.shape, s.dtype) for s in stash]
        + [kept, kept]
        + [half] * (2 * late),
        input_output_aliases=aliases,
        compiler_params=PARAMS,
        cost_estimate=COST,
        name=f"backward_{tick}",
    )(tab, *arrays, *wait_for)
    return out[0], out[1:3], out[3:5], out[5:]


def body(embedded, out_grad, stored, sample_ids, lengths, weight, gain):
    section = lax.axis_index("section")
    data = lax.axis_index("dp")
    y, a = section // 2, section % 2
    xh, c = data // 16, data % 2
    z = (data // 2) % N_Z
    place = jnp.stack([xh, a, c])
    table = jnp.stack([2 * y + c, 3 * y + c, z, a])
    stored = stored.reshape(24, 2, QTR, D)

    embedded_other = send(embedded, CORES)
    pieces, middle = gather_weight(place, weight[0])
    gain_row = send(gain, TURN)
    later = (middle[0, 0].astype(F32) * 0.0).astype(jnp.int32)
    grad_other = send(out_grad, CORES)
    limits = jnp.where(a == c, lengths, send(lengths, CORES))
    late_table = jnp.concatenate([table, limits])
    held = held_rows(sample_ids + later, stored)
    full, held = assemble(place, pieces, held, [embedded_other, grad_other, gain_row, late_table])
    held = send(held, TURN)

    stash = slopes = None
    normed, leaving = [], [[], []]
    up_core, up_chip, down_core, down_chip = {}, {}, {}, {}
    for tick in range(LAST + TICKS):
        if tick < TICKS:
            blocks = {}
            if tick < N_MICRO:
                blocks["first"] = (embedded, tick)
                blocks["first_other"] = (embedded_other, tick)
            if tick in up_core:
                blocks["core"] = (up_core[tick], 0)
            if tick in up_chip:
                blocks["chip"] = (up_chip[tick], 0)
            if tick >= LAST:
                blocks["held"] = (held, tick - LAST)
            msg, *stash = forward_tick(
                tick,
                late_table if tick >= LAST else table,
                blocks,
                full,
                gain_row,
                stash,
                [held] if tick == LAST - 1 else [],
            )
            if tick < TICKS - 1:
                up_core[tick + 1] = send(msg, UP_CORE)
            if 1 <= tick <= LAST:
                up_chip[tick + 2] = send(msg, UP_CHIP)
            if tick == TICKS - 1:
                normed.append(send(stash[3][:N_MICRO], TURN))
                normed.append(send(normed[0], CORES))
        if tick >= LAST:
            step = tick - LAST
            blocks = {}
            if step < N_MICRO:
                blocks["given"] = (out_grad, step)
                blocks["given_other"] = (grad_other, step)
            if step in down_core:
                blocks["core"] = (down_core[step], 0)
            if step in down_chip:
                blocks["chip"] = (down_chip[step], 0)
            msg, stash[:2], slopes, halves = backward_tick(
                step,
                late_table if step < N_MICRO else table,
                blocks,
                full,
                gain_row,
                stash[:2],
                slopes,
                {8: normed[:1], 10: normed[1:]}.get(step, []),
            )
            if step < TICKS - 1:
                down_core[step + 1] = send(msg, DOWN_CORE)
            if 1 <= step <= LAST:
                down_chip[step + 2] = send(msg, DOWN_CHIP)
            for j, half in enumerate(halves):
                leaving[j].append(send(half, TO_PLACE[j]))

    after = (leaving[0][-1][0, 0].astype(F32) * 0.0).astype(jnp.int32)
    kept = lax.dynamic_slice(stash[2], (after, 0, 0), (N_MICRO, ROWS, D))
    kept = send(kept.reshape(-1, D), TURN)
    last = (section == N_SEC - 1).astype(jnp.int32)
    boundary = boundary_rows(sample_ids, jnp.concatenate([lengths, last[None]]), kept, stored)
    shard = scatter_grad(place, (*normed, *leaving[0], *leaving[1]), c)
    return (boundary[None], shard[None])


def solution(mesh):
    in_specs = (
        P("dp", None),
        P("dp", None),
        P("section", None, "dp", None, None),
        P("dp"),
        P("dp"),
        P("section", "dp", None),
        P("section", None),
    )
    out_specs = (P("section", "dp", None), P("section", "dp", None))
    return jax.shard_map(body, mesh=mesh, in_specs=in_specs, out_specs=out_specs, check_vma=False)
```

```python
import functools

import jax
import jax.numpy as jnp
from jax import lax
from jax.experimental import pallas as pl
from jax.experimental.pallas import tpu as pltpu
from jax.sharding import PartitionSpec as P

D = 2048
QTR = 32
N_MICRO = 4
ROWS = 128
N_SEC = 8
N_Z = 8
LAST = 10
TICKS = LAST + N_MICRO
EPS = 1e-6
BF = jnp.bfloat16
F32 = jnp.float32
BOTH = ("section", "dp")


def device(y, a, xh, z, c):
    return (2 * y + a) * 32 + 16 * xh + 2 * z + c


def pairs_of(target):
    out = []
    for y in range(4):
        for a in range(2):
            for xh in range(2):
                for z in range(N_Z):
                    for c in range(2):
                        to = target(y, a, xh, z, c)
                        if to is not None:
                            out.append((device(y, a, xh, z, c), device(*to)))
    return out


TURN = pairs_of(lambda y, a, xh, z, c: (y, c, xh, z, a))
CORES = pairs_of(lambda y, a, xh, z, c: (y, a, xh, z, 1 - c))
RIGHT = pairs_of(lambda y, a, xh, z, c: (y, a, xh, (z + 1) % N_Z, c))
LEFT = pairs_of(lambda y, a, xh, z, c: (y, a, xh, (z - 1) % N_Z, c))
UP_CORE = pairs_of(lambda y, a, xh, z, c: (y, a, xh, z, 1) if c == 0 else None)
UP_CHIP = pairs_of(lambda y, a, xh, z, c: (y + 1, a, xh, z, 0) if c == 1 and y < 3 else None)
DOWN_CORE = pairs_of(lambda y, a, xh, z, c: (y, a, xh, z, 0) if c == 1 else None)
DOWN_CHIP = pairs_of(lambda y, a, xh, z, c: (y - 1, a, xh, z, 1) if c == 0 and y > 0 else None)
FAR_X = pairs_of(lambda y, a, xh, z, c: (y, a, 1 - xh, z, c))
FAR_X_CORE = pairs_of(lambda y, a, xh, z, c: (y, a, 1 - xh, z, 1 - c))
TO_PLACE = [pairs_of(lambda y, a, xh, z, c: (y, c, xh, z, a ^ j)) for j in range(2)]


def beside(y, a, xh, z, step, core):
    x = (2 * xh + a + step) % 4
    return (y, x % 2, x // 2, z, core)


TO_NEXT = pairs_of(
    lambda y, a, xh, z, c: beside(y, a, xh, z, 1, a) if c == 0 else (y, a, xh, z, 0) if a == 0 else None
)
TO_PREVIOUS = pairs_of(
    lambda y, a, xh, z, c: beside(y, a, xh, z, -1, a) if c == 1 else (y, a, xh, z, 1) if a == 1 else None
)

CHUNK = 256
HALF = 1024
QUARTER = 512


def send(array, pairs):
    return lax.ppermute(array, BOTH, pairs)


ANY = pl.BlockSpec(memory_space=pl.ANY)
WHOLE = pl.BlockSpec((ROWS, D), lambda i, tab: (0, 0))
COST = pl.CostEstimate(flops=2**20, bytes_accessed=2**18, transcendentals=0)
PARAMS = pltpu.CompilerParams(vmem_limit_bytes=18 * 2**20)


def feature_columns(z, k, xh):
    return pl.ds(pl.multiple_of((xh * N_Z + lax.rem(z + k, N_Z)) * 128, 128), 128)


def whole(shape):
    return pl.BlockSpec(shape, lambda i, place: (0,) * len(shape))


def placed(kernel, name, place, arrays, outs):
    return pl.pallas_call(
        kernel,
        grid_spec=pltpu.PrefetchScalarGridSpec(
            num_scalar_prefetch=1,
            grid=(1,),
            in_specs=[whole(r.shape) for r in arrays],
            out_specs=[whole(shape) for shape, _ in outs],
        ),
        out_shape=[jax.ShapeDtypeStruct(shape, dtype) for shape, dtype in outs],
        compiler_params=pltpu.CompilerParams(vmem_limit_bytes=28 * 2**20),
        name=name,
    )(place, *arrays)


def half_columns(index):
    return pl.ds(pl.multiple_of(index * HALF, HALF), HALF)


def part_rows(index, rows):
    return pl.ds(pl.multiple_of(index * rows, rows), rows)


def divide_kernel(place, shard, mine, other):
    mine[...] = shard[:, half_columns(place[2])]
    other[...] = shard[:, half_columns(1 - place[2])]


def arrange_kernel(place, p00, p01, p10, p11, out):
    for dx, dt, part in ((0, 0, p00), (0, 1, p01), (1, 0, p10), (1, 1, p11)):
        out[part_rows((place[0] ^ dx) * 2 + (place[2] ^ dt), 64), :] = part[...]


def pack(pieces, wait_for):
    rows = sum(piece.shape[0] for piece in pieces)

    def kernel(*refs):
        out, at = refs[len(pieces) + len(wait_for)], 0
        for piece in refs[: len(pieces)]:
            out[at : at + piece.shape[0], :] = piece[...]
            at += piece.shape[0]

    return pl.pallas_call(
        kernel,
        grid=(1,),
        in_specs=[pl.BlockSpec(p.shape, lambda i: (0, 0)) for p in pieces] + [ANY] * len(wait_for),
        out_specs=[pl.BlockSpec((rows, HALF), lambda i: (0, 0))] + [ANY] * len(pieces),
        out_shape=[jax.ShapeDtypeStruct((rows, HALF), BF)]
        + [jax.ShapeDtypeStruct(p.shape, BF) for p in pieces],
        input_output_aliases={i: 1 + i for i in range(len(pieces))},
        compiler_params=PARAMS,
        name="pack",
    )(*pieces, *wait_for)


def place_chunk(place, k, full, own, following, previous, at, wait_for):
    count = len(own)
    skip = 0 if full is None else 1

    def kernel(place, *refs):
        pieces, arrived, out = refs[:count], refs[count : count + 2], refs[count + 2 + skip + len(wait_for)]
        same = place[1] == place[2]
        for c in range(2):

            @pl.when(same & (place[2] == c))
            def _():
                row = 0
                for piece in pieces:
                    out[row : row + piece.shape[0], c * HALF : (c + 1) * HALF] = piece[...]
                    row += piece.shape[0]
                out[:, (1 - c) * HALF : (2 - c) * HALF] = arrived[c][...]

        @pl.when(jnp.logical_not(same))
        def _():
            for c in range(2):
                out[:, c * HALF : (c + 1) * HALF] = arrived[c][...]

    block = pl.BlockSpec((CHUNK, HALF), lambda i, place: (at, 0))
    old = [] if full is None else [full]
    return pl.pallas_call(
        kernel,
        grid_spec=pltpu.PrefetchScalarGridSpec(
            num_scalar_prefetch=1,
            grid=(1,),
            in_specs=[whole(p.shape) for p in own] + [block] * 2 + [ANY] * (skip + len(wait_for)),
            out_specs=pl.BlockSpec((CHUNK, D), lambda i, place: (k, 0)),
        ),
        out_shape=jax.ShapeDtypeStruct((D, D), BF),
        input_output_aliases={} if full is None else {count + 3: 0},
        compiler_params=PARAMS,
        name=f"place_{k}",
    )(place, *own, following, previous, *old, *wait_for)


def gather_weight(place, shard, prepare):
    quarter, chunk = ((64, HALF), BF), ((CHUNK, HALF), BF)
    mine, other = placed(divide_kernel, "divide", place, [shard], [quarter, quarter])
    parts = [mine, send(other, CORES), send(mine, FAR_X), send(other, FAR_X_CORE)]
    first = placed(arrange_kernel, "arrange", place, parts, [chunk])[0]
    right, left, rows = first, first, first
    order = [(0, 0)]
    own = {0: [first]}
    full = None
    for step in range(1, 6):
        if step < 4:
            right, left = send(right, RIGHT), send(left, LEFT)
        elif step == 4:
            right, left = send(right[:128], RIGHT), send(left[128:], LEFT)
        moved = [send(rows, TO_NEXT), send(rows, TO_PREVIOUS)]
        if step < 5:
            rows, right, left = pack([right, left], moved)
        ready = prepare(right) if step == 2 else ready if step > 2 else []
        for k, at in order:
            full = place_chunk(place, k, full, own[k], *moved, at, ready if k == 4 else [])
        order = [(-step % N_Z, 0), (step, 1)] if step < 4 else [(4, 0)]
        if step < 4:
            own[-step % N_Z], own[step] = [right], [left]
        else:
            own[4] = [right, left]
    return full, ready


def sample_of(group):
    early = group < 8
    return jnp.where(early, group // 2, group - 4), jnp.where(early, lax.rem(group, 2), 0)


def held_block(side):
    def index(group, ids, *rest):
        sample, half = sample_of(group)
        return (side * 12 + ids[sample], half, 0, 0)

    return pl.BlockSpec((1, 1, QTR, D), index)


def held_rows(ids, stored):
    def kernel(ids, held_ref, out_ref):
        out_ref[...] = held_ref[0, 0]

    return pl.pallas_call(
        kernel,
        grid_spec=pltpu.PrefetchScalarGridSpec(
            num_scalar_prefetch=1,
            grid=(16,),
            in_specs=[held_block(0)],
            out_specs=pl.BlockSpec((QTR, D), lambda g, ids: (g, 0)),
        ),
        out_shape=jax.ShapeDtypeStruct((N_MICRO * ROWS, D), BF),
        compiler_params=PARAMS,
        name="held_rows",
    )(ids, stored)


def boundary_rows(ids, limits, kept, stored):
    def held_at(quarter):
        def index(micro, ids, limits):
            sample, half = sample_of(micro * 4 + quarter)
            return (12 + ids[sample], half, 0, 0)

        return pl.BlockSpec((1, 1, QTR, D), index)

    def kernel(ids, limits, kept_ref, h0, h1, h2, h3, out_ref):
        for quarter, held_ref in enumerate((h0, h1, h2, h3)):
            sample, half = sample_of(pl.program_id(0) * 4 + quarter)
            row = lax.broadcasted_iota(jnp.int32, (QTR, 1), 0) + half * QTR
            live = (row < limits[sample]) | (limits[12] == 1)
            rows = slice(quarter * QTR, (quarter + 1) * QTR)
            value = jnp.where(live, kept_ref[0, rows, :].astype(F32), held_ref[0, 0].astype(F32))
            out_ref[0, rows, :] = value.astype(BF)

    return pl.pallas_call(
        kernel,
        grid_spec=pltpu.PrefetchScalarGridSpec(
            num_scalar_prefetch=2,
            grid=(N_MICRO,),
            in_specs=[pl.BlockSpec((1, ROWS, D), lambda m, *tables: (m, 0, 0))]
            + [held_at(quarter) for quarter in range(4)],
            out_specs=pl.BlockSpec((1, ROWS, D), lambda m, *tables: (0, m, 0)),
        ),
        out_shape=jax.ShapeDtypeStruct((1, N_MICRO * ROWS, D), BF),
        compiler_params=PARAMS,
        name="boundary_rows",
    )(ids, limits, kept, stored, stored, stored, stored)


def product_kernel(has, *refs):
    rows = N_MICRO * ROWS
    total = jnp.zeros((CHUNK, QUARTER), F32)
    for j in range(2):
        slope = jnp.concatenate([ref[...] for ref in refs[2 + 4 * j : 6 + 4 * j]], axis=0)
        total = total + lax.dot_general(
            refs[j][...].reshape(rows, CHUNK),
            slope,
            (((0,), (0,)), ((), ())),
            preferred_element_type=F32,
        )
    for ref in refs[10 : 10 + has]:
        total = total + ref[...].astype(F32)
    refs[-1][...] = total.astype(BF)


def product(sums, k, part, arrived):
    piece = pl.BlockSpec((CHUNK, QUARTER), lambda i: (0, 0))
    return pl.pallas_call(
        functools.partial(product_kernel, len(arrived)),
        grid=(1,),
        in_specs=[pl.BlockSpec((N_MICRO, ROWS, CHUNK), lambda i: (0, 0, k))] * 2
        + [pl.BlockSpec((ROWS, QUARTER), lambda i: (0, part))] * 8
        + [piece] * len(arrived),
        out_specs=piece,
        out_shape=jax.ShapeDtypeStruct((CHUNK, QUARTER), BF),
        compiler_params=PARAMS,
        cost_estimate=COST,
        name=f"product_{k}_{part}",
    )(*sums, *arrived)


def split_x_kernel(place, q0, q1, mine, other):
    for out, xh in ((mine, place[0]), (other, 1 - place[0])):
        rows = part_rows(xh, 128)
        out[:, :QUARTER] = q0[rows, :]
        out[:, QUARTER:] = q1[rows, :]


def split_core_kernel(place, mine, arrived, own, other, total):
    total[...] = mine[...].astype(F32) + arrived[...].astype(F32)
    own[...] = total[part_rows(place[2], 64), :]
    other[...] = total[part_rows(1 - place[2], 64), :].astype(BF)


def scatter_grad(place, sums, core):
    to_right = [send(product(sums, 4, 0, []), RIGHT), None]
    to_left = [None, send(product(sums, 4, 1, []), LEFT)]
    for step in range(3, 0, -1):
        for part in (1, 0):
            held = to_right[part]
            to_right[part] = send(product(sums, step, part, [] if held is None else [held]), RIGHT)
            held = to_left[1 - part]
            to_left[1 - part] = send(
                product(sums, N_Z - step, 1 - part, [] if held is None else [held]), LEFT
            )
    quarters = [product(sums, 0, part, [to_right[part], to_left[part]]) for part in range(2)]
    block = ((128, HALF), BF)
    mine, other = placed(split_x_kernel, "split_x", place, quarters, [block, block])
    arrived = send(other, FAR_X)
    own, other, _ = placed(
        split_core_kernel, "split_core", place, [mine, arrived],
        [((64, HALF), F32), ((64, HALF), BF), ((128, HALF), F32)],
    )
    arrived = send(other, CORES).astype(F32)
    return jnp.where(
        core == 0,
        jnp.concatenate([own, arrived], axis=1),
        jnp.concatenate([arrived, own], axis=1),
    )


def live_mask(tab, micro):
    row = lax.broadcasted_iota(jnp.int32, (ROWS, 1), 0)
    if micro < 2:
        limit = jnp.where(row < 64, tab[4 + 2 * micro], tab[5 + 2 * micro])
        return row % 64 < limit
    limit = jnp.zeros((ROWS, 1), jnp.int32)
    for q in range(4):
        limit = jnp.where(row // QTR == q, tab[4 * micro + q], limit)
    return row % QTR < limit


def slot_block(micro):
    return jnp.where((micro >= 0) & (micro < N_MICRO), micro, N_MICRO)


def forward_kernel(tick, names, tab, *refs):
    ref = dict(zip(names, refs))
    micro = tick - tab[1]
    block = tab[0]
    active = (micro >= 0) & (micro < N_MICRO)
    x_ref, normed_ref, plain_ref = ref["x"], ref["normed"], refs[-1]

    if "first" in ref:

        @pl.when(active & (block == 0) & (tab[3] == 0))
        def _():
            x_ref[0] = ref["first"][...]

        @pl.when(active & (block == 0) & (tab[3] == 1))
        def _():
            x_ref[0] = ref["first_other"][...]

    if "core" in ref:

        @pl.when(active & (block % 2 == 1))
        def _():
            x_ref[0] = ref["core"][...]

    if "chip" in ref:

        @pl.when(active & (block % 2 == 0) & (block > 0))
        def _():
            x_ref[0] = ref["chip"][...]

    if "held" in ref:

        @pl.when(block == N_SEC - 1)
        def _():
            live = live_mask(tab, tick - LAST)
            x = jnp.where(live, x_ref[0].astype(F32), ref["held"][...].astype(F32))
            x_ref[0] = x.astype(BF)

    @pl.when(active)
    def _():
        values = x_ref[0].astype(F32)
        inverse = lax.rsqrt(jnp.mean(values * values, axis=1, keepdims=True) + EPS)
        plain_ref[...] = (values * inverse * ref["gain"][...].astype(F32)).astype(BF)
        for k in range(N_Z):
            for xh in range(2):
                to = k * CHUNK + xh * 128
                normed_ref[0, :, to : to + 128] = plain_ref[:, feature_columns(tab[2], k, xh)]
        mixed = jnp.dot(normed_ref[0], ref["weight"][...], preferred_element_type=F32)
        ref["mixed"][0] = mixed
        output = (x_ref[0].astype(F32) + mixed / (1.0 + jnp.exp(-mixed))).astype(BF)
        ref["msg"][...] = output
        ref["kept"][0] = output


STASH = {"x": BF, "mixed": F32, "kept": BF, "normed": BF}


def forward_tick(tick, tab, blocks, weight, gain, stash, wait_for):
    slot = pl.BlockSpec((1, ROWS, D), lambda i, tab: (slot_block(tick - tab[1]), 0, 0))
    names = [*blocks, "weight", "gain"]
    arrays = [array for array, _ in blocks.values()] + [weight, gain]
    specs = [pl.BlockSpec((ROWS, D), lambda i, tab, at=at: (at, 0)) for _, at in blocks.values()]
    specs += [whole((D, D)), whole((1, D))]
    old = [] if stash is None else list(stash)
    aliases = {1 + len(arrays) + i: 1 + i for i in range(len(old))}
    names += [None] * (len(old) + len(wait_for)) + ["msg", *STASH]
    return pl.pallas_call(
        functools.partial(forward_kernel, tick, names),
        grid_spec=pltpu.PrefetchScalarGridSpec(
            num_scalar_prefetch=1,
            grid=(1,),
            in_specs=specs + [ANY] * (len(old) + len(wait_for)),
            out_specs=[WHOLE] + [slot] * 4,
            scratch_shapes=[pltpu.VMEM((ROWS, D), BF)],
        ),
        out_shape=[jax.ShapeDtypeStruct((ROWS, D), BF)]
        + [jax.ShapeDtypeStruct((N_MICRO + 1, ROWS, D), kind) for kind in STASH.values()],
        input_output_aliases=aliases,
        compiler_params=PARAMS,
        cost_estimate=COST,
        name=f"forward_{tick}",
    )(tab, *arrays, *old, *wait_for)


def backward_kernel(tick, names, tab, *refs):
    ref = dict(zip(names, refs))
    up_ref, slope_ref = refs[-2:]
    x_ref, msg_ref = ref["x"], ref["msg"]
    micro = tick - (LAST - tab[1])
    block = tab[0]
    active = (micro >= 0) & (micro < N_MICRO)

    if "given" in ref:
        for a, name in ((1, "given"), (0, "given_other")):

            @pl.when(active & (block == N_SEC - 1) & (tab[3] == a))
            def _():
                given = ref[name][...].astype(F32)
                up_ref[...] = jnp.where(live_mask(tab, tick), given, 0.0).astype(BF)

    if "core" in ref:

        @pl.when(active & (block % 2 == 0))
        def _():
            up_ref[...] = ref["core"][...]

    if "chip" in ref:

        @pl.when(active & (block % 2 == 1) & (block < N_SEC - 1))
        def _():
            up_ref[...] = ref["chip"][...]

    @pl.when(active)
    def _():
        mixed = ref["mixed"][0]
        gated = 1.0 / (1.0 + jnp.exp(-mixed))
        up = up_ref[...].astype(F32)
        slope_ref[...] = (up * gated * (1.0 + mixed * (1.0 - gated))).astype(BF)
        for j, name in enumerate(("slope_0", "slope_1")):
            ref[name][0] = slope_ref[:, half_columns(tab[3] ^ j)]

    if tick >= LAST:
        for source, condition in (("slope", block == 0), ("old", block != 0)):

            @pl.when(condition)
            def _():
                for j in "01":
                    ref["leave_" + j][...] = ref[source + "_" + j][0]

    @pl.when(active & (block > 0))
    def _():
        back = lax.dot_general(
            slope_ref[...], ref["weight"][...], (((1,), (1,)), ((), ())), preferred_element_type=F32
        )
        values = x_ref[0].astype(F32)
        inverse = lax.rsqrt(jnp.mean(values * values, axis=1, keepdims=True) + EPS)
        total = jnp.zeros((ROWS, 128), F32)
        weighted = []
        for k in range(N_Z):
            for xh in range(2):
                cols = feature_columns(tab[2], k, xh)
                at = k * CHUNK + xh * 128
                part = back[:, at : at + 128] * ref["gain"][:, cols].astype(F32)
                total = total + part * x_ref[0, :, cols].astype(F32)
                weighted.append((cols, part))
        centre = jnp.sum(total, axis=1, keepdims=True) * (1.0 / D)
        factor = inverse * inverse * inverse * centre
        for cols, part in weighted:
            grad = up_ref[:, cols].astype(F32) + inverse * part
            msg_ref[:, cols] = (grad - x_ref[0, :, cols].astype(F32) * factor).astype(BF)


def backward_tick(tick, tab, blocks, weight, gain, stash, slopes, wait_for):
    def micro_of(tab):
        return tick - (LAST - tab[1])

    read = pl.BlockSpec(
        (1, ROWS, D), lambda i, tab: (jnp.clip(micro_of(tab), 0, N_MICRO - 1), 0, 0)
    )
    slot = pl.BlockSpec((1, ROWS, HALF), lambda i, tab: (slot_block(micro_of(tab)), 0, 0))
    late = tick >= LAST
    names = [*blocks, "weight", "gain", "x", "mixed"]
    arrays = [array for array, _ in blocks.values()] + [weight, gain, *stash]
    specs = [pl.BlockSpec((ROWS, D), lambda i, tab, at=at: (at, 0)) for _, at in blocks.values()]
    specs += [whole((D, D)), whole((1, D)), read, read]
    aliases = {len(arrays) - 1: 1, len(arrays): 2}
    if slopes is not None:
        aliases |= {len(arrays) + 1: 3, len(arrays) + 2: 4}
        arrays += slopes
        names += ["old_0", "old_1"]
        specs += [
            pl.BlockSpec((1, ROWS, HALF), lambda i, tab: (tick - LAST, 0, 0)) if late else ANY
        ] * 2
    names += [None] * len(wait_for) + ["msg", None, None, "slope_0", "slope_1"]
    names += ["leave_0", "leave_1"] if late else []
    half = jax.ShapeDtypeStruct((ROWS, HALF), BF)
    kept = jax.ShapeDtypeStruct((N_MICRO + 1, ROWS, HALF), BF)
    out = pl.pallas_call(
        functools.partial(backward_kernel, tick, names),
        grid_spec=pltpu.PrefetchScalarGridSpec(
            num_scalar_prefetch=1,
            grid=(1,),
            in_specs=specs + [ANY] * len(wait_for),
            out_specs=[WHOLE, ANY, ANY, slot, slot] + [whole((ROWS, HALF))] * (2 * late),
            scratch_shapes=[pltpu.VMEM((ROWS, D), BF)] * 2,
        ),
        out_shape=[jax.ShapeDtypeStruct((ROWS, D), BF)]
        + [jax.ShapeDtypeStruct(s.shape, s.dtype) for s in stash]
        + [kept, kept]
        + [half] * (2 * late),
        input_output_aliases=aliases,
        compiler_params=PARAMS,
        cost_estimate=COST,
        name=f"backward_{tick}",
    )(tab, *arrays, *wait_for)
    return out[0], out[1:3], out[3:5], out[5:]


def hand_on(array, wait_for):
    def kernel(*refs):
        pass

    return pl.pallas_call(
        kernel,
        in_specs=[ANY, ANY],
        out_specs=ANY,
        out_shape=jax.ShapeDtypeStruct(array.shape, array.dtype),
        input_output_aliases={0: 0},
        compiler_params=PARAMS,
        name="hand_on",
    )(array, wait_for)


def body(embedded, out_grad, stored, sample_ids, lengths, weight, gain):
    section = lax.axis_index("section")
    data = lax.axis_index("dp")
    y, a = section // 2, section % 2
    xh, c = data // 16, data % 2
    z = (data // 2) % N_Z
    place = jnp.stack([xh, a, c])
    table = jnp.stack([2 * y + c, 3 * y + c, z, a])
    stored = stored.reshape(24, 2, QTR, D)

    embedded_other = send(embedded, CORES)
    gain_row = send(gain, TURN)

    def prepare(arrived):
        later = (arrived[0, 0].astype(F32) * 0.0).astype(jnp.int32)
        limits = jnp.where(a == c, lengths, send(lengths + later, CORES))
        held = held_rows(sample_ids + later, stored)
        return [held, jnp.concatenate([table, limits]), embedded_other, gain_row]

    full, ready = gather_weight(place, weight[0], prepare)
    held, late_table = ready[:2]
    held = send(held, TURN)
    grad_other = send(out_grad, CORES)

    stash = slopes = None
    kept, normed, leaving = None, [], [[], []]
    up_core, up_chip, down_core, down_chip = {}, {}, {}, {}
    for tick in range(LAST + TICKS):
        if tick < TICKS:
            blocks = {}
            if tick < N_MICRO:
                blocks["first"] = (embedded, tick)
                blocks["first_other"] = (embedded_other, tick)
            if tick in up_core:
                blocks["core"] = (up_core[tick], 0)
            if tick in up_chip:
                blocks["chip"] = (up_chip[tick], 0)
            if tick >= LAST:
                blocks["held"] = (held, tick - LAST)
            msg, *stash = forward_tick(
                tick,
                late_table if tick >= LAST else table,
                blocks,
                full,
                gain_row,
                stash,
                [held] if tick == LAST - 1 else [],
            )
            if tick < TICKS - 1:
                up_core[tick + 1] = send(msg, UP_CORE)
            if 1 <= tick <= LAST:
                up_chip[tick + 2] = send(msg, UP_CHIP)
            if tick == TICKS - 1:
                normed.append(send(stash[3], TURN))
                normed.append(send(normed[0], CORES))
                kept = send(hand_on(stash[2], normed[0]), TURN)
        if tick >= LAST:
            step = tick - LAST
            blocks = {}
            if step < N_MICRO:
                blocks["given"] = (out_grad, step)
                blocks["given_other"] = (grad_other, step)
            if step in down_core:
                blocks["core"] = (down_core[step], 0)
            if step in down_chip:
                blocks["chip"] = (down_chip[step], 0)
            msg, stash[:2], slopes, halves = backward_tick(
                step,
                late_table if step < N_MICRO else table,
                blocks,
                full,
                gain_row,
                stash[:2],
                slopes,
                {7: normed[:1], 9: normed[1:], 12: [kept]}.get(step, []),
            )
            if step < TICKS - 1:
                down_core[step + 1] = send(msg, DOWN_CORE)
            if 1 <= step <= LAST:
                down_chip[step + 2] = send(msg, DOWN_CHIP)
            for j, half in enumerate(halves):
                leaving[j].append(send(half, TO_PLACE[j]))

    last = (section == N_SEC - 1).astype(jnp.int32)
    boundary = boundary_rows(sample_ids, jnp.concatenate([lengths, last[None]]), kept, stored)
    shard = scatter_grad(place, (*normed, *leaving[0], *leaving[1]), c)
    return (boundary, shard[None])


def solution(mesh):
    in_specs = (
        P("dp", None),
        P("dp", None),
        P("section", None, "dp", None, None),
        P("dp"),
        P("dp"),
        P("section", "dp", None),
        P("section", None),
    )
    out_specs = (P("section", "dp", None), P("section", "dp", None))
    return jax.shard_map(body, mesh=mesh, in_specs=in_specs, out_specs=out_specs, check_vma=False)
```

```python
import functools

import jax
import jax.numpy as jnp
from jax import lax
from jax.experimental import pallas as pl
from jax.experimental.pallas import tpu as pltpu
from jax.sharding import PartitionSpec as P

D = 2048
QTR = 32
N_MICRO = 4
ROWS = 128
N_SEC = 8
N_Z = 8
LAST = 10
TICKS = LAST + N_MICRO
EPS = 1e-6
BF = jnp.bfloat16
F32 = jnp.float32
BOTH = ("section", "dp")


def device(y, a, xh, z, c):
    return (2 * y + a) * 32 + 16 * xh + 2 * z + c


def pairs_of(target):
    out = []
    for y in range(4):
        for a in range(2):
            for xh in range(2):
                for z in range(N_Z):
                    for c in range(2):
                        to = target(y, a, xh, z, c)
                        if to is not None:
                            out.append((device(y, a, xh, z, c), device(*to)))
    return out


TURN = pairs_of(lambda y, a, xh, z, c: (y, c, xh, z, a))
CORES = pairs_of(lambda y, a, xh, z, c: (y, a, xh, z, 1 - c))
RIGHT = pairs_of(lambda y, a, xh, z, c: (y, a, xh, (z + 1) % N_Z, c))
LEFT = pairs_of(lambda y, a, xh, z, c: (y, a, xh, (z - 1) % N_Z, c))
UP_CORE = pairs_of(lambda y, a, xh, z, c: (y, a, xh, z, 1) if c == 0 else None)
UP_CHIP = pairs_of(lambda y, a, xh, z, c: (y + 1, a, xh, z, 0) if c == 1 and y < 3 else None)
DOWN_CORE = pairs_of(lambda y, a, xh, z, c: (y, a, xh, z, 0) if c == 1 else None)
DOWN_CHIP = pairs_of(lambda y, a, xh, z, c: (y - 1, a, xh, z, 1) if c == 0 and y > 0 else None)
FAR_X = pairs_of(lambda y, a, xh, z, c: (y, a, 1 - xh, z, c))
FAR_X_CORE = pairs_of(lambda y, a, xh, z, c: (y, a, 1 - xh, z, 1 - c))
TO_PLACE = [pairs_of(lambda y, a, xh, z, c: (y, c, xh, z, a ^ j)) for j in range(2)]


def beside(y, a, xh, z, step, core):
    x = (2 * xh + a + step) % 4
    return (y, x % 2, x // 2, z, core)


TO_NEXT = pairs_of(
    lambda y, a, xh, z, c: beside(y, a, xh, z, 1, a) if c == 0 else (y, a, xh, z, 0) if a == 0 else None
)
TO_PREVIOUS = pairs_of(
    lambda y, a, xh, z, c: beside(y, a, xh, z, -1, a) if c == 1 else (y, a, xh, z, 1) if a == 1 else None
)

CHUNK = 256
HALF = 1024
QUARTER = 512


def send(array, pairs):
    return lax.ppermute(array, BOTH, pairs)


ANY = pl.BlockSpec(memory_space=pl.ANY)
WHOLE = pl.BlockSpec((ROWS, D), lambda i, tab: (0, 0))
COST = pl.CostEstimate(flops=2**20, bytes_accessed=2**18, transcendentals=0)
PARAMS = pltpu.CompilerParams(vmem_limit_bytes=12 * 2**20)


def feature_columns(z, k, xh):
    return pl.ds(pl.multiple_of((xh * N_Z + lax.rem(z + k, N_Z)) * 128, 128), 128)


def whole(shape):
    return pl.BlockSpec(shape, lambda i, place: (0,) * len(shape))


def placed(kernel, name, place, arrays, outs):
    return pl.pallas_call(
        kernel,
        grid_spec=pltpu.PrefetchScalarGridSpec(
            num_scalar_prefetch=1,
            grid=(1,),
            in_specs=[whole(r.shape) for r in arrays],
            out_specs=[whole(shape) for shape, _ in outs],
        ),
        out_shape=[jax.ShapeDtypeStruct(shape, dtype) for shape, dtype in outs],
        compiler_params=PARAMS,
        name=name,
    )(place, *arrays)


def half_columns(index):
    return pl.ds(pl.multiple_of(index * HALF, HALF), HALF)


def part_rows(index, rows):
    return pl.ds(pl.multiple_of(index * rows, rows), rows)


def divide_kernel(place, shard, mine, other):
    mine[...] = shard[:, half_columns(place[2])]
    other[...] = shard[:, half_columns(1 - place[2])]


def arrange_kernel(place, p00, p01, p10, p11, out):
    for dx, dt, part in ((0, 0, p00), (0, 1, p01), (1, 0, p10), (1, 1, p11)):
        out[part_rows((place[0] ^ dx) * 2 + (place[2] ^ dt), 64), :] = part[...]


def pack(pieces, wait_for):
    rows = sum(piece.shape[0] for piece in pieces)

    def kernel(*refs):
        out, at = refs[len(pieces) + len(wait_for)], 0
        for piece in refs[: len(pieces)]:
            out[at : at + piece.shape[0], :] = piece[...]
            at += piece.shape[0]

    return pl.pallas_call(
        kernel,
        grid=(1,),
        in_specs=[pl.BlockSpec(p.shape, lambda i: (0, 0)) for p in pieces] + [ANY] * len(wait_for),
        out_specs=[pl.BlockSpec((rows, HALF), lambda i: (0, 0))] + [ANY] * len(pieces),
        out_shape=[jax.ShapeDtypeStruct((rows, HALF), BF)]
        + [jax.ShapeDtypeStruct(p.shape, BF) for p in pieces],
        input_output_aliases={i: 1 + i for i in range(len(pieces))},
        compiler_params=PARAMS,
        name="pack",
    )(*pieces, *wait_for)


def place_chunk(place, k, full, own, following, previous, at, wait_for):
    count = len(own)
    skip = 0 if full is None else 1

    def kernel(place, *refs):
        pieces, arrived, out = refs[:count], refs[count : count + 2], refs[count + 2 + skip + len(wait_for)]
        same = place[1] == place[2]
        for c in range(2):

            @pl.when(same & (place[2] == c))
            def _():
                row = 0
                for piece in pieces:
                    out[row : row + piece.shape[0], c * HALF : (c + 1) * HALF] = piece[...]
                    row += piece.shape[0]
                out[:, (1 - c) * HALF : (2 - c) * HALF] = arrived[c][...]

        @pl.when(jnp.logical_not(same))
        def _():
            for c in range(2):
                out[:, c * HALF : (c + 1) * HALF] = arrived[c][...]

    block = pl.BlockSpec((CHUNK, HALF), lambda i, place: (at, 0))
    old = [] if full is None else [full]
    return pl.pallas_call(
        kernel,
        grid_spec=pltpu.PrefetchScalarGridSpec(
            num_scalar_prefetch=1,
            grid=(1,),
            in_specs=[whole(p.shape) for p in own] + [block] * 2 + [ANY] * (skip + len(wait_for)),
            out_specs=pl.BlockSpec((CHUNK, D), lambda i, place: (k, 0)),
        ),
        out_shape=jax.ShapeDtypeStruct((D, D), BF),
        input_output_aliases={} if full is None else {count + 3: 0},
        compiler_params=PARAMS,
        name=f"place_{k}",
    )(place, *own, following, previous, *old, *wait_for)


def gather_weight(place, shard, early, ready):
    quarter, chunk = ((64, HALF), BF), ((CHUNK, HALF), BF)
    mine, other = placed(divide_kernel, "divide", place, [shard], [quarter, quarter])
    parts = [mine, send(other, CORES), send(mine, FAR_X), send(other, FAR_X_CORE)]
    first = placed(arrange_kernel, "arrange", place, parts, [chunk])[0]
    right, left, rows = first, first, first
    order = [(0, 0)]
    own = {0: [first]}
    full, before = None, early
    for step in range(1, 6):
        if step < 4:
            right, left = send(right, RIGHT), send(left, LEFT)
        elif step == 4:
            right, left = send(right[:128], RIGHT), send(left[128:], LEFT)
        moved = [send(rows, TO_NEXT), send(rows, TO_PREVIOUS)]
        if step < 5:
            rows, right, left = pack([right, left], before)
        before = moved
        for k, at in order:
            full = place_chunk(place, k, full, own[k], *moved, at, ready if k == 4 else [])
        order = [(-step % N_Z, 0), (step, 1)] if step < 4 else [(4, 0)]
        if step < 4:
            own[-step % N_Z], own[step] = [right], [left]
        else:
            own[4] = [right, left]
    return full


def sample_of(group):
    early = group < 8
    return jnp.where(early, group // 2, group - 4), jnp.where(early, lax.rem(group, 2), 0)


def held_block(side):
    def index(group, ids, *rest):
        sample, half = sample_of(group)
        return (side * 12 + ids[sample], half, 0, 0)

    return pl.BlockSpec((1, 1, QTR, D), index)


def held_rows(ids, stored):
    def kernel(ids, held_ref, out_ref):
        out_ref[...] = held_ref[0, 0]

    return pl.pallas_call(
        kernel,
        grid_spec=pltpu.PrefetchScalarGridSpec(
            num_scalar_prefetch=1,
            grid=(16,),
            in_specs=[held_block(0)],
            out_specs=pl.BlockSpec((QTR, D), lambda g, ids: (g, 0)),
        ),
        out_shape=jax.ShapeDtypeStruct((N_MICRO * ROWS, D), BF),
        compiler_params=PARAMS,
        name="held_rows",
    )(ids, stored)


def boundary_rows(ids, limits, kept, stored):
    def held_at(quarter):
        def index(micro, ids, limits):
            sample, half = sample_of(micro * 4 + quarter)
            return (12 + ids[sample], half, 0, 0)

        return pl.BlockSpec((1, 1, QTR, D), index)

    def kernel(ids, limits, kept_ref, h0, h1, h2, h3, out_ref):
        for quarter, held_ref in enumerate((h0, h1, h2, h3)):
            sample, half = sample_of(pl.program_id(0) * 4 + quarter)
            row = lax.broadcasted_iota(jnp.int32, (QTR, 1), 0) + half * QTR
            live = (row < limits[sample]) | (limits[12] == 1)
            rows = slice(quarter * QTR, (quarter + 1) * QTR)
            value = jnp.where(live, kept_ref[0, rows, :].astype(F32), held_ref[0, 0].astype(F32))
            out_ref[0, rows, :] = value.astype(BF)

    return pl.pallas_call(
        kernel,
        grid_spec=pltpu.PrefetchScalarGridSpec(
            num_scalar_prefetch=2,
            grid=(N_MICRO,),
            in_specs=[pl.BlockSpec((1, ROWS, D), lambda m, *tables: (m, 0, 0))]
            + [held_at(quarter) for quarter in range(4)],
            out_specs=pl.BlockSpec((1, ROWS, D), lambda m, *tables: (0, m, 0)),
        ),
        out_shape=jax.ShapeDtypeStruct((1, N_MICRO * ROWS, D), BF),
        compiler_params=PARAMS,
        name="boundary_rows",
    )(ids, limits, kept, stored, stored, stored, stored)


def product_kernel(has, *refs):
    rows = N_MICRO * ROWS
    total = jnp.zeros((CHUNK, QUARTER), F32)
    for j in range(2):
        slope = jnp.concatenate([ref[...] for ref in refs[2 + 4 * j : 6 + 4 * j]], axis=0)
        total = total + lax.dot_general(
            refs[j][...].reshape(rows, CHUNK),
            slope,
            (((0,), (0,)), ((), ())),
            preferred_element_type=F32,
        )
    for ref in refs[10 : 10 + has]:
        total = total + ref[...].astype(F32)
    refs[-1][...] = total.astype(BF)


def product(sums, k, part, arrived, wait_for=()):
    piece = pl.BlockSpec((CHUNK, QUARTER), lambda i: (0, 0))
    return pl.pallas_call(
        functools.partial(product_kernel, len(arrived)),
        grid=(1,),
        in_specs=[pl.BlockSpec((N_MICRO, ROWS, CHUNK), lambda i: (0, 0, k))] * 2
        + [pl.BlockSpec((ROWS, QUARTER), lambda i: (0, part))] * 8
        + [piece] * len(arrived)
        + [ANY] * len(wait_for),
        out_specs=piece,
        out_shape=jax.ShapeDtypeStruct((CHUNK, QUARTER), BF),
        compiler_params=PARAMS,
        cost_estimate=COST,
        name=f"product_{k}_{part}",
    )(*sums, *arrived, *wait_for)


def split_x_kernel(place, q0, q1, mine, other):
    for out, xh in ((mine, place[0]), (other, 1 - place[0])):
        rows = part_rows(xh, 128)
        out[:, :QUARTER] = q0[rows, :]
        out[:, QUARTER:] = q1[rows, :]


def split_core_kernel(place, mine, arrived, own, other, total):
    total[...] = mine[...].astype(F32) + arrived[...].astype(F32)
    own[...] = total[part_rows(place[2], 64), :]
    other[...] = total[part_rows(1 - place[2], 64), :].astype(BF)


def scatter_grad(place, sums, core, wait_for):
    to_right = [send(product(sums, 4, 0, []), RIGHT), None]
    to_left = [None, send(product(sums, 4, 1, []), LEFT)]
    for step in range(3, 0, -1):
        for part in (1, 0):
            held = to_right[part]
            to_right[part] = send(product(sums, step, part, [] if held is None else [held]), RIGHT)
            held = to_left[1 - part]
            to_left[1 - part] = send(
                product(sums, N_Z - step, 1 - part, [] if held is None else [held]), LEFT
            )
    quarters = [
        product(sums, 0, part, [to_right[part], to_left[part]], [wait_for]) for part in range(2)
    ]
    block = ((128, HALF), BF)
    mine, other = placed(split_x_kernel, "split_x", place, quarters, [block, block])
    arrived = send(other, FAR_X)
    own, other, _ = placed(
        split_core_kernel, "split_core", place, [mine, arrived],
        [((64, HALF), F32), ((64, HALF), BF), ((128, HALF), F32)],
    )
    arrived = send(other, CORES).astype(F32)
    return jnp.where(
        core == 0,
        jnp.concatenate([own, arrived], axis=1),
        jnp.concatenate([arrived, own], axis=1),
    )


def live_mask(tab, micro):
    row = lax.broadcasted_iota(jnp.int32, (ROWS, 1), 0)
    if micro < 2:
        limit = jnp.where(row < 64, tab[4 + 2 * micro], tab[5 + 2 * micro])
        return row % 64 < limit
    limit = jnp.zeros((ROWS, 1), jnp.int32)
    for q in range(4):
        limit = jnp.where(row // QTR == q, tab[4 * micro + q], limit)
    return row % QTR < limit


def slot_block(micro):
    return jnp.where((micro >= 0) & (micro < N_MICRO), micro, N_MICRO)


def forward_kernel(tick, names, tab, *refs):
    ref = dict(zip(names, refs))
    micro = tick - tab[1]
    block = tab[0]
    active = (micro >= 0) & (micro < N_MICRO)
    x_ref, normed_ref, plain_ref = ref["x"], ref["normed"], refs[-1]

    if "first" in ref:

        @pl.when(active & (block == 0) & (tab[3] == 0))
        def _():
            x_ref[0] = ref["first"][...]

        @pl.when(active & (block == 0) & (tab[3] == 1))
        def _():
            x_ref[0] = ref["first_other"][...]

    if "core" in ref:

        @pl.when(active & (block % 2 == 1))
        def _():
            x_ref[0] = ref["core"][...]

    if "chip" in ref:

        @pl.when(active & (block % 2 == 0) & (block > 0))
        def _():
            x_ref[0] = ref["chip"][...]

    if "held" in ref:

        @pl.when(block == N_SEC - 1)
        def _():
            live = live_mask(tab, tick - LAST)
            x = jnp.where(live, x_ref[0].astype(F32), ref["held"][...].astype(F32))
            x_ref[0] = x.astype(BF)

    @pl.when(active)
    def _():
        values = x_ref[0].astype(F32)
        inverse = lax.rsqrt(jnp.mean(values * values, axis=1, keepdims=True) + EPS)
        plain_ref[...] = (values * inverse * ref["gain"][...].astype(F32)).astype(BF)
        for k in range(N_Z):
            for xh in range(2):
                to = k * CHUNK + xh * 128
                normed_ref[0, :, to : to + 128] = plain_ref[:, feature_columns(tab[2], k, xh)]
        for at in range(0, D, QUARTER):
            cols = slice(at, at + QUARTER)
            mixed = jnp.dot(normed_ref[0], ref["weight"][:, cols], preferred_element_type=F32)
            ref["mixed"][0, :, cols] = mixed
            output = (x_ref[0, :, cols].astype(F32) + mixed / (1.0 + jnp.exp(-mixed))).astype(BF)
            ref["msg"][:, cols] = output
            ref["kept"][0, :, cols] = output


STASH = {"x": BF, "mixed": F32, "kept": BF, "normed": BF}


def forward_tick(tick, tab, blocks, weight, gain, stash, wait_for):
    slot = pl.BlockSpec((1, ROWS, D), lambda i, tab: (slot_block(tick - tab[1]), 0, 0))
    names = [*blocks, "weight", "gain"]
    arrays = [array for array, _ in blocks.values()] + [weight, gain]
    specs = [pl.BlockSpec((ROWS, D), lambda i, tab, at=at: (at, 0)) for _, at in blocks.values()]
    specs += [whole((D, D)), whole((1, D))]
    old = [] if stash is None else list(stash)
    aliases = {1 + len(arrays) + i: 1 + i for i in range(len(old))}
    names += [None] * (len(old) + len(wait_for)) + ["msg", *STASH]
    return pl.pallas_call(
        functools.partial(forward_kernel, tick, names),
        grid_spec=pltpu.PrefetchScalarGridSpec(
            num_scalar_prefetch=1,
            grid=(1,),
            in_specs=specs + [ANY] * (len(old) + len(wait_for)),
            out_specs=[WHOLE] + [slot] * 4,
            scratch_shapes=[pltpu.VMEM((ROWS, D), BF)],
        ),
        out_shape=[jax.ShapeDtypeStruct((ROWS, D), BF)]
        + [jax.ShapeDtypeStruct((N_MICRO + 1, ROWS, D), kind) for kind in STASH.values()],
        input_output_aliases=aliases,
        compiler_params=PARAMS,
        cost_estimate=COST,
        name=f"forward_{tick}",
    )(tab, *arrays, *old, *wait_for)


def backward_kernel(tick, names, tab, *refs):
    ref = dict(zip(names, refs))
    up_ref, slope_ref, weighted_ref = refs[-3:]
    x_ref, msg_ref = ref["x"], ref["msg"]
    micro = tick - (LAST - tab[1])
    slot = jnp.clip(micro, 0, N_MICRO - 1)
    block = tab[0]
    active = (micro >= 0) & (micro < N_MICRO)

    if "given" in ref:
        for a, name in ((1, "given"), (0, "given_other")):

            @pl.when(active & (block == N_SEC - 1) & (tab[3] == a))
            def _():
                given = ref[name][...].astype(F32)
                up_ref[...] = jnp.where(live_mask(tab, tick), given, 0.0).astype(BF)

    if "core" in ref:

        @pl.when(active & (block % 2 == 0))
        def _():
            up_ref[...] = ref["core"][...]

    if "chip" in ref:

        @pl.when(active & (block % 2 == 1) & (block < N_SEC - 1))
        def _():
            up_ref[...] = ref["chip"][...]

    @pl.when(active)
    def _():
        mixed = ref["mixed"][slot]
        gated = 1.0 / (1.0 + jnp.exp(-mixed))
        up = up_ref[...].astype(F32)
        slope_ref[...] = (up * gated * (1.0 + mixed * (1.0 - gated))).astype(BF)
        for j, name in enumerate(("slope_0", "slope_1")):
            ref[name][0] = slope_ref[:, half_columns(tab[3] ^ j)]

    if tick >= LAST:
        for source, condition in (("slope", block == 0), ("old", block != 0)):

            @pl.when(condition)
            def _():
                for j in "01":
                    ref["leave_" + j][...] = ref[source + "_" + j][0]

    @pl.when(active & (block > 0))
    def _():
        values = x_ref[slot].astype(F32)
        inverse = lax.rsqrt(jnp.mean(values * values, axis=1, keepdims=True) + EPS)
        total = jnp.zeros((ROWS, 128), F32)
        for k in range(N_Z):
            back = lax.dot_general(
                slope_ref[...],
                ref["weight"][k * CHUNK : (k + 1) * CHUNK, :],
                (((1,), (1,)), ((), ())),
                preferred_element_type=F32,
            )
            for xh in range(2):
                cols = feature_columns(tab[2], k, xh)
                part = back[:, xh * 128 : xh * 128 + 128] * ref["gain"][:, cols].astype(F32)
                total = total + part * x_ref[slot, :, cols].astype(F32)
                weighted_ref[:, cols] = part
        centre = jnp.sum(total, axis=1, keepdims=True) * (1.0 / D)
        factor = inverse * inverse * inverse * centre
        grad = up_ref[...].astype(F32) + inverse * weighted_ref[...]
        msg_ref[...] = (grad - x_ref[slot].astype(F32) * factor).astype(BF)


def backward_tick(tick, tab, blocks, weight, gain, stash, slopes, wait_for):
    def micro_of(tab):
        return tick - (LAST - tab[1])

    read = whole((N_MICRO + 1, ROWS, D))
    slot = pl.BlockSpec((1, ROWS, HALF), lambda i, tab: (slot_block(micro_of(tab)), 0, 0))
    late = tick >= LAST
    names = [*blocks, "weight", "gain", "x", "mixed"]
    arrays = [array for array, _ in blocks.values()] + [weight, gain, *stash]
    specs = [pl.BlockSpec((ROWS, D), lambda i, tab, at=at: (at, 0)) for _, at in blocks.values()]
    specs += [whole((D, D)), whole((1, D)), read, read]
    aliases = {len(arrays) - 1: 1, len(arrays): 2}
    if slopes is not None:
        aliases |= {len(arrays) + 1: 3, len(arrays) + 2: 4}
        arrays += slopes
        names += ["old_0", "old_1"]
        specs += [
            pl.BlockSpec((1, ROWS, HALF), lambda i, tab: (tick - LAST, 0, 0)) if late else ANY
        ] * 2
    names += [None] * len(wait_for) + ["msg", None, None, "slope_0", "slope_1"]
    names += ["leave_0", "leave_1"] if late else []
    half = jax.ShapeDtypeStruct((ROWS, HALF), BF)
    kept = jax.ShapeDtypeStruct((N_MICRO + 1, ROWS, HALF), BF)
    out = pl.pallas_call(
        functools.partial(backward_kernel, tick, names),
        grid_spec=pltpu.PrefetchScalarGridSpec(
            num_scalar_prefetch=1,
            grid=(1,),
            in_specs=specs + [ANY] * len(wait_for),
            out_specs=[WHOLE, ANY, ANY, slot, slot] + [whole((ROWS, HALF))] * (2 * late),
            scratch_shapes=[pltpu.VMEM((ROWS, D), BF)] * 2 + [pltpu.VMEM((ROWS, D), F32)],
        ),
        out_shape=[jax.ShapeDtypeStruct((ROWS, D), BF)]
        + [jax.ShapeDtypeStruct(s.shape, s.dtype) for s in stash]
        + [kept, kept]
        + [half] * (2 * late),
        input_output_aliases=aliases,
        compiler_params=PARAMS,
        cost_estimate=COST,
        name=f"backward_{tick}",
    )(tab, *arrays, *wait_for)
    return out[0], out[1:3], out[3:5], out[5:]


def hand_on(array, wait_for):
    def kernel(*refs):
        pass

    return pl.pallas_call(
        kernel,
        in_specs=[ANY, ANY],
        out_specs=ANY,
        out_shape=jax.ShapeDtypeStruct(array.shape, array.dtype),
        input_output_aliases={0: 0},
        compiler_params=PARAMS,
        name="hand_on",
    )(array, wait_for)


def body(embedded, out_grad, stored, sample_ids, lengths, weight, gain):
    section = lax.axis_index("section")
    data = lax.axis_index("dp")
    y, a = section // 2, section % 2
    xh, c = data // 16, data % 2
    z = (data // 2) % N_Z
    place = jnp.stack([xh, a, c])
    table = jnp.stack([2 * y + c, 3 * y + c, z, a])
    stored = stored.reshape(24, 2, QTR, D)

    embedded_other = send(embedded, CORES)
    gain_row = send(gain, TURN)

    limits = jnp.where(a == c, lengths, send(lengths, CORES))
    late_table = jnp.concatenate([table, limits])
    held = held_rows(sample_ids, stored)
    full = gather_weight(place, weight[0], [held], [late_table, embedded_other, gain_row])
    held = send(held, TURN)
    grad_other = send(out_grad, CORES)

    stash = slopes = None
    kept, normed, leaving = None, [], [[], []]
    up_core, up_chip, down_core, down_chip = {}, {}, {}, {}
    for tick in range(LAST + TICKS):
        if tick < TICKS:
            blocks = {}
            if tick < N_MICRO:
                blocks["first"] = (embedded, tick)
                blocks["first_other"] = (embedded_other, tick)
            if tick in up_core:
                blocks["core"] = (up_core[tick], 0)
            if tick in up_chip:
                blocks["chip"] = (up_chip[tick], 0)
            if tick >= LAST:
                blocks["held"] = (held, tick - LAST)
            msg, *stash = forward_tick(
                tick,
                late_table if tick >= LAST else table,
                blocks,
                full,
                gain_row,
                stash,
                [held] if tick == LAST - 1 else [],
            )
            if tick < TICKS - 1:
                up_core[tick + 1] = send(msg, UP_CORE)
            if 1 <= tick <= LAST:
                up_chip[tick + 2] = send(msg, UP_CHIP)
            if tick == TICKS - 1:
                normed.append(send(stash[3], TURN))
                kept = stash[2]
        if tick >= LAST:
            step = tick - LAST
            blocks = {}
            if step < N_MICRO:
                blocks["given"] = (out_grad, step)
                blocks["given_other"] = (grad_other, step)
            if step in down_core:
                blocks["core"] = (down_core[step], 0)
            if step in down_chip:
                blocks["chip"] = (down_chip[step], 0)
            msg, stash[:2], slopes, halves = backward_tick(
                step,
                late_table if step < N_MICRO else table,
                blocks,
                full,
                gain_row,
                stash[:2],
                slopes,
                [],
            )
            if step < TICKS - 1:
                down_core[step + 1] = send(msg, DOWN_CORE)
            if 1 <= step <= LAST:
                down_chip[step + 2] = send(msg, DOWN_CHIP)
            if step == 6:
                kept = send(hand_on(kept, msg), TURN)
            if step == 9:
                normed[0] = hand_on(normed[0], msg)
                normed.append(send(normed[0], CORES))
            for j, half in enumerate(halves):
                leaving[j].append(send(half, TO_PLACE[j]))

    last = (section == N_SEC - 1).astype(jnp.int32)
    boundary = boundary_rows(sample_ids, jnp.concatenate([lengths, last[None]]), kept, stored)
    shard = scatter_grad(place, (*normed, *leaving[0], *leaving[1]), c, boundary)
    return (boundary, shard[None])


def solution(mesh):
    in_specs = (
        P("dp", None),
        P("dp", None),
        P("section", None, "dp", None, None),
        P("dp"),
        P("dp"),
        P("section", "dp", None),
        P("section", None),
    )
    out_specs = (P("section", "dp", None), P("section", "dp", None))
    return jax.shard_map(body, mesh=mesh, in_specs=in_specs, out_specs=out_specs, check_vma=False)
```

```python
import functools

import jax
import jax.numpy as jnp
from jax import lax
from jax.experimental import pallas as pl
from jax.experimental.pallas import tpu as pltpu
from jax.sharding import PartitionSpec as P

D = 2048
QTR = 32
N_MICRO = 4
ROWS = 128
N_SEC = 8
N_Z = 8
LAST = 10
TICKS = LAST + N_MICRO
EPS = 1e-6
BF = jnp.bfloat16
F32 = jnp.float32
BOTH = ("section", "dp")


def device(y, a, xh, z, c):
    return (2 * y + a) * 32 + 16 * xh + 2 * z + c


def pairs_of(target):
    out = []
    for y in range(4):
        for a in range(2):
            for xh in range(2):
                for z in range(N_Z):
                    for c in range(2):
                        to = target(y, a, xh, z, c)
                        if to is not None:
                            out.append((device(y, a, xh, z, c), device(*to)))
    return out


TURN = pairs_of(lambda y, a, xh, z, c: (y, c, xh, z, a) if a != c else None)
CORES = pairs_of(lambda y, a, xh, z, c: (y, a, xh, z, 1 - c))
RIGHT = pairs_of(lambda y, a, xh, z, c: (y, a, xh, (z + 1) % N_Z, c))
LEFT = pairs_of(lambda y, a, xh, z, c: (y, a, xh, (z - 1) % N_Z, c))
UP_CORE = pairs_of(lambda y, a, xh, z, c: (y, a, xh, z, 1) if c == 0 else None)
UP_CHIP = pairs_of(lambda y, a, xh, z, c: (y + 1, a, xh, z, 0) if c == 1 and y < 3 else None)
DOWN_CORE = pairs_of(lambda y, a, xh, z, c: (y, a, xh, z, 0) if c == 1 else None)
DOWN_CHIP = pairs_of(lambda y, a, xh, z, c: (y - 1, a, xh, z, 1) if c == 0 and y > 0 else None)
FAR_X = pairs_of(lambda y, a, xh, z, c: (y, a, 1 - xh, z, c))
FAR_X_CORE = pairs_of(lambda y, a, xh, z, c: (y, a, 1 - xh, z, 1 - c))


def beside(y, a, xh, z, step, core):
    x = (2 * xh + a + step) % 4
    return (y, x % 2, x // 2, z, core)


TO_NEXT = pairs_of(
    lambda y, a, xh, z, c: beside(y, a, xh, z, 1, a) if c == 0 else (y, a, xh, z, 0) if a == 0 else None
)
TO_PREVIOUS = pairs_of(
    lambda y, a, xh, z, c: beside(y, a, xh, z, -1, a) if c == 1 else (y, a, xh, z, 1) if a == 1 else None
)

FIRST = pairs_of(
    lambda y, a, xh, z, c: (y, a, xh, z, 1 - a)
    if c == a
    else beside(y, a, xh, z, -1, 0)
    if a == 1
    else beside(y, a, xh, z, 1, 1)
)
SECOND = pairs_of(
    lambda y, a, xh, z, c: None
    if c == a
    else beside(y, a, xh, z, 1, 1)
    if a == 1
    else beside(y, a, xh, z, -1, 0)
)

CHUNK = 256
HALF = 1024
QUARTER = 512


def send(array, pairs):
    return lax.ppermute(array, BOTH, pairs)


ANY = pl.BlockSpec(memory_space=pl.ANY)
WHOLE = pl.BlockSpec((ROWS, D), lambda i, tab: (0, 0))
COST = pl.CostEstimate(flops=2**20, bytes_accessed=2**18, transcendentals=0)
PARAMS = pltpu.CompilerParams(vmem_limit_bytes=12 * 2**20)


def whole(shape):
    return pl.BlockSpec(shape, lambda i, place: (0,) * len(shape))


def placed(kernel, name, place, arrays, outs):
    return pl.pallas_call(
        kernel,
        grid_spec=pltpu.PrefetchScalarGridSpec(
            num_scalar_prefetch=1,
            grid=(1,),
            in_specs=[whole(r.shape) for r in arrays],
            out_specs=[whole(shape) for shape, _ in outs],
        ),
        out_shape=[jax.ShapeDtypeStruct(shape, dtype) for shape, dtype in outs],
        compiler_params=PARAMS,
        name=name,
    )(place, *arrays)


def half_columns(index):
    return pl.ds(pl.multiple_of(index * HALF, HALF), HALF)


def part_rows(index, rows):
    return pl.ds(pl.multiple_of(index * rows, rows), rows)


def divide_kernel(place, shard, mine, other):
    mine[...] = shard[:, half_columns(place[2])]
    other[...] = shard[:, half_columns(1 - place[2])]


def arrange_kernel(place, p00, p01, p10, p11, out):
    for dx, dt, part in ((0, 0, p00), (0, 1, p01), (1, 0, p10), (1, 1, p11)):
        out[part_rows((place[0] ^ dx) * 2 + (place[2] ^ dt), 64), :] = part[...]


def pack(pieces, wait_for):
    rows = sum(piece.shape[0] for piece in pieces)

    def kernel(*refs):
        out, at = refs[len(pieces) + len(wait_for)], 0
        for piece in refs[: len(pieces)]:
            out[at : at + piece.shape[0], :] = piece[...]
            at += piece.shape[0]

    return pl.pallas_call(
        kernel,
        grid=(1,),
        in_specs=[pl.BlockSpec(p.shape, lambda i: (0, 0)) for p in pieces] + [ANY] * len(wait_for),
        out_specs=[pl.BlockSpec((rows, HALF), lambda i: (0, 0))] + [ANY] * len(pieces),
        out_shape=[jax.ShapeDtypeStruct((rows, HALF), BF)]
        + [jax.ShapeDtypeStruct(p.shape, BF) for p in pieces],
        input_output_aliases={i: 1 + i for i in range(len(pieces))},
        compiler_params=PARAMS,
        name="pack",
    )(*pieces, *wait_for)


def place_chunk(place, k, full, own, following, previous, at, wait_for):
    count = len(own)
    skip = 0 if full is None else 1

    def kernel(place, *refs):
        pieces, arrived, out = refs[:count], refs[count : count + 2], refs[count + 2 + skip + len(wait_for)]
        same = place[1] == place[2]
        for c in range(2):

            @pl.when(same & (place[2] == c))
            def _():
                row = 0
                for piece in pieces:
                    for at in range(0, piece.shape[0], 128):
                        out[(row + at) // 128, :, c * HALF : (c + 1) * HALF] = piece[at : at + 128, :]
                    row += piece.shape[0]
                for xh in range(2):
                    rows = slice(xh * 128, xh * 128 + 128)
                    out[xh, :, (1 - c) * HALF : (2 - c) * HALF] = arrived[c][rows, :]

        @pl.when(jnp.logical_not(same))
        def _():
            for c in range(2):
                for xh in range(2):
                    rows = slice(xh * 128, xh * 128 + 128)
                    out[xh, :, c * HALF : (c + 1) * HALF] = arrived[c][rows, :]

    block = pl.BlockSpec((CHUNK, HALF), lambda i, place: (at, 0))
    old = [] if full is None else [full]
    return pl.pallas_call(
        kernel,
        grid_spec=pltpu.PrefetchScalarGridSpec(
            num_scalar_prefetch=1,
            grid=(1,),
            in_specs=[whole(p.shape) for p in own] + [block] * 2 + [ANY] * (skip + len(wait_for)),
            out_specs=pl.BlockSpec(
                (2, 128, D), lambda i, place: (0, lax.rem(place[3] + k, N_Z), 0)
            ),
        ),
        out_shape=jax.ShapeDtypeStruct((2, HALF, D), BF),
        input_output_aliases={} if full is None else {count + 3: 0},
        compiler_params=PARAMS,
        name=f"place_{k}",
    )(place, *own, following, previous, *old, *wait_for)


def gather_weight(place, shard, early, ready):
    quarter, chunk = ((64, HALF), BF), ((CHUNK, HALF), BF)
    mine, other = placed(divide_kernel, "divide", place, [shard], [quarter, quarter])
    parts = [mine, send(other, CORES), send(mine, FAR_X), send(other, FAR_X_CORE)]
    first = placed(arrange_kernel, "arrange", place, parts, [chunk])[0]
    right, left, rows = first, first, first
    order = [(0, 0)]
    own = {0: [first]}
    full, before = None, early
    for step in range(1, 6):
        if step < 4:
            right, left = send(right, RIGHT), send(left, LEFT)
        elif step == 4:
            right, left = send(right[:128], RIGHT), send(left[128:], LEFT)
        moved = [send(rows, TO_NEXT), send(rows, TO_PREVIOUS)]
        if step < 5:
            rows, right, left = pack([right, left], before)
        before = moved
        for k, at in order:
            full = place_chunk(place, k, full, own[k], *moved, at, ready if k == 4 else [])
        order = [(-step % N_Z, 0), (step, 1)] if step < 4 else [(4, 0)]
        if step < 4:
            own[-step % N_Z], own[step] = [right], [left]
        else:
            own[4] = [right, left]
    return full.reshape(D, D)


def sample_of(group):
    early = group < 8
    return jnp.where(early, group // 2, group - 4), jnp.where(early, lax.rem(group, 2), 0)


def held_block(side):
    def index(group, ids, *rest):
        sample, half = sample_of(group)
        return (side * 12 + ids[sample], half, 0, 0)

    return pl.BlockSpec((1, 1, QTR, D), index)


def held_rows(ids, stored):
    def kernel(ids, held_ref, out_ref):
        out_ref[...] = held_ref[0, 0]

    return pl.pallas_call(
        kernel,
        grid_spec=pltpu.PrefetchScalarGridSpec(
            num_scalar_prefetch=1,
            grid=(16,),
            in_specs=[held_block(0)],
            out_specs=pl.BlockSpec((QTR, D), lambda g, ids: (g, 0)),
        ),
        out_shape=jax.ShapeDtypeStruct((N_MICRO * ROWS, D), BF),
        compiler_params=PARAMS,
        name="held_rows",
    )(ids, stored)


def boundary_rows(ids, limits, own, arrived, stored):
    def held_at(quarter):
        def index(micro, ids, limits):
            sample, half = sample_of(micro * 4 + quarter)
            return (12 + ids[sample], half, 0, 0)

        return pl.BlockSpec((1, 1, QTR, D), index)

    def kernel(ids, limits, own_ref, arrived_ref, h0, h1, h2, h3, out_ref):
        for quarter, held_ref in enumerate((h0, h1, h2, h3)):
            sample, half = sample_of(pl.program_id(0) * 4 + quarter)
            row = lax.broadcasted_iota(jnp.int32, (QTR, 1), 0) + half * QTR
            live = (row < limits[sample]) | (limits[12] == 1)
            rows = slice(quarter * QTR, (quarter + 1) * QTR)
            held = held_ref[0, 0].astype(F32)

            @pl.when(limits[13] == 1)
            def _():
                out_ref[0, rows, :] = jnp.where(live, own_ref[0, rows, :].astype(F32), held).astype(BF)

            @pl.when(limits[13] != 1)
            def _():
                kept = arrived_ref[0, rows, :].astype(F32)
                out_ref[0, rows, :] = jnp.where(live, kept, held).astype(BF)

    return pl.pallas_call(
        kernel,
        grid_spec=pltpu.PrefetchScalarGridSpec(
            num_scalar_prefetch=2,
            grid=(N_MICRO,),
            in_specs=[pl.BlockSpec((1, ROWS, D), lambda m, *tables: (m, 0, 0))] * 2
            + [held_at(quarter) for quarter in range(4)],
            out_specs=pl.BlockSpec((1, ROWS, D), lambda m, *tables: (0, m, 0)),
        ),
        out_shape=jax.ShapeDtypeStruct((1, N_MICRO * ROWS, D), BF),
        compiler_params=PARAMS,
        name="boundary_rows",
    )(ids, limits, own, arrived, stored, stored, stored, stored)


def product_kernel(has, place, *refs):
    rows = N_MICRO * ROWS
    out, total_ref = refs[-2:]

    def add(sources):
        total = jnp.zeros((CHUNK, QUARTER), F32)
        for source in sources:
            low, high, three, one = refs[4 * source : 4 * source + 4]
            normed = jnp.concatenate(
                [low[...].reshape(rows, 128), high[...].reshape(rows, 128)], axis=1
            )
            slope = jnp.concatenate([three[...].reshape(rows - ROWS, QUARTER), one[0]], axis=0)
            total = total + lax.dot_general(
                normed, slope, (((0,), (0,)), ((), ())), preferred_element_type=F32
            )
        total_ref[...] = total

    @pl.when(place[1] == place[2])
    def _():
        add((0, 1))

    @pl.when(place[1] != place[2])
    def _():
        add((1, 2))

    total = total_ref[...]
    for ref in refs[12 : 12 + has]:
        total = total + ref[...].astype(F32)
    out[...] = total.astype(BF)


def product(place, sums, k, part, arrived, wait_for=()):
    piece = pl.BlockSpec((CHUNK, QUARTER), lambda i, place: (0, 0))

    def columns(xh):
        return pl.BlockSpec(
            (N_MICRO, ROWS, 128), lambda i, place: (0, 0, xh * N_Z + lax.rem(place[3] + k, N_Z))
        )

    specs, arrays = [], []
    for normed, three, one in sums:
        specs += [columns(0), columns(1)]
        specs += [pl.BlockSpec((n, ROWS, QUARTER), lambda i, place: (0, 0, part)) for n in (3, 1)]
        arrays += [normed, normed, three, one]
    return pl.pallas_call(
        functools.partial(product_kernel, len(arrived)),
        grid_spec=pltpu.PrefetchScalarGridSpec(
            num_scalar_prefetch=1,
            grid=(1,),
            in_specs=specs + [piece] * len(arrived) + [ANY] * len(wait_for),
            out_specs=piece,
            scratch_shapes=[pltpu.VMEM((CHUNK, QUARTER), F32)],
        ),
        out_shape=jax.ShapeDtypeStruct((CHUNK, QUARTER), BF),
        compiler_params=PARAMS,
        cost_estimate=COST,
        name=f"product_{k}_{part}",
    )(place, *arrays, *arrived, *wait_for)


def split_x_kernel(place, q0, q1, mine, other):
    for out, xh in ((mine, place[0]), (other, 1 - place[0])):
        rows = part_rows(xh, 128)
        out[:, :QUARTER] = q0[rows, :]
        out[:, QUARTER:] = q1[rows, :]


def split_core_kernel(place, mine, arrived, own, other, total):
    total[...] = mine[...].astype(F32) + arrived[...].astype(F32)
    own[...] = total[part_rows(place[2], 64), :]
    other[...] = total[part_rows(1 - place[2], 64), :].astype(BF)


def scatter_grad(place, sums, core, wait_for):
    to_right = [send(product(place, sums, 4, 0, []), RIGHT), None]
    to_left = [None, send(product(place, sums, 4, 1, []), LEFT)]
    for step in range(3, 0, -1):
        for part in (1, 0):
            held = to_right[part]
            to_right[part] = send(
                product(place, sums, step, part, [] if held is None else [held]), RIGHT
            )
            held = to_left[1 - part]
            to_left[1 - part] = send(
                product(place, sums, N_Z - step, 1 - part, [] if held is None else [held]), LEFT
            )
    quarters = [
        product(place, sums, 0, part, [to_right[part], to_left[part]], [wait_for]) for part in range(2)
    ]
    block = ((128, HALF), BF)
    mine, other = placed(split_x_kernel, "split_x", place, quarters, [block, block])
    arrived = send(other, FAR_X)
    own, other, _ = placed(
        split_core_kernel, "split_core", place, [mine, arrived],
        [((64, HALF), F32), ((64, HALF), BF), ((128, HALF), F32)],
    )
    arrived = send(other, CORES).astype(F32)
    return jnp.where(
        core == 0,
        jnp.concatenate([own, arrived], axis=1),
        jnp.concatenate([arrived, own], axis=1),
    )


def live_mask(tab, micro):
    row = lax.broadcasted_iota(jnp.int32, (ROWS, 1), 0)
    if micro < 2:
        limit = jnp.where(row < 64, tab[4 + 2 * micro], tab[5 + 2 * micro])
        return row % 64 < limit
    limit = jnp.zeros((ROWS, 1), jnp.int32)
    for q in range(4):
        limit = jnp.where(row // QTR == q, tab[4 * micro + q], limit)
    return row % QTR < limit


def slot_block(micro):
    return jnp.where((micro >= 0) & (micro < N_MICRO), micro, N_MICRO)


def forward_kernel(tick, names, tab, *refs):
    ref = dict(zip(names, refs))
    micro = tick - tab[1]
    block = tab[0]
    active = (micro >= 0) & (micro < N_MICRO)
    x_ref, normed_ref = ref["x"], ref["normed"]

    if "first" in ref:

        @pl.when(active & (block == 0))
        def _():
            x_ref[0] = ref["first"][...]

    if "core" in ref:

        @pl.when(active & (block % 2 == 1))
        def _():
            x_ref[0] = ref["core"][...]

    if "chip" in ref:

        @pl.when(active & (block % 2 == 0) & (block > 0))
        def _():
            x_ref[0] = ref["chip"][...]

    if "held" in ref:

        for name, mine in (("held", True), ("held_other", False)):

            @pl.when((block == N_SEC - 1) & ((tab[2] == tab[3]) == mine))
            def _():
                live = live_mask(tab, tick - LAST)
                x = jnp.where(live, x_ref[0].astype(F32), ref[name][...].astype(F32))
                x_ref[0] = x.astype(BF)

    @pl.when(active)
    def _():
        values = x_ref[0].astype(F32)
        inverse = lax.rsqrt(jnp.mean(values * values, axis=1, keepdims=True) + EPS)
        normed_ref[0] = (values * inverse * ref["gain"][...].astype(F32)).astype(BF)
        for at in range(0, D, QUARTER):
            cols = slice(at, at + QUARTER)
            mixed = jnp.dot(normed_ref[0], ref["weight"][:, cols], preferred_element_type=F32)
            ref["mixed"][0, :, cols] = mixed
            output = (x_ref[0, :, cols].astype(F32) + mixed / (1.0 + jnp.exp(-mixed))).astype(BF)
            ref["msg"][:, cols] = output
            ref["kept"][0, :, cols] = output


STASH = {"x": BF, "mixed": F32, "kept": BF, "normed": BF}


def forward_tick(tick, tab, blocks, weight, gain, stash, wait_for):
    slot = pl.BlockSpec((1, ROWS, D), lambda i, tab: (slot_block(tick - tab[1]), 0, 0))
    names = [*blocks, "weight", "gain"]
    arrays = [array for array, _ in blocks.values()] + [weight, gain]
    specs = [pl.BlockSpec((ROWS, D), lambda i, tab, at=at: (at, 0)) for _, at in blocks.values()]
    specs += [whole((D, D)), whole((1, D))]
    old = [] if stash is None else list(stash)
    aliases = {1 + len(arrays) + i: 1 + i for i in range(len(old))}
    names += [None] * (len(old) + len(wait_for)) + ["msg", *STASH]
    return pl.pallas_call(
        functools.partial(forward_kernel, tick, names),
        grid_spec=pltpu.PrefetchScalarGridSpec(
            num_scalar_prefetch=1,
            grid=(1,),
            in_specs=specs + [ANY] * (len(old) + len(wait_for)),
            out_specs=[WHOLE] + [slot] * 4,
        ),
        out_shape=[jax.ShapeDtypeStruct((ROWS, D), BF)]
        + [jax.ShapeDtypeStruct((N_MICRO + 1, ROWS, D), kind) for kind in STASH.values()],
        input_output_aliases=aliases,
        compiler_params=PARAMS,
        cost_estimate=COST,
        name=f"forward_{tick}",
    )(tab, *arrays, *old, *wait_for)


def backward_kernel(tick, names, tab, *refs):
    ref = dict(zip(names, refs))
    up_ref, slope_ref, weighted_ref = refs[-3:]
    x_ref, msg_ref = ref["x"], ref["msg"]
    micro = tick - (LAST - tab[1])
    slot = jnp.clip(micro, 0, N_MICRO - 1)
    block = tab[0]
    active = (micro >= 0) & (micro < N_MICRO)

    if "given" in ref:
        @pl.when(active & (block == N_SEC - 1))
        def _():
            given = ref["given"][...].astype(F32)
            up_ref[...] = jnp.where(live_mask(tab, tick), given, 0.0).astype(BF)

    if "core" in ref:

        @pl.when(active & (block % 2 == 0))
        def _():
            up_ref[...] = ref["core"][...]

    if "chip" in ref:

        @pl.when(active & (block % 2 == 1) & (block < N_SEC - 1))
        def _():
            up_ref[...] = ref["chip"][...]

    @pl.when(active)
    def _():
        mixed = ref["mixed"][slot]
        gated = 1.0 / (1.0 + jnp.exp(-mixed))
        up = up_ref[...].astype(F32)
        slope_ref[...] = (up * gated * (1.0 + mixed * (1.0 - gated))).astype(BF)
        for j, name in enumerate(("slope_0", "slope_1")):
            ref[name][0] = slope_ref[:, half_columns(tab[3] ^ (1 - j))]

    if tick >= LAST + 2:
        for j in "01":
            leave, old = ref["leave_" + j], ref["old_" + j]
            for at in range(2 if tick == LAST + 2 else 0):
                leave[at] = old[at]
            end = leave.shape[0] - 1

            @pl.when(block == 0)
            def _():
                leave[end] = ref["slope_" + j][0]

            @pl.when(block != 0)
            def _():
                leave[end] = old[tick - LAST]

    @pl.when(active & (block > 0))
    def _():
        values = x_ref[slot].astype(F32)
        inverse = lax.rsqrt(jnp.mean(values * values, axis=1, keepdims=True) + EPS)
        total = jnp.zeros((ROWS, 128), F32)
        for at in range(0, D, QUARTER):
            cols = slice(at, at + QUARTER)
            back = lax.dot_general(
                slope_ref[...],
                ref["weight"][cols, :],
                (((1,), (1,)), ((), ())),
                preferred_element_type=F32,
            )
            weighted = back * ref["gain"][:, cols].astype(F32)
            weighted_ref[:, cols] = weighted
            terms = weighted * x_ref[slot, :, cols].astype(F32)
            for part in range(0, QUARTER, 128):
                total = total + terms[:, part : part + 128]
        centre = jnp.sum(total, axis=1, keepdims=True) * (1.0 / D)
        factor = inverse * inverse * inverse * centre
        grad = up_ref[...].astype(F32) + inverse * weighted_ref[...]
        msg_ref[...] = (grad - x_ref[slot].astype(F32) * factor).astype(BF)


def backward_tick(tick, tab, blocks, weight, gain, stash, slopes, wait_for):
    def micro_of(tab):
        return tick - (LAST - tab[1])

    read = whole((N_MICRO + 1, ROWS, D))
    slot = pl.BlockSpec((1, ROWS, HALF), lambda i, tab: (slot_block(micro_of(tab)), 0, 0))
    leaving = {LAST + 2: 3, LAST + 3: 1}.get(tick, 0)
    hold = tick < N_MICRO
    names = [*blocks, "weight", "gain", "x", "mixed"]
    arrays = [array for array, _ in blocks.values()] + [weight, gain, *stash]
    specs = [pl.BlockSpec((ROWS, D), lambda i, tab, at=at: (at, 0)) for _, at in blocks.values()]
    specs += [whole((D, D)), whole((1, D)), read, read]
    aliases = {len(arrays) - 1: 3, len(arrays): 4} if hold else {}
    if slopes is not None:
        aliases |= {len(arrays) + 1: 1, len(arrays) + 2: 2}
        arrays += slopes
        names += ["old_0", "old_1"]
        specs += [whole((N_MICRO + 1, ROWS, HALF)) if leaving else ANY] * 2
    names += [None] * len(wait_for) + ["msg", "slope_0", "slope_1"] + [None] * (2 * hold)
    names += ["leave_0", "leave_1"] if leaving else []
    leave = (leaving, ROWS, HALF)
    kept = jax.ShapeDtypeStruct((N_MICRO + 1, ROWS, HALF), BF)
    out = pl.pallas_call(
        functools.partial(backward_kernel, tick, names),
        grid_spec=pltpu.PrefetchScalarGridSpec(
            num_scalar_prefetch=1,
            grid=(1,),
            in_specs=specs + [ANY] * len(wait_for),
            out_specs=[WHOLE, slot, slot] + [ANY] * (2 * hold) + [whole(leave)] * (2 * (leaving > 0)),
            scratch_shapes=[pltpu.VMEM((ROWS, D), BF)] * 2 + [pltpu.VMEM((ROWS, D), F32)],
        ),
        out_shape=[jax.ShapeDtypeStruct((ROWS, D), BF), kept, kept]
        + [jax.ShapeDtypeStruct(s.shape, s.dtype) for s in stash if hold]
        + [jax.ShapeDtypeStruct(leave, BF)] * (2 * (leaving > 0)),
        input_output_aliases=aliases,
        compiler_params=PARAMS,
        cost_estimate=COST,
        name=f"backward_{tick}",
    )(tab, *arrays, *wait_for)
    return out[0], out[3:5] if hold else stash, out[1:3], out[3:] if leaving else []


def hand_on(array, wait_for):
    def kernel(*refs):
        pass

    return pl.pallas_call(
        kernel,
        in_specs=[ANY, ANY],
        out_specs=ANY,
        out_shape=jax.ShapeDtypeStruct(array.shape, array.dtype),
        input_output_aliases={0: 0},
        compiler_params=PARAMS,
        name="hand_on",
    )(array, wait_for)


def body(embedded, out_grad, stored, sample_ids, lengths, weight, gain):
    section = lax.axis_index("section")
    data = lax.axis_index("dp")
    y, a = section // 2, section % 2
    xh, c = data // 16, data % 2
    z = (data // 2) % N_Z
    place = jnp.stack([xh, a, c, z])
    table = jnp.stack([2 * y + c, 3 * y + c, c, a])
    stored = stored.reshape(24, 2, QTR, D)

    first = jnp.where(a == 0, embedded, send(embedded, CORES))
    given = jnp.where(a == 1, out_grad, send(out_grad, CORES))
    gain_row = jnp.where(a == c, gain, send(gain, TURN))

    limits = jnp.where(a == c, lengths, send(lengths, CORES))
    late_table = jnp.concatenate([table, limits])
    held = held_rows(sample_ids, stored)
    full = gather_weight(place, weight[0], [held], [late_table, first, given, gain_row])
    held_other = send(held, TURN)

    stash = slopes = None
    kept, normed, leaving = None, [], []
    up_core, up_chip, down_core, down_chip = {}, {}, {}, {}
    for tick in range(LAST + TICKS):
        if tick < TICKS:
            blocks = {}
            if tick < N_MICRO:
                blocks["first"] = (first, tick)
            if tick in up_core:
                blocks["core"] = (up_core[tick], 0)
            if tick in up_chip:
                blocks["chip"] = (up_chip[tick], 0)
            if tick >= LAST:
                blocks["held"] = (held, tick - LAST)
                blocks["held_other"] = (held_other, tick - LAST)
            msg, *stash = forward_tick(
                tick,
                late_table if tick >= LAST else table,
                blocks,
                full,
                gain_row,
                stash,
                [held_other] if tick == LAST - 1 else [],
            )
            if tick < TICKS - 1:
                up_core[tick + 1] = send(msg, UP_CORE)
            if 1 <= tick <= LAST:
                up_chip[tick + 2] = send(msg, UP_CHIP)
            if tick == TICKS - 1:
                normed = [stash[3], send(stash[3], FIRST), send(stash[3], SECOND)]
                kept = stash[2]
        if tick >= LAST:
            step = tick - LAST
            blocks = {}
            if step < N_MICRO:
                blocks["given"] = (given, step)
            if step in down_core:
                blocks["core"] = (down_core[step], 0)
            if step in down_chip:
                blocks["chip"] = (down_chip[step], 0)
            msg, stash[:2], slopes, halves = backward_tick(
                step,
                late_table if step < N_MICRO else table,
                blocks,
                full,
                gain_row,
                stash[:2],
                slopes,
                normed[1:] if step == 8 else [],
            )
            if step < TICKS - 1:
                down_core[step + 1] = send(msg, DOWN_CORE)
            if 1 <= step <= LAST:
                down_chip[step + 2] = send(msg, DOWN_CHIP)
            if halves:
                leaving.append((halves[1], send(halves[0], FIRST), send(halves[1], SECOND)))

    kept = hand_on(kept, leaving[1][1])
    kept_other = send(kept, TURN)
    flags = jnp.stack([section == N_SEC - 1, a == c]).astype(jnp.int32)
    boundary = boundary_rows(sample_ids, jnp.concatenate([lengths, flags]), kept, kept_other, stored)
    shard = scatter_grad(place, list(zip(normed, *leaving)), c, boundary)
    return (boundary, shard[None])


def solution(mesh):
    in_specs = (
        P("dp", None),
        P("dp", None),
        P("section", None, "dp", None, None),
        P("dp"),
        P("dp"),
        P("section", "dp", None),
        P("section", None),
    )
    out_specs = (P("section", "dp", None), P("section", "dp", None))
    return jax.shard_map(body, mesh=mesh, in_specs=in_specs, out_specs=out_specs, check_vma=False)
```

```python
import functools

import jax
import jax.numpy as jnp
from jax import lax
from jax.experimental import pallas as pl
from jax.experimental.pallas import tpu as pltpu
from jax.sharding import PartitionSpec as P

D = 2048
QTR = 32
N_MICRO = 4
ROWS = 128
N_SEC = 8
N_Z = 8
LAST = 10
TICKS = LAST + N_MICRO
EPS = 1e-6
BF = jnp.bfloat16
F32 = jnp.float32
BOTH = ("section", "dp")


def device(y, a, xh, z, c):
    return (2 * y + a) * 32 + 16 * xh + 2 * z + c


def pairs_of(target):
    out = []
    for y in range(4):
        for a in range(2):
            for xh in range(2):
                for z in range(N_Z):
                    for c in range(2):
                        to = target(y, a, xh, z, c)
                        if to is not None:
                            out.append((device(y, a, xh, z, c), device(*to)))
    return out


TURN = pairs_of(lambda y, a, xh, z, c: (y, c, xh, z, a) if a != c else None)
TO_BEFORE = pairs_of(
    lambda y, a, xh, z, c: (y, 0, xh, z, a) if c == 1 else (y - 1, 1, xh, z, a) if y > 0 else None
)
TURN_LAST = pairs_of(lambda y, a, xh, z, c: (y, 1, xh, z, a) if y == 3 and c == 1 and a == 0 else None)
CORES = pairs_of(lambda y, a, xh, z, c: (y, a, xh, z, 1 - c))
RIGHT = pairs_of(lambda y, a, xh, z, c: (y, a, xh, (z + 1) % N_Z, c))
LEFT = pairs_of(lambda y, a, xh, z, c: (y, a, xh, (z - 1) % N_Z, c))
UP_CORE = pairs_of(lambda y, a, xh, z, c: (y, a, xh, z, 1) if c == 0 else None)
UP_CHIP = pairs_of(lambda y, a, xh, z, c: (y + 1, a, xh, z, 0) if c == 1 and y < 3 else None)
DOWN_CORE = pairs_of(lambda y, a, xh, z, c: (y, a, xh, z, 0) if c == 1 else None)
DOWN_CHIP = pairs_of(lambda y, a, xh, z, c: (y - 1, a, xh, z, 1) if c == 0 and y > 0 else None)
FAR_X = pairs_of(lambda y, a, xh, z, c: (y, a, 1 - xh, z, c))
FAR_X_CORE = pairs_of(lambda y, a, xh, z, c: (y, a, 1 - xh, z, 1 - c))


def beside(y, a, xh, z, step, core):
    x = (2 * xh + a + step) % 4
    return (y, x % 2, x // 2, z, core)


TO_NEXT = pairs_of(
    lambda y, a, xh, z, c: beside(y, a, xh, z, 1, a) if c == 0 else (y, a, xh, z, 0) if a == 0 else None
)
TO_PREVIOUS = pairs_of(
    lambda y, a, xh, z, c: beside(y, a, xh, z, -1, a) if c == 1 else (y, a, xh, z, 1) if a == 1 else None
)

FIRST = pairs_of(
    lambda y, a, xh, z, c: (y, a, xh, z, 1 - a)
    if c == a
    else beside(y, a, xh, z, -1, 0)
    if a == 1
    else beside(y, a, xh, z, 1, 1)
)
SECOND = pairs_of(
    lambda y, a, xh, z, c: None
    if c == a
    else beside(y, a, xh, z, 1, 1)
    if a == 1
    else beside(y, a, xh, z, -1, 0)
)

CHUNK = 256
HALF = 1024
QUARTER = 512


def send(array, pairs):
    return lax.ppermute(array, BOTH, pairs)


ANY = pl.BlockSpec(memory_space=pl.ANY)
WHOLE = pl.BlockSpec((ROWS, D), lambda i, tab: (0, 0))
COST = pl.CostEstimate(flops=2**20, bytes_accessed=2**18, transcendentals=0)
PARAMS = pltpu.CompilerParams(vmem_limit_bytes=12 * 2**20)


def whole(shape):
    return pl.BlockSpec(shape, lambda i, place: (0,) * len(shape))


def placed(kernel, name, place, arrays, outs):
    return pl.pallas_call(
        kernel,
        grid_spec=pltpu.PrefetchScalarGridSpec(
            num_scalar_prefetch=1,
            grid=(1,),
            in_specs=[whole(r.shape) for r in arrays],
            out_specs=[whole(shape) for shape, _ in outs],
        ),
        out_shape=[jax.ShapeDtypeStruct(shape, dtype) for shape, dtype in outs],
        compiler_params=PARAMS,
        name=name,
    )(place, *arrays)


def half_columns(index):
    return pl.ds(pl.multiple_of(index * HALF, HALF), HALF)


def part_rows(index, rows):
    return pl.ds(pl.multiple_of(index * rows, rows), rows)


def divide_kernel(place, shard, mine, other):
    mine[...] = shard[:, half_columns(place[2])]
    other[...] = shard[:, half_columns(1 - place[2])]


def arrange_kernel(place, p00, p01, p10, p11, out):
    for dx, dt, part in ((0, 0, p00), (0, 1, p01), (1, 0, p10), (1, 1, p11)):
        out[part_rows((place[0] ^ dx) * 2 + (place[2] ^ dt), 64), :] = part[...]


def pack(pieces, wait_for):
    rows = sum(piece.shape[0] for piece in pieces)

    def kernel(*refs):
        out, at = refs[len(pieces) + len(wait_for)], 0
        for piece in refs[: len(pieces)]:
            out[at : at + piece.shape[0], :] = piece[...]
            at += piece.shape[0]

    return pl.pallas_call(
        kernel,
        grid=(1,),
        in_specs=[pl.BlockSpec(p.shape, lambda i: (0, 0)) for p in pieces] + [ANY] * len(wait_for),
        out_specs=[pl.BlockSpec((rows, HALF), lambda i: (0, 0))] + [ANY] * len(pieces),
        out_shape=[jax.ShapeDtypeStruct((rows, HALF), BF)]
        + [jax.ShapeDtypeStruct(p.shape, BF) for p in pieces],
        input_output_aliases={i: 1 + i for i in range(len(pieces))},
        compiler_params=PARAMS,
        name="pack",
    )(*pieces, *wait_for)


def place_chunk(place, k, full, own, following, previous, at, wait_for):
    count = len(own)
    skip = 0 if full is None else 1

    def kernel(place, *refs):
        pieces, arrived, out = refs[:count], refs[count : count + 2], refs[count + 2 + skip + len(wait_for)]
        same = place[1] == place[2]
        for c in range(2):

            @pl.when(same & (place[2] == c))
            def _():
                row = 0
                for piece in pieces:
                    for at in range(0, piece.shape[0], 128):
                        out[(row + at) // 128, :, c * HALF : (c + 1) * HALF] = piece[at : at + 128, :]
                    row += piece.shape[0]
                for xh in range(2):
                    rows = slice(xh * 128, xh * 128 + 128)
                    out[xh, :, (1 - c) * HALF : (2 - c) * HALF] = arrived[c][rows, :]

        @pl.when(jnp.logical_not(same))
        def _():
            for c in range(2):
                for xh in range(2):
                    rows = slice(xh * 128, xh * 128 + 128)
                    out[xh, :, c * HALF : (c + 1) * HALF] = arrived[c][rows, :]

    block = pl.BlockSpec((CHUNK, HALF), lambda i, place: (at, 0))
    old = [] if full is None else [full]
    return pl.pallas_call(
        kernel,
        grid_spec=pltpu.PrefetchScalarGridSpec(
            num_scalar_prefetch=1,
            grid=(1,),
            in_specs=[whole(p.shape) for p in own] + [block] * 2 + [ANY] * (skip + len(wait_for)),
            out_specs=pl.BlockSpec(
                (2, 128, D), lambda i, place: (0, lax.rem(place[3] + k, N_Z), 0)
            ),
        ),
        out_shape=jax.ShapeDtypeStruct((2, HALF, D), BF),
        input_output_aliases={} if full is None else {count + 3: 0},
        compiler_params=PARAMS,
        name=f"place_{k}",
    )(place, *own, following, previous, *old, *wait_for)


def gather_weight(place, shard, early, ready):
    quarter, chunk = ((64, HALF), BF), ((CHUNK, HALF), BF)
    mine, other = placed(divide_kernel, "divide", place, [shard], [quarter, quarter])
    parts = [mine, send(other, CORES), send(mine, FAR_X), send(other, FAR_X_CORE)]
    first = placed(arrange_kernel, "arrange", place, parts, [chunk])[0]
    right, left, rows = first, first, first
    order = [(0, 0)]
    own = {0: [first]}
    full, before = None, early[:1]
    for step in range(1, 6):
        if step < 4:
            right, left = send(right, RIGHT), send(left, LEFT)
        elif step == 4:
            right, left = send(right[:128], RIGHT), send(left[128:], LEFT)
        moved = [send(rows, TO_NEXT), send(rows, TO_PREVIOUS)]
        if step < 5:
            rows, right, left = pack([right, left], before)
        before = moved + early[step : step + 1]
        for k, at in order:
            full = place_chunk(place, k, full, own[k], *moved, at, ready if k == 4 else [])
        order = [(-step % N_Z, 0), (step, 1)] if step < 4 else [(4, 0)]
        if step < 4:
            own[-step % N_Z], own[step] = [right], [left]
        else:
            own[4] = [right, left]
    return full.reshape(D, D)


def sample_of(group):
    early = group < 8
    return jnp.where(early, group // 2, group - 4), jnp.where(early, lax.rem(group, 2), 0)


def held_block(side):
    def index(group, ids, *rest):
        sample, half = sample_of(group)
        return (side * 12 + ids[sample], half, 0, 0)

    return pl.BlockSpec((1, 1, QTR, D), index)


def held_rows(ids, stored):
    def kernel(ids, held_ref, out_ref):
        out_ref[...] = held_ref[0, 0]

    return pl.pallas_call(
        kernel,
        grid_spec=pltpu.PrefetchScalarGridSpec(
            num_scalar_prefetch=1,
            grid=(16,),
            in_specs=[held_block(0)],
            out_specs=pl.BlockSpec((QTR, D), lambda g, ids: (g, 0)),
        ),
        out_shape=jax.ShapeDtypeStruct((N_MICRO * ROWS, D), BF),
        compiler_params=PARAMS,
        name="held_rows",
    )(ids, stored)


def boundary_rows(ids, limits, sources, stored):
    def held_at(quarter):
        def index(micro, ids, limits):
            sample, half = sample_of(micro * 4 + quarter)
            return (12 + ids[sample], half, 0, 0)

        return pl.BlockSpec((1, 1, QTR, D), index)

    def kernel(ids, limits, s0, s1, s2, h0, h1, h2, h3, out_ref):
        for quarter, held_ref in enumerate((h0, h1, h2, h3)):
            sample, half = sample_of(pl.program_id(0) * 4 + quarter)
            row = lax.broadcasted_iota(jnp.int32, (QTR, 1), 0) + half * QTR
            live = (row < limits[sample]) | (limits[12] == 1)
            rows = slice(quarter * QTR, (quarter + 1) * QTR)
            held = held_ref[0, 0].astype(F32)

            for which, source in enumerate((s0, s1, s2)):

                @pl.when(limits[13] == which)
                def _():
                    value = source[0, rows, :].astype(F32)
                    out_ref[0, rows, :] = jnp.where(live, value, held).astype(BF)

    return pl.pallas_call(
        kernel,
        grid_spec=pltpu.PrefetchScalarGridSpec(
            num_scalar_prefetch=2,
            grid=(N_MICRO,),
            in_specs=[pl.BlockSpec((1, ROWS, D), lambda m, *tables: (m, 0, 0))] * 3
            + [held_at(quarter) for quarter in range(4)],
            out_specs=pl.BlockSpec((1, ROWS, D), lambda m, *tables: (0, m, 0)),
        ),
        out_shape=jax.ShapeDtypeStruct((1, N_MICRO * ROWS, D), BF),
        compiler_params=PARAMS,
        name="boundary_rows",
    )(ids, limits, *sources, stored, stored, stored, stored)


def product_kernel(has, place, *refs):
    rows = N_MICRO * ROWS
    out, total_ref = refs[-2:]

    def add(sources):
        total = jnp.zeros((CHUNK, QUARTER), F32)
        for source in sources:
            low, high, early, late = refs[4 * source : 4 * source + 4]
            normed = jnp.concatenate(
                [low[...].reshape(rows, 128), high[...].reshape(rows, 128)], axis=1
            )
            slope = jnp.concatenate(
                [early[...].reshape(rows // 2, QUARTER), late[...].reshape(rows // 2, QUARTER)], axis=0
            )
            total = total + lax.dot_general(
                normed, slope, (((0,), (0,)), ((), ())), preferred_element_type=F32
            )
        total_ref[...] = total

    @pl.when(place[1] == place[2])
    def _():
        add((0, 1))

    @pl.when(place[1] != place[2])
    def _():
        add((1, 2))

    total = total_ref[...]
    for ref in refs[12 : 12 + has]:
        total = total + ref[...].astype(F32)
    out[...] = total.astype(BF)


def product(place, sums, k, part, arrived, wait_for=()):
    piece = pl.BlockSpec((CHUNK, QUARTER), lambda i, place: (0, 0))

    def columns(xh):
        return pl.BlockSpec(
            (N_MICRO, ROWS, 128), lambda i, place: (0, 0, xh * N_Z + lax.rem(place[3] + k, N_Z))
        )

    specs, arrays = [], []
    for normed, early, late in sums:
        specs += [columns(0), columns(1)]
        specs += [pl.BlockSpec((2, ROWS, QUARTER), lambda i, place: (0, 0, part))] * 2
        arrays += [normed, normed, early, late]
    return pl.pallas_call(
        functools.partial(product_kernel, len(arrived)),
        grid_spec=pltpu.PrefetchScalarGridSpec(
            num_scalar_prefetch=1,
            grid=(1,),
            in_specs=specs + [piece] * len(arrived) + [ANY] * len(wait_for),
            out_specs=piece,
            scratch_shapes=[pltpu.VMEM((CHUNK, QUARTER), F32)],
        ),
        out_shape=jax.ShapeDtypeStruct((CHUNK, QUARTER), BF),
        compiler_params=PARAMS,
        cost_estimate=COST,
        name=f"product_{k}_{part}",
    )(place, *arrays, *arrived, *wait_for)


def split_x_kernel(place, q0, q1, mine, other):
    for out, xh in ((mine, place[0]), (other, 1 - place[0])):
        rows = part_rows(xh, 128)
        out[:, :QUARTER] = q0[rows, :]
        out[:, QUARTER:] = q1[rows, :]


def split_core_kernel(place, mine, arrived, own, other, total):
    total[...] = mine[...].astype(F32) + arrived[...].astype(F32)
    own[...] = total[part_rows(place[2], 64), :]
    other[...] = total[part_rows(1 - place[2], 64), :].astype(BF)


def scatter_grad(place, sums, core, wait_for):
    to_right = [send(product(place, sums, 4, 0, []), RIGHT), None]
    to_left = [None, send(product(place, sums, 4, 1, []), LEFT)]
    for step in range(3, 0, -1):
        for part in (1, 0):
            held = to_right[part]
            to_right[part] = send(
                product(place, sums, step, part, [] if held is None else [held]), RIGHT
            )
            held = to_left[1 - part]
            to_left[1 - part] = send(
                product(place, sums, N_Z - step, 1 - part, [] if held is None else [held]), LEFT
            )
    quarters = [
        product(place, sums, 0, part, [to_right[part], to_left[part]], [wait_for]) for part in range(2)
    ]
    block = ((128, HALF), BF)
    mine, other = placed(split_x_kernel, "split_x", place, quarters, [block, block])
    arrived = send(other, FAR_X)
    own, other, _ = placed(
        split_core_kernel, "split_core", place, [mine, arrived],
        [((64, HALF), F32), ((64, HALF), BF), ((128, HALF), F32)],
    )
    arrived = send(other, CORES).astype(F32)
    return jnp.where(
        core == 0,
        jnp.concatenate([own, arrived], axis=1),
        jnp.concatenate([arrived, own], axis=1),
    )


def live_mask(tab, micro):
    row = lax.broadcasted_iota(jnp.int32, (ROWS, 1), 0)
    if micro < 2:
        limit = jnp.where(row < 64, tab[4 + 2 * micro], tab[5 + 2 * micro])
        return row % 64 < limit
    limit = jnp.zeros((ROWS, 1), jnp.int32)
    for q in range(4):
        limit = jnp.where(row // QTR == q, tab[4 * micro + q], limit)
    return row % QTR < limit


def slot_block(micro):
    return jnp.where((micro >= 0) & (micro < N_MICRO), micro, N_MICRO)


def forward_kernel(tick, names, tab, *refs):
    ref = dict(zip(names, refs))
    micro = tick - tab[1]
    block = tab[0]
    active = (micro >= 0) & (micro < N_MICRO)
    x_ref, normed_ref = ref["x"], ref["normed"]

    if "first" in ref:

        @pl.when(active & (block == 0))
        def _():
            x_ref[0] = ref["first"][...]

    if "core" in ref:

        @pl.when(active & (block % 2 == 1))
        def _():
            x_ref[0] = ref["core"][...]

    if "chip" in ref:

        @pl.when(active & (block % 2 == 0) & (block > 0))
        def _():
            x_ref[0] = ref["chip"][...]

    if "held" in ref:

        for name, mine in (("held", True), ("held_other", False)):

            @pl.when((block == N_SEC - 1) & ((tab[2] == tab[3]) == mine))
            def _():
                live = live_mask(tab, tick - LAST)
                x = jnp.where(live, x_ref[0].astype(F32), ref[name][...].astype(F32))
                x_ref[0] = x.astype(BF)

    @pl.when(active)
    def _():
        values = x_ref[0].astype(F32)
        inverse = lax.rsqrt(jnp.mean(values * values, axis=1, keepdims=True) + EPS)
        normed_ref[0] = (values * inverse * ref["gain"][...].astype(F32)).astype(BF)
        for at in range(0, D, QUARTER):
            cols = slice(at, at + QUARTER)
            mixed = jnp.dot(normed_ref[0], ref["weight"][:, cols], preferred_element_type=F32)
            ref["mixed"][0, :, cols] = mixed
            output = (x_ref[0, :, cols].astype(F32) + mixed / (1.0 + jnp.exp(-mixed))).astype(BF)
            ref["msg"][:, cols] = output


STASH = {"x": BF, "mixed": F32, "normed": BF}


def forward_tick(tick, tab, blocks, weight, gain, stash, wait_for):
    slot = pl.BlockSpec((1, ROWS, D), lambda i, tab: (slot_block(tick - tab[1]), 0, 0))
    names = [*blocks, "weight", "gain"]
    arrays = [array for array, _ in blocks.values()] + [weight, gain]
    specs = [pl.BlockSpec((ROWS, D), lambda i, tab, at=at: (at, 0)) for _, at in blocks.values()]
    specs += [whole((D, D)), whole((1, D))]
    old = [] if stash is None else list(stash)
    aliases = {1 + len(arrays) + i: 1 + i for i in range(len(old))}
    names += [None] * (len(old) + len(wait_for)) + ["msg", *STASH]
    return pl.pallas_call(
        functools.partial(forward_kernel, tick, names),
        grid_spec=pltpu.PrefetchScalarGridSpec(
            num_scalar_prefetch=1,
            grid=(1,),
            in_specs=specs + [ANY] * (len(old) + len(wait_for)),
            out_specs=[WHOLE] + [slot] * 3,
        ),
        out_shape=[jax.ShapeDtypeStruct((ROWS, D), BF)]
        + [jax.ShapeDtypeStruct((N_MICRO + 1, ROWS, D), kind) for kind in STASH.values()],
        input_output_aliases=aliases,
        compiler_params=PARAMS,
        cost_estimate=COST,
        name=f"forward_{tick}",
    )(tab, *arrays, *old, *wait_for)


def backward_kernel(tick, names, tab, *refs):
    ref = dict(zip(names, refs))
    up_ref, slope_ref, weighted_ref = refs[-3:]
    x_ref, msg_ref = ref["x"], ref["msg"]
    micro = tick - (LAST - tab[1])
    slot = jnp.clip(micro, 0, N_MICRO - 1)
    block = tab[0]
    active = (micro >= 0) & (micro < N_MICRO)

    if "given" in ref:
        @pl.when(active & (block == N_SEC - 1))
        def _():
            given = ref["given"][...].astype(F32)
            up_ref[...] = jnp.where(live_mask(tab, tick), given, 0.0).astype(BF)

    if "core" in ref:

        @pl.when(active & (block % 2 == 0))
        def _():
            up_ref[...] = ref["core"][...]

    if "chip" in ref:

        @pl.when(active & (block % 2 == 1) & (block < N_SEC - 1))
        def _():
            up_ref[...] = ref["chip"][...]

    @pl.when(active)
    def _():
        mixed = ref["mixed"][slot]
        gated = 1.0 / (1.0 + jnp.exp(-mixed))
        up = up_ref[...].astype(F32)
        slope_ref[...] = (up * gated * (1.0 + mixed * (1.0 - gated))).astype(BF)
        for j, name in enumerate(("slope_0", "slope_1")):
            ref[name][0] = slope_ref[:, half_columns(tab[3] ^ (1 - j))]

    if tick in (LAST + 1, LAST + 3):
        for j in "01":
            leave, old = ref["leave_" + j], ref["old_" + j]
            leave[0] = old[tick - LAST - 1]

            @pl.when(block == 0)
            def _():
                leave[1] = ref["slope_" + j][0]

            @pl.when(block != 0)
            def _():
                leave[1] = old[tick - LAST]

    @pl.when(active & (block > 0))
    def _():
        values = x_ref[slot].astype(F32)
        inverse = lax.rsqrt(jnp.mean(values * values, axis=1, keepdims=True) + EPS)
        total = jnp.zeros((ROWS, 128), F32)
        for at in range(0, D, QUARTER):
            cols = slice(at, at + QUARTER)
            back = lax.dot_general(
                slope_ref[...],
                ref["weight"][cols, :],
                (((1,), (1,)), ((), ())),
                preferred_element_type=F32,
            )
            weighted = back * ref["gain"][:, cols].astype(F32)
            weighted_ref[:, cols] = weighted
            terms = weighted * x_ref[slot, :, cols].astype(F32)
            for part in range(0, QUARTER, 128):
                total = total + terms[:, part : part + 128]
        centre = jnp.sum(total, axis=1, keepdims=True) * (1.0 / D)
        factor = inverse * inverse * inverse * centre
        grad = up_ref[...].astype(F32) + inverse * weighted_ref[...]
        msg_ref[...] = (grad - x_ref[slot].astype(F32) * factor).astype(BF)


def backward_tick(tick, tab, blocks, weight, gain, stash, slopes, wait_for):
    def micro_of(tab):
        return tick - (LAST - tab[1])

    read = whole((N_MICRO + 1, ROWS, D))
    slot = pl.BlockSpec((1, ROWS, HALF), lambda i, tab: (slot_block(micro_of(tab)), 0, 0))
    leaving = tick in (LAST + 1, LAST + 3)
    hold = tick < N_MICRO
    names = [*blocks, "weight", "gain", "x", "mixed"]
    arrays = [array for array, _ in blocks.values()] + [weight, gain, *stash]
    specs = [pl.BlockSpec((ROWS, D), lambda i, tab, at=at: (at, 0)) for _, at in blocks.values()]
    specs += [whole((D, D)), whole((1, D)), read, read]
    aliases = {len(arrays) - 1: 3, len(arrays): 4} if hold else {}
    if slopes is not None:
        aliases |= {len(arrays) + 1: 1, len(arrays) + 2: 2}
        arrays += slopes
        names += ["old_0", "old_1"]
        specs += [whole((N_MICRO + 1, ROWS, HALF)) if leaving else ANY] * 2
    names += [None] * len(wait_for) + ["msg", "slope_0", "slope_1"] + [None] * (2 * hold)
    names += ["leave_0", "leave_1"] if leaving else []
    leave = (2, ROWS, HALF)
    kept = jax.ShapeDtypeStruct((N_MICRO + 1, ROWS, HALF), BF)
    out = pl.pallas_call(
        functools.partial(backward_kernel, tick, names),
        grid_spec=pltpu.PrefetchScalarGridSpec(
            num_scalar_prefetch=1,
            grid=(1,),
            in_specs=specs + [ANY] * len(wait_for),
            out_specs=[WHOLE, slot, slot] + [ANY] * (2 * hold) + [whole(leave)] * (2 * leaving),
            scratch_shapes=[pltpu.VMEM((ROWS, D), BF)] * 2 + [pltpu.VMEM((ROWS, D), F32)],
        ),
        out_shape=[jax.ShapeDtypeStruct((ROWS, D), BF), kept, kept]
        + [jax.ShapeDtypeStruct(s.shape, s.dtype) for s in stash if hold]
        + [jax.ShapeDtypeStruct(leave, BF)] * (2 * leaving),
        input_output_aliases=aliases,
        compiler_params=PARAMS,
        cost_estimate=COST,
        name=f"backward_{tick}",
    )(tab, *arrays, *wait_for)
    return out[0], out[3:5] if hold else stash, out[1:3], out[3:] if leaving else []


def hand_on(array, wait_for):
    def kernel(*refs):
        pass

    return pl.pallas_call(
        kernel,
        in_specs=[ANY] * (1 + len(wait_for)),
        out_specs=ANY,
        out_shape=jax.ShapeDtypeStruct(array.shape, array.dtype),
        input_output_aliases={0: 0},
        compiler_params=PARAMS,
        name="hand_on",
    )(array, *wait_for)


def join(pieces):
    def kernel(*refs):
        for i, piece in enumerate(refs[:-1]):
            refs[-1][i] = piece[...]

    return pl.pallas_call(
        kernel,
        grid=(1,),
        in_specs=[pl.BlockSpec((ROWS, D), lambda i: (0, 0))] * len(pieces),
        out_specs=pl.BlockSpec((len(pieces), ROWS, D), lambda i: (0, 0, 0)),
        out_shape=jax.ShapeDtypeStruct((len(pieces), ROWS, D), BF),
        compiler_params=PARAMS,
        name="join",
    )(*pieces)


def body(embedded, out_grad, stored, sample_ids, lengths, weight, gain):
    section = lax.axis_index("section")
    data = lax.axis_index("dp")
    y, a = section // 2, section % 2
    xh, c = data // 16, data % 2
    z = (data // 2) % N_Z
    place = jnp.stack([xh, a, c, z])
    table = jnp.stack([2 * y + c, 3 * y + c, c, a])
    stored = stored.reshape(24, 2, QTR, D)

    first = jnp.where(a == 0, embedded, send(embedded, CORES))
    given = jnp.where(a == 1, out_grad, send(out_grad, CORES))
    gain_row = jnp.where(a == c, gain, send(gain, TURN))

    limits = jnp.where(a == c, lengths, send(lengths, CORES))
    late_table = jnp.concatenate([table, limits])
    held = held_rows(sample_ids, stored)
    full = gather_weight(place, weight[0], [held, first, given], [late_table, gain_row])
    held_other = send(held, TURN)

    stash = slopes = None
    normed, leaving, finals = [], [], []
    up_core, up_chip, down_core, down_chip = {}, {}, {}, {}
    for tick in range(LAST + TICKS):
        if tick < TICKS:
            blocks = {}
            if tick < N_MICRO:
                blocks["first"] = (first, tick)
            if tick in up_core:
                blocks["core"] = (up_core[tick], 0)
            if tick in up_chip:
                blocks["chip"] = (up_chip[tick], 0)
            if tick >= LAST:
                blocks["held"] = (held, tick - LAST)
                blocks["held_other"] = (held_other, tick - LAST)
            msg, *stash = forward_tick(
                tick,
                late_table if tick >= LAST else table,
                blocks,
                full,
                gain_row,
                stash,
                [held_other] if tick == LAST - 1 else [],
            )
            if tick >= LAST:
                finals.append(msg)
            if tick < TICKS - 1:
                up_core[tick + 1] = send(msg, UP_CORE)
            if 1 <= tick <= LAST:
                up_chip[tick + 2] = send(msg, UP_CHIP)
            if tick == TICKS - 1:
                normed = [stash[2], send(stash[2], FIRST), send(stash[2], SECOND)]
        if tick >= LAST:
            step = tick - LAST
            blocks = {}
            if step < N_MICRO:
                blocks["given"] = (given, step)
            if step in down_core:
                blocks["core"] = (down_core[step], 0)
            if step in down_chip:
                blocks["chip"] = (down_chip[step], 0)
            msg, stash[:2], slopes, halves = backward_tick(
                step,
                late_table if step < N_MICRO else table,
                blocks,
                full,
                gain_row,
                stash[:2],
                slopes,
                normed[1:] if step == 8 else list(leaving[0][1:]) if step == LAST + 3 else [],
            )
            if step < TICKS - 1:
                down_core[step + 1] = send(msg, DOWN_CORE)
            if 1 <= step <= LAST:
                down_chip[step + 2] = send(msg, DOWN_CHIP)
            if halves:
                leaving.append((halves[1], send(halves[0], FIRST), send(halves[1], SECOND)))

    slopes_there = [*leaving[1][1:], *leaving[0][1:]]
    following = send(hand_on(stash[0], slopes_there), TO_BEFORE)
    finals = join(finals)
    finals_other = send(finals, TURN_LAST)
    last = section == N_SEC - 1
    flags = jnp.stack([last, jnp.where(last, jnp.where(a == c, 1, 2), 0)]).astype(jnp.int32)
    boundary = boundary_rows(sample_ids, jnp.concatenate([lengths, flags]), [following, finals, finals_other], stored)
    shard = scatter_grad(place, list(zip(normed, *leaving)), c, boundary)
    return (boundary, shard[None])


def solution(mesh):
    in_specs = (
        P("dp", None),
        P("dp", None),
        P("section", None, "dp", None, None),
        P("dp"),
        P("dp"),
        P("section", "dp", None),
        P("section", None),
    )
    out_specs = (P("section", "dp", None), P("section", "dp", None))
    return jax.shard_map(body, mesh=mesh, in_specs=in_specs, out_specs=out_specs, check_vma=False)
```

```python
import functools

import jax
import jax.numpy as jnp
from jax import lax
from jax.experimental import pallas as pl
from jax.experimental.pallas import tpu as pltpu
from jax.sharding import PartitionSpec as P

D = 2048
QTR = 32
N_MICRO = 4
ROWS = 128
N_SEC = 8
N_Z = 8
LAST = 10
TICKS = LAST + N_MICRO
EPS = 1e-6
BF = jnp.bfloat16
F32 = jnp.float32
BOTH = ("section", "dp")


def device(y, a, xh, z, c):
    return (2 * y + a) * 32 + 16 * xh + 2 * z + c


def pairs_of(target):
    out = []
    for y in range(4):
        for a in range(2):
            for xh in range(2):
                for z in range(N_Z):
                    for c in range(2):
                        to = target(y, a, xh, z, c)
                        if to is not None:
                            out.append((device(y, a, xh, z, c), device(*to)))
    return out


TURN = pairs_of(lambda y, a, xh, z, c: (y, c, xh, z, a) if a != c else None)
TO_BEFORE = pairs_of(
    lambda y, a, xh, z, c: (y, 0, xh, z, a) if c == 1 else (y - 1, 1, xh, z, a) if y > 0 else None
)
TURN_LAST = pairs_of(lambda y, a, xh, z, c: (y, 1, xh, z, a) if y == 3 and c == 1 and a == 0 else None)
CORES = pairs_of(lambda y, a, xh, z, c: (y, a, xh, z, 1 - c))
RIGHT = pairs_of(lambda y, a, xh, z, c: (y, a, xh, (z + 1) % N_Z, c))
LEFT = pairs_of(lambda y, a, xh, z, c: (y, a, xh, (z - 1) % N_Z, c))
UP_CORE = pairs_of(lambda y, a, xh, z, c: (y, a, xh, z, 1) if c == 0 else None)
UP_CHIP = pairs_of(lambda y, a, xh, z, c: (y + 1, a, xh, z, 0) if c == 1 and y < 3 else None)
DOWN_CORE = pairs_of(lambda y, a, xh, z, c: (y, a, xh, z, 0) if c == 1 else None)
DOWN_CHIP = pairs_of(lambda y, a, xh, z, c: (y - 1, a, xh, z, 1) if c == 0 and y > 0 else None)
FAR_X = pairs_of(lambda y, a, xh, z, c: (y, a, 1 - xh, z, c))
FAR_X_CORE = pairs_of(lambda y, a, xh, z, c: (y, a, 1 - xh, z, 1 - c))


def beside(y, a, xh, z, step, core):
    x = (2 * xh + a + step) % 4
    return (y, x % 2, x // 2, z, core)


TO_NEXT = pairs_of(
    lambda y, a, xh, z, c: beside(y, a, xh, z, 1, a) if c == 0 else (y, a, xh, z, 0) if a == 0 else None
)
TO_PREVIOUS = pairs_of(
    lambda y, a, xh, z, c: beside(y, a, xh, z, -1, a) if c == 1 else (y, a, xh, z, 1) if a == 1 else None
)

FIRST = pairs_of(
    lambda y, a, xh, z, c: (y, a, xh, z, 1 - a)
    if c == a
    else beside(y, a, xh, z, -1, 0)
    if a == 1
    else beside(y, a, xh, z, 1, 1)
)
SECOND = pairs_of(
    lambda y, a, xh, z, c: None
    if c == a
    else beside(y, a, xh, z, 1, 1)
    if a == 1
    else beside(y, a, xh, z, -1, 0)
)

CHUNK = 256
HALF = 1024
QUARTER = 512


def send(array, pairs):
    return lax.ppermute(array, BOTH, pairs)


ANY = pl.BlockSpec(memory_space=pl.ANY)
WHOLE = pl.BlockSpec((ROWS, D), lambda i, tab: (0, 0))
COST = pl.CostEstimate(flops=2**20, bytes_accessed=2**18, transcendentals=0)
PARAMS = pltpu.CompilerParams(vmem_limit_bytes=12 * 2**20)


def whole(shape):
    return pl.BlockSpec(shape, lambda i, place: (0,) * len(shape))


def placed(kernel, name, place, arrays, outs, wait_for=()):
    return pl.pallas_call(
        kernel,
        grid_spec=pltpu.PrefetchScalarGridSpec(
            num_scalar_prefetch=1,
            grid=(1,),
            in_specs=[whole(r.shape) for r in arrays] + [ANY] * len(wait_for),
            out_specs=[whole(shape) for shape, _ in outs],
        ),
        out_shape=[jax.ShapeDtypeStruct(shape, dtype) for shape, dtype in outs],
        compiler_params=PARAMS,
        name=name,
    )(place, *arrays, *wait_for)


def half_columns(index):
    return pl.ds(pl.multiple_of(index * HALF, HALF), HALF)


def part_rows(index, rows):
    return pl.ds(pl.multiple_of(index * rows, rows), rows)


def divide_kernel(place, shard, mine, other):
    mine[...] = shard[:, half_columns(place[2])]
    other[...] = shard[:, half_columns(1 - place[2])]


def arrange_kernel(place, p00, p01, p10, p11, out):
    for dx, dt, part in ((0, 0, p00), (0, 1, p01), (1, 0, p10), (1, 1, p11)):
        out[part_rows((place[0] ^ dx) * 2 + (place[2] ^ dt), 64), :] = part[...]


def pack(pieces, wait_for):
    rows = sum(piece.shape[0] for piece in pieces)

    def kernel(*refs):
        out, at = refs[len(pieces) + len(wait_for)], 0
        for piece in refs[: len(pieces)]:
            out[at : at + piece.shape[0], :] = piece[...]
            at += piece.shape[0]

    return pl.pallas_call(
        kernel,
        grid=(1,),
        in_specs=[pl.BlockSpec(p.shape, lambda i: (0, 0)) for p in pieces] + [ANY] * len(wait_for),
        out_specs=[pl.BlockSpec((rows, HALF), lambda i: (0, 0))] + [ANY] * len(pieces),
        out_shape=[jax.ShapeDtypeStruct((rows, HALF), BF)]
        + [jax.ShapeDtypeStruct(p.shape, BF) for p in pieces],
        input_output_aliases={i: 1 + i for i in range(len(pieces))},
        compiler_params=PARAMS,
        name="pack",
    )(*pieces, *wait_for)


def place_chunk(place, k, full, own, following, previous, at, wait_for):
    count = len(own)
    skip = 0 if full is None else 1

    def kernel(place, *refs):
        pieces, arrived, out = refs[:count], refs[count : count + 2], refs[count + 2 + skip + len(wait_for)]
        same = place[1] == place[2]
        for c in range(2):

            @pl.when(same & (place[2] == c))
            def _():
                row = 0
                for piece in pieces:
                    for at in range(0, piece.shape[0], 128):
                        out[(row + at) // 128, :, c * HALF : (c + 1) * HALF] = piece[at : at + 128, :]
                    row += piece.shape[0]
                for xh in range(2):
                    rows = slice(xh * 128, xh * 128 + 128)
                    out[xh, :, (1 - c) * HALF : (2 - c) * HALF] = arrived[c][rows, :]

        @pl.when(jnp.logical_not(same))
        def _():
            for c in range(2):
                for xh in range(2):
                    rows = slice(xh * 128, xh * 128 + 128)
                    out[xh, :, c * HALF : (c + 1) * HALF] = arrived[c][rows, :]

    block = pl.BlockSpec((CHUNK, HALF), lambda i, place: (at, 0))
    old = [] if full is None else [full]
    return pl.pallas_call(
        kernel,
        grid_spec=pltpu.PrefetchScalarGridSpec(
            num_scalar_prefetch=1,
            grid=(1,),
            in_specs=[whole(p.shape) for p in own] + [block] * 2 + [ANY] * (skip + len(wait_for)),
            out_specs=pl.BlockSpec(
                (2, 128, D), lambda i, place: (0, lax.rem(place[3] + k, N_Z), 0)
            ),
        ),
        out_shape=jax.ShapeDtypeStruct((2, HALF, D), BF),
        input_output_aliases={} if full is None else {count + 3: 0},
        compiler_params=PARAMS,
        name=f"place_{k}",
    )(place, *own, following, previous, *old, *wait_for)


def gather_weight(place, shard, early, ready):
    quarter, chunk = ((64, HALF), BF), ((CHUNK, HALF), BF)
    mine, other = placed(divide_kernel, "divide", place, [shard], [quarter, quarter])
    parts = [mine, send(other, CORES), send(mine, FAR_X), send(other, FAR_X_CORE)]
    first = placed(arrange_kernel, "arrange", place, parts, [chunk])[0]
    right, left, rows = first, first, first
    order = [(0, 0)]
    own = {0: [first]}
    full, before = None, early[:1]
    for step in range(1, 6):
        if step < 4:
            right, left = send(right, RIGHT), send(left, LEFT)
        elif step == 4:
            right, left = send(right[:128], RIGHT), send(left[128:], LEFT)
        moved = [send(rows, TO_NEXT), send(rows, TO_PREVIOUS)]
        if step < 5:
            rows, right, left = pack([right, left], before)
        before = moved + early[step : step + 1]
        for k, at in order:
            full = place_chunk(place, k, full, own[k], *moved, at, ready if k == 4 else [])
        order = [(-step % N_Z, 0), (step, 1)] if step < 4 else [(4, 0)]
        if step < 4:
            own[-step % N_Z], own[step] = [right], [left]
        else:
            own[4] = [right, left]
    return full.reshape(D, D)


def sample_of(group):
    early = group < 8
    return jnp.where(early, group // 2, group - 4), jnp.where(early, lax.rem(group, 2), 0)


def held_block(side):
    def index(group, ids, *rest):
        sample, half = sample_of(group)
        return (side * 12 + ids[sample], half, 0, 0)

    return pl.BlockSpec((1, 1, QTR, D), index)


def held_rows(ids, stored):
    def kernel(ids, held_ref, out_ref):
        out_ref[...] = held_ref[0, 0]

    return pl.pallas_call(
        kernel,
        grid_spec=pltpu.PrefetchScalarGridSpec(
            num_scalar_prefetch=1,
            grid=(16,),
            in_specs=[held_block(0)],
            out_specs=pl.BlockSpec((QTR, D), lambda g, ids: (g, 0)),
        ),
        out_shape=jax.ShapeDtypeStruct((N_MICRO * ROWS, D), BF),
        compiler_params=PARAMS,
        name="held_rows",
    )(ids, stored)


def boundary_rows(ids, limits, sources, stored):
    def held_at(quarter):
        def index(micro, ids, limits):
            sample, half = sample_of(micro * 4 + quarter)
            return (12 + ids[sample], half, 0, 0)

        return pl.BlockSpec((1, 1, QTR, D), index)

    def kernel(ids, limits, s0, s1, s2, h0, h1, h2, h3, out_ref):
        for quarter, held_ref in enumerate((h0, h1, h2, h3)):
            sample, half = sample_of(pl.program_id(0) * 4 + quarter)
            row = lax.broadcasted_iota(jnp.int32, (QTR, 1), 0) + half * QTR
            live = (row < limits[sample]) | (limits[12] == 1)
            rows = slice(quarter * QTR, (quarter + 1) * QTR)
            held = held_ref[0, 0].astype(F32)

            for which, source in enumerate((s0, s1, s2)):

                @pl.when(limits[13] == which)
                def _():
                    value = source[0, rows, :].astype(F32)
                    out_ref[0, rows, :] = jnp.where(live, value, held).astype(BF)

    return pl.pallas_call(
        kernel,
        grid_spec=pltpu.PrefetchScalarGridSpec(
            num_scalar_prefetch=2,
            grid=(N_MICRO,),
            in_specs=[pl.BlockSpec((1, ROWS, D), lambda m, *tables: (m, 0, 0))] * 3
            + [held_at(quarter) for quarter in range(4)],
            out_specs=pl.BlockSpec((1, ROWS, D), lambda m, *tables: (0, m, 0)),
        ),
        out_shape=jax.ShapeDtypeStruct((1, N_MICRO * ROWS, D), BF),
        compiler_params=PARAMS,
        name="boundary_rows",
    )(ids, limits, *sources, stored, stored, stored, stored)


def product_kernel(has, place, *refs):
    rows = N_MICRO * ROWS
    out = refs[-1]

    total = jnp.zeros((CHUNK, QUARTER), F32)
    for source in range(2):
        low, high, early, late = refs[4 * source : 4 * source + 4]
        normed = jnp.concatenate(
            [low[...].reshape(rows, 128), high[...].reshape(rows, 128)], axis=1
        )
        slope = jnp.concatenate(
            [early[...].reshape(rows // 2, QUARTER), late[...].reshape(rows // 2, QUARTER)], axis=0
        )
        total = total + lax.dot_general(
            normed, slope, (((0,), (0,)), ((), ())), preferred_element_type=F32
        )
    for ref in refs[8 : 8 + has]:
        total = total + ref[...].astype(F32)
    out[...] = total.astype(BF)


def product(place, sums, k, part, arrived, wait_for=()):
    piece = pl.BlockSpec((CHUNK, QUARTER), lambda i, place: (0, 0))

    def columns(xh):
        return pl.BlockSpec(
            (N_MICRO, ROWS, 128), lambda i, place: (0, 0, xh * N_Z + lax.rem(place[3] + k, N_Z))
        )

    specs, arrays = [], []
    for normed, early, late in sums:
        specs += [columns(0), columns(1)]
        specs += [pl.BlockSpec((2, ROWS, QUARTER), lambda i, place: (0, 0, part))] * 2
        arrays += [normed, normed, early, late]
    return pl.pallas_call(
        functools.partial(product_kernel, len(arrived)),
        grid_spec=pltpu.PrefetchScalarGridSpec(
            num_scalar_prefetch=1,
            grid=(1,),
            in_specs=specs + [piece] * len(arrived) + [ANY] * len(wait_for),
            out_specs=piece,
        ),
        out_shape=jax.ShapeDtypeStruct((CHUNK, QUARTER), BF),
        compiler_params=PARAMS,
        cost_estimate=COST,
        name=f"product_{k}_{part}",
    )(place, *arrays, *arrived, *wait_for)


def split_x_kernel(place, q0, q1, mine, other):
    for out, xh in ((mine, place[0]), (other, 1 - place[0])):
        rows = part_rows(xh, 128)
        out[:, :QUARTER] = q0[rows, :]
        out[:, QUARTER:] = q1[rows, :]


def split_core_kernel(place, mine, arrived, _, own, other, total):
    total[...] = mine[...].astype(F32) + arrived[...].astype(F32)
    own[...] = total[part_rows(place[2], 64), :]
    other[...] = total[part_rows(1 - place[2], 64), :].astype(BF)


def scatter_grad(place, sums, core, wait_for):
    to_right = [send(product(place, sums, 4, 0, []), RIGHT), None]
    to_left = [None, send(product(place, sums, 4, 1, []), LEFT)]
    for step in range(3, 0, -1):
        for part in (1, 0):
            held = to_right[part]
            to_right[part] = send(
                product(place, sums, step, part, [] if held is None else [held]), RIGHT
            )
            held = to_left[1 - part]
            to_left[1 - part] = send(
                product(place, sums, N_Z - step, 1 - part, [] if held is None else [held]), LEFT
            )
    quarters = [
        product(place, sums, 0, part, [to_right[part], to_left[part]]) for part in range(2)
    ]
    block = ((128, HALF), BF)
    mine, other = placed(split_x_kernel, "split_x", place, quarters, [block, block])
    arrived = send(other, FAR_X)
    own, other, _ = placed(
        split_core_kernel, "split_core", place, [mine, arrived],
        [((64, HALF), F32), ((64, HALF), BF), ((128, HALF), F32)], [wait_for],
    )
    arrived = send(other, CORES).astype(F32)
    return jnp.where(
        core == 0,
        jnp.concatenate([own, arrived], axis=1),
        jnp.concatenate([arrived, own], axis=1),
    )


def live_mask(tab, micro):
    row = lax.broadcasted_iota(jnp.int32, (ROWS, 1), 0)
    if micro < 2:
        limit = jnp.where(row < 64, tab[4 + 2 * micro], tab[5 + 2 * micro])
        return row % 64 < limit
    limit = jnp.zeros((ROWS, 1), jnp.int32)
    for q in range(4):
        limit = jnp.where(row // QTR == q, tab[4 * micro + q], limit)
    return row % QTR < limit


def slot_block(micro):
    return jnp.where((micro >= 0) & (micro < N_MICRO), micro, N_MICRO)


def forward_kernel(tick, names, tab, *refs):
    ref = dict(zip(names, refs))
    micro = tick - tab[1]
    block = tab[0]
    active = (micro >= 0) & (micro < N_MICRO)
    x_ref, normed_ref = ref["x"], ref["normed"]

    if "first" in ref:

        for a, name in ((0, "first"), (1, "first_other")):

            @pl.when(active & (block == 0) & (tab[3] == a))
            def _():
                x_ref[0] = ref[name][...]

    if "core" in ref:

        @pl.when(active & (block % 2 == 1))
        def _():
            x_ref[0] = ref["core"][...]

    if "chip" in ref:

        @pl.when(active & (block % 2 == 0) & (block > 0))
        def _():
            x_ref[0] = ref["chip"][...]

    if "held" in ref:

        for name, mine in (("held", True), ("held_other", False)):

            @pl.when((block == N_SEC - 1) & ((tab[2] == tab[3]) == mine))
            def _():
                live = live_mask(tab, tick - LAST)
                x = jnp.where(live, x_ref[0].astype(F32), ref[name][...].astype(F32))
                x_ref[0] = x.astype(BF)

    @pl.when(active)
    def _():
        values = x_ref[0].astype(F32)
        inverse = lax.rsqrt(jnp.mean(values * values, axis=1, keepdims=True) + EPS)
        normed_ref[0] = (values * inverse * ref["gain"][...].astype(F32)).astype(BF)
        for at in range(0, D, QUARTER):
            cols = slice(at, at + QUARTER)
            mixed = jnp.dot(normed_ref[0], ref["weight"][:, cols], preferred_element_type=F32)
            ref["mixed"][0, :, cols] = mixed.astype(BF)
            output = (x_ref[0, :, cols].astype(F32) + mixed / (1.0 + jnp.exp(-mixed))).astype(BF)
            ref["msg"][:, cols] = output


STASH = {"x": BF, "mixed": BF, "normed": BF}


def forward_tick(tick, tab, blocks, weight, gain, stash, wait_for):
    slot = pl.BlockSpec((1, ROWS, D), lambda i, tab: (slot_block(tick - tab[1]), 0, 0))
    names = [*blocks, "weight", "gain"]
    arrays = [array for array, _ in blocks.values()] + [weight, gain]
    specs = [pl.BlockSpec((ROWS, D), lambda i, tab, at=at: (at, 0)) for _, at in blocks.values()]
    specs += [whole((D, D)), whole((1, D))]
    old = [] if stash is None else list(stash)
    aliases = {1 + len(arrays) + i: 1 + i for i in range(len(old))}
    names += [None] * (len(old) + len(wait_for)) + ["msg", *STASH]
    return pl.pallas_call(
        functools.partial(forward_kernel, tick, names),
        grid_spec=pltpu.PrefetchScalarGridSpec(
            num_scalar_prefetch=1,
            grid=(1,),
            in_specs=specs + [ANY] * (len(old) + len(wait_for)),
            out_specs=[WHOLE] + [slot] * 3,
        ),
        out_shape=[jax.ShapeDtypeStruct((ROWS, D), BF)]
        + [jax.ShapeDtypeStruct((N_MICRO + 1, ROWS, D), kind) for kind in STASH.values()],
        input_output_aliases=aliases,
        compiler_params=PARAMS,
        cost_estimate=COST,
        name=f"forward_{tick}",
    )(tab, *arrays, *old, *wait_for)


def backward_kernel(tick, names, tab, *refs):
    ref = dict(zip(names, refs))
    up_ref, slope_ref, weighted_ref = refs[-3:]
    x_ref, msg_ref = ref["x"], ref["msg"]
    micro = tick - (LAST - tab[1])
    block = tab[0]
    active = (micro >= 0) & (micro < N_MICRO)

    if "given" in ref:
        for a, name in ((1, "given"), (0, "given_other")):

            @pl.when(active & (block == N_SEC - 1) & (tab[3] == a))
            def _():
                given = ref[name][...].astype(F32)
                up_ref[...] = jnp.where(live_mask(tab, tick), given, 0.0).astype(BF)

    if "core" in ref:

        @pl.when(active & (block % 2 == 0))
        def _():
            up_ref[...] = ref["core"][...]

    if "chip" in ref:

        @pl.when(active & (block % 2 == 1) & (block < N_SEC - 1))
        def _():
            up_ref[...] = ref["chip"][...]

    @pl.when(active)
    def _():
        mixed = ref["mixed"][0].astype(F32)
        gated = 1.0 / (1.0 + jnp.exp(-mixed))
        up = up_ref[...].astype(F32)
        slope_ref[...] = (up * gated * (1.0 + mixed * (1.0 - gated))).astype(BF)
        for j, name in enumerate(("slope_0", "slope_1")):
            ref[name][0] = slope_ref[:, half_columns(tab[3] ^ (1 - j))]

    if tick in (LAST + 1, LAST + 3):
        for j in "01":
            leave, old = ref["leave_" + j], ref["old_" + j]
            leave[0] = old[tick - LAST - 1]

            @pl.when(block == 0)
            def _():
                leave[1] = ref["slope_" + j][0]

            @pl.when(block != 0)
            def _():
                leave[1] = old[tick - LAST]

    @pl.when(active & (block > 0))
    def _():
        values = x_ref[0].astype(F32)
        inverse = lax.rsqrt(jnp.mean(values * values, axis=1, keepdims=True) + EPS)
        total = jnp.zeros((ROWS, 128), F32)
        for at in range(0, D, QUARTER):
            cols = slice(at, at + QUARTER)
            back = lax.dot_general(
                slope_ref[...],
                ref["weight"][cols, :],
                (((1,), (1,)), ((), ())),
                preferred_element_type=F32,
            )
            weighted = back * ref["gain"][:, cols].astype(F32)
            weighted_ref[:, cols] = weighted
            terms = weighted * x_ref[0, :, cols].astype(F32)
            for part in range(0, QUARTER, 128):
                total = total + terms[:, part : part + 128]
        centre = jnp.sum(total, axis=1, keepdims=True) * (1.0 / D)
        factor = inverse * inverse * inverse * centre
        grad = up_ref[...].astype(F32) + inverse * weighted_ref[...]
        msg_ref[...] = (grad - x_ref[0].astype(F32) * factor).astype(BF)


def backward_tick(tick, tab, blocks, weight, gain, stash, slopes, wait_for):
    def micro_of(tab):
        return tick - (LAST - tab[1])

    read = pl.BlockSpec(
        (1, ROWS, D), lambda i, tab: (jnp.clip(micro_of(tab), 0, N_MICRO - 1), 0, 0)
    )
    slot = pl.BlockSpec((1, ROWS, HALF), lambda i, tab: (slot_block(micro_of(tab)), 0, 0))
    leaving = tick in (LAST + 1, LAST + 3)
    hold = tick < N_MICRO
    names = [*blocks, "weight", "gain", "x", "mixed"]
    arrays = [array for array, _ in blocks.values()] + [weight, gain, *stash]
    specs = [pl.BlockSpec((ROWS, D), lambda i, tab, at=at: (at, 0)) for _, at in blocks.values()]
    specs += [whole((D, D)), whole((1, D)), read, read]
    aliases = {len(arrays) - 1: 3, len(arrays): 4} if hold else {}
    if slopes is not None:
        aliases |= {len(arrays) + 1: 1, len(arrays) + 2: 2}
        arrays += slopes
        names += ["old_0", "old_1"]
        specs += [whole((N_MICRO + 1, ROWS, HALF)) if leaving else ANY] * 2
    names += [None] * len(wait_for) + ["msg", "slope_0", "slope_1"] + [None] * (2 * hold)
    names += ["leave_0", "leave_1"] if leaving else []
    leave = (2, ROWS, HALF)
    kept = jax.ShapeDtypeStruct((N_MICRO + 1, ROWS, HALF), BF)
    out = pl.pallas_call(
        functools.partial(backward_kernel, tick, names),
        grid_spec=pltpu.PrefetchScalarGridSpec(
            num_scalar_prefetch=1,
            grid=(1,),
            in_specs=specs + [ANY] * len(wait_for),
            out_specs=[WHOLE, slot, slot] + [ANY] * (2 * hold) + [whole(leave)] * (2 * leaving),
            scratch_shapes=[pltpu.VMEM((ROWS, D), BF)] * 2 + [pltpu.VMEM((ROWS, D), F32)],
        ),
        out_shape=[jax.ShapeDtypeStruct((ROWS, D), BF), kept, kept]
        + [jax.ShapeDtypeStruct(s.shape, s.dtype) for s in stash if hold]
        + [jax.ShapeDtypeStruct(leave, BF)] * (2 * leaving),
        input_output_aliases=aliases,
        compiler_params=PARAMS,
        cost_estimate=COST,
        name=f"backward_{tick}",
    )(tab, *arrays, *wait_for)
    return out[0], out[3:5] if hold else stash, out[1:3], out[3:] if leaving else []


def hand_on(array, wait_for):
    def kernel(*refs):
        pass

    return pl.pallas_call(
        kernel,
        in_specs=[ANY] * (1 + len(wait_for)),
        out_specs=ANY,
        out_shape=jax.ShapeDtypeStruct(array.shape, array.dtype),
        input_output_aliases={0: 0},
        compiler_params=PARAMS,
        name="hand_on",
    )(array, *wait_for)


def join(pieces):
    def kernel(*refs):
        for i, piece in enumerate(refs[:-1]):
            refs[-1][i] = piece[...]

    return pl.pallas_call(
        kernel,
        grid=(1,),
        in_specs=[pl.BlockSpec((ROWS, D), lambda i: (0, 0))] * len(pieces),
        out_specs=pl.BlockSpec((len(pieces), ROWS, D), lambda i: (0, 0, 0)),
        out_shape=jax.ShapeDtypeStruct((len(pieces), ROWS, D), BF),
        compiler_params=PARAMS,
        name="join",
    )(*pieces)


def body(embedded, out_grad, stored, sample_ids, lengths, weight, gain):
    section = lax.axis_index("section")
    data = lax.axis_index("dp")
    y, a = section // 2, section % 2
    xh, c = data // 16, data % 2
    z = (data // 2) % N_Z
    place = jnp.stack([xh, a, c, z])
    table = jnp.stack([2 * y + c, 3 * y + c, c, a])
    stored = stored.reshape(24, 2, QTR, D)

    first_other = send(embedded, CORES)
    gain_row = jnp.where(a == c, gain, send(gain, TURN))

    limits = jnp.where(a == c, lengths, send(lengths, CORES))
    late_table = jnp.concatenate([table, limits])
    held = held_rows(sample_ids, stored)
    full = gather_weight(place, weight[0], [held], [late_table, gain_row, first_other])
    held_other = send(held, TURN)
    given_other = send(out_grad, CORES)

    stash = slopes = None
    normed, leaving, finals = [], [], []
    up_core, up_chip, down_core, down_chip = {}, {}, {}, {}
    for tick in range(LAST + TICKS):
        if tick < TICKS:
            blocks = {}
            if tick < N_MICRO:
                blocks["first"] = (embedded, tick)
                blocks["first_other"] = (first_other, tick)
            if tick in up_core:
                blocks["core"] = (up_core[tick], 0)
            if tick in up_chip:
                blocks["chip"] = (up_chip[tick], 0)
            if tick >= LAST:
                blocks["held"] = (held, tick - LAST)
                blocks["held_other"] = (held_other, tick - LAST)
            msg, *stash = forward_tick(
                tick,
                late_table if tick >= LAST else table,
                blocks,
                full,
                gain_row,
                stash,
                [held_other, given_other] if tick == LAST - 1 else [],
            )
            if tick >= LAST:
                finals.append(msg)
            if tick < TICKS - 1:
                up_core[tick + 1] = send(msg, UP_CORE)
            if 1 <= tick <= LAST:
                up_chip[tick + 2] = send(msg, UP_CHIP)
            if tick == TICKS - 1:
                normed = [stash[2], send(stash[2], FIRST), send(stash[2], SECOND)]
        if tick >= LAST:
            step = tick - LAST
            blocks = {}
            if step < N_MICRO:
                blocks["given"] = (out_grad, step)
                blocks["given_other"] = (given_other, step)
            if step in down_core:
                blocks["core"] = (down_core[step], 0)
            if step in down_chip:
                blocks["chip"] = (down_chip[step], 0)
            msg, stash[:2], slopes, halves = backward_tick(
                step,
                late_table if step < N_MICRO else table,
                blocks,
                full,
                gain_row,
                stash[:2],
                slopes,
                normed[1:] if step == 8 else list(leaving[0][1:]) if step == LAST + 3 else [],
            )
            if step < TICKS - 1:
                down_core[step + 1] = send(msg, DOWN_CORE)
            if 1 <= step <= LAST:
                down_chip[step + 2] = send(msg, DOWN_CHIP)
            if halves:
                leaving.append((halves[1], send(halves[0], FIRST), send(halves[1], SECOND)))
            if step == LAST:
                normed = [normed[1], jnp.where(a == c, normed[0], normed[2])]

    slopes_there = [*leaving[1][1:], *leaving[0][1:]]
    following = send(hand_on(stash[0], slopes_there), TO_BEFORE)
    finals = join(finals)
    finals_other = send(finals, TURN_LAST)
    last = section == N_SEC - 1
    slopes_of = [(came, jnp.where(a == c, own, second)) for own, came, second in leaving]
    flags = jnp.stack([last, jnp.where(last, jnp.where(a == c, 1, 2), 0)]).astype(jnp.int32)
    boundary = boundary_rows(sample_ids, jnp.concatenate([lengths, flags]), [following, finals, finals_other], stored)
    shard = scatter_grad(place, list(zip(normed, *slopes_of)), c, boundary)
    return (boundary, shard[None])


def solution(mesh):
    in_specs = (
        P("dp", None),
        P("dp", None),
        P("section", None, "dp", None, None),
        P("dp"),
        P("dp"),
        P("section", "dp", None),
        P("section", None),
    )
    out_specs = (P("section", "dp", None), P("section", "dp", None))
    return jax.shard_map(body, mesh=mesh, in_specs=in_specs, out_specs=out_specs, check_vma=False)
```

```python
import functools

import jax
import jax.numpy as jnp
from jax import lax
from jax.experimental import pallas as pl
from jax.experimental.pallas import tpu as pltpu
from jax.sharding import PartitionSpec as P

D = 2048
QTR = 32
N_MICRO = 4
ROWS = 128
N_SEC = 8
N_Z = 8
LAST = 10
TICKS = LAST + N_MICRO
EPS = 1e-6
BF = jnp.bfloat16
F32 = jnp.float32
BOTH = ("section", "dp")


def device(y, a, xh, z, c):
    return (2 * y + a) * 32 + 16 * xh + 2 * z + c


def pairs_of(target):
    out = []
    for y in range(4):
        for a in range(2):
            for xh in range(2):
                for z in range(N_Z):
                    for c in range(2):
                        to = target(y, a, xh, z, c)
                        if to is not None:
                            out.append((device(y, a, xh, z, c), device(*to)))
    return out


TURN = pairs_of(lambda y, a, xh, z, c: (y, c, xh, z, a) if a != c else None)
TO_BEFORE = pairs_of(
    lambda y, a, xh, z, c: (y, 0, xh, z, a) if c == 1 else (y - 1, 1, xh, z, a) if y > 0 else None
)
TURN_LAST = pairs_of(lambda y, a, xh, z, c: (y, 1, xh, z, a) if y == 3 and c == 1 and a == 0 else None)
CORES = pairs_of(lambda y, a, xh, z, c: (y, a, xh, z, 1 - c))
RIGHT = pairs_of(lambda y, a, xh, z, c: (y, a, xh, (z + 1) % N_Z, c))
LEFT = pairs_of(lambda y, a, xh, z, c: (y, a, xh, (z - 1) % N_Z, c))
UP_CORE = pairs_of(lambda y, a, xh, z, c: (y, a, xh, z, 1) if c == 0 else None)
UP_CHIP = pairs_of(lambda y, a, xh, z, c: (y + 1, a, xh, z, 0) if c == 1 and y < 3 else None)
DOWN_CORE = pairs_of(lambda y, a, xh, z, c: (y, a, xh, z, 0) if c == 1 else None)
DOWN_CHIP = pairs_of(lambda y, a, xh, z, c: (y - 1, a, xh, z, 1) if c == 0 and y > 0 else None)
FAR_X = pairs_of(lambda y, a, xh, z, c: (y, a, 1 - xh, z, c))
FAR_X_CORE = pairs_of(lambda y, a, xh, z, c: (y, a, 1 - xh, z, 1 - c))


def beside(y, a, xh, z, step, core):
    x = (2 * xh + a + step) % 4
    return (y, x % 2, x // 2, z, core)


TO_NEXT = pairs_of(
    lambda y, a, xh, z, c: beside(y, a, xh, z, 1, a) if c == 0 else (y, a, xh, z, 0) if a == 0 else None
)
TO_PREVIOUS = pairs_of(
    lambda y, a, xh, z, c: beside(y, a, xh, z, -1, a) if c == 1 else (y, a, xh, z, 1) if a == 1 else None
)

FIRST = pairs_of(
    lambda y, a, xh, z, c: (y, a, xh, z, 1 - a)
    if c == a
    else beside(y, a, xh, z, -1, 0)
    if a == 1
    else beside(y, a, xh, z, 1, 1)
)
SECOND = pairs_of(
    lambda y, a, xh, z, c: None
    if c == a
    else beside(y, a, xh, z, 1, 1)
    if a == 1
    else beside(y, a, xh, z, -1, 0)
)

CHUNK = 256
HALF = 1024
QUARTER = 512


def send(array, pairs):
    return lax.ppermute(array, BOTH, pairs)


ANY = pl.BlockSpec(memory_space=pl.ANY)
WHOLE = pl.BlockSpec((ROWS, D), lambda i, tab: (0, 0))
COST = pl.CostEstimate(flops=2**20, bytes_accessed=2**18, transcendentals=0)
PARAMS = pltpu.CompilerParams(vmem_limit_bytes=12 * 2**20)


def whole(shape):
    return pl.BlockSpec(shape, lambda i, place: (0,) * len(shape))


def placed(kernel, name, place, arrays, outs, wait_for=()):
    return pl.pallas_call(
        kernel,
        grid_spec=pltpu.PrefetchScalarGridSpec(
            num_scalar_prefetch=1,
            grid=(1,),
            in_specs=[whole(r.shape) for r in arrays] + [ANY] * len(wait_for),
            out_specs=[whole(shape) for shape, _ in outs],
        ),
        out_shape=[jax.ShapeDtypeStruct(shape, dtype) for shape, dtype in outs],
        compiler_params=PARAMS,
        name=name,
    )(place, *arrays, *wait_for)


def half_columns(index):
    return pl.ds(pl.multiple_of(index * HALF, HALF), HALF)


def part_rows(index, rows):
    return pl.ds(pl.multiple_of(index * rows, rows), rows)


def divide_kernel(place, shard, mine, other):
    mine[...] = shard[:, half_columns(place[2])]
    other[...] = shard[:, half_columns(1 - place[2])]


def arrange_kernel(place, p00, p01, p10, p11, out):
    for dx, dt, part in ((0, 0, p00), (0, 1, p01), (1, 0, p10), (1, 1, p11)):
        out[part_rows((place[0] ^ dx) * 2 + (place[2] ^ dt), 64), :] = part[...]


def pack(pieces, full, wait_for):
    rows = sum(piece.shape[0] for piece in pieces)
    passed = pieces + ([] if full is None else [full])

    def kernel(*refs):
        out, at = refs[len(passed) + len(wait_for)], 0
        for piece in refs[: len(pieces)]:
            out[at : at + piece.shape[0], :] = piece[...]
            at += piece.shape[0]

    return pl.pallas_call(
        kernel,
        grid=(1,),
        in_specs=[pl.BlockSpec(p.shape, lambda i: (0, 0)) for p in pieces]
        + [ANY] * (len(passed) - len(pieces) + len(wait_for)),
        out_specs=[pl.BlockSpec((rows, HALF), lambda i: (0, 0))] + [ANY] * len(passed),
        out_shape=[jax.ShapeDtypeStruct((rows, HALF), BF)]
        + [jax.ShapeDtypeStruct(p.shape, BF) for p in passed],
        input_output_aliases={i: 1 + i for i in range(len(passed))},
        compiler_params=PARAMS,
        name="pack",
    )(*passed, *wait_for)


def place_chunk(place, k, full, own, following, previous, at, wait_for):
    count = len(own)
    skip = 0 if full is None else 1

    def kernel(place, *refs):
        pieces, arrived, out = refs[:count], refs[count : count + 2], refs[count + 2 + skip + len(wait_for)]
        same = place[1] == place[2]
        for c in range(2):

            @pl.when(same & (place[2] == c))
            def _():
                row = 0
                for piece in pieces:
                    for at in range(0, piece.shape[0], 128):
                        out[(row + at) // 128, :, c * HALF : (c + 1) * HALF] = piece[at : at + 128, :]
                    row += piece.shape[0]
                for xh in range(2):
                    rows = slice(xh * 128, xh * 128 + 128)
                    out[xh, :, (1 - c) * HALF : (2 - c) * HALF] = arrived[c][rows, :]

        @pl.when(jnp.logical_not(same))
        def _():
            for c in range(2):
                for xh in range(2):
                    rows = slice(xh * 128, xh * 128 + 128)
                    out[xh, :, c * HALF : (c + 1) * HALF] = arrived[c][rows, :]

    block = pl.BlockSpec((CHUNK, HALF), lambda i, place: (at, 0))
    old = [] if full is None else [full]
    return pl.pallas_call(
        kernel,
        grid_spec=pltpu.PrefetchScalarGridSpec(
            num_scalar_prefetch=1,
            grid=(1,),
            in_specs=[whole(p.shape) for p in own] + [block] * 2 + [ANY] * (skip + len(wait_for)),
            out_specs=pl.BlockSpec(
                (2, 128, D), lambda i, place: (0, lax.rem(place[3] + k, N_Z), 0)
            ),
        ),
        out_shape=jax.ShapeDtypeStruct((2, HALF, D), BF),
        input_output_aliases={} if full is None else {count + 3: 0},
        compiler_params=PARAMS,
        name=f"place_{k}",
    )(place, *own, following, previous, *old, *wait_for)


def gather_weight(place, shard, early, ready):
    quarter, chunk = ((64, HALF), BF), ((CHUNK, HALF), BF)
    mine, other = placed(divide_kernel, "divide", place, [shard], [quarter, quarter])
    parts = [mine, send(other, CORES), send(mine, FAR_X), send(other, FAR_X_CORE)]
    first = placed(arrange_kernel, "arrange", place, parts, [chunk])[0]
    right, left, rows = first, first, first
    order = [(0, 0)]
    own = {0: [first]}
    full, before = None, early[:1]
    for step in range(1, 6):
        if step < 4:
            right, left = send(right, RIGHT), send(left, LEFT)
        elif step == 4:
            right, left = send(right[:128], RIGHT), send(left[128:], LEFT)
        moved = [send(rows, TO_NEXT), send(rows, TO_PREVIOUS)]
        if step < 5:
            rows, right, left, *through = pack([right, left], full, before)
            full = through[0] if through else None
        before = moved + early[step : step + 1]
        for k, at in order:
            full = place_chunk(place, k, full, own[k], *moved, at, ready if k == 4 else [])
        order = [(-step % N_Z, 0), (step, 1)] if step < 4 else [(4, 0)]
        if step < 4:
            own[-step % N_Z], own[step] = [right], [left]
        else:
            own[4] = [right, left]
    return full.reshape(D, D)


def sample_of(group):
    early = group < 8
    return jnp.where(early, group // 2, group - 4), jnp.where(early, lax.rem(group, 2), 0)


def held_block(side):
    def index(group, ids, *rest):
        sample, half = sample_of(group)
        return (side * 12 + ids[sample], half, 0, 0)

    return pl.BlockSpec((1, 1, QTR, D), index)


def held_rows(ids, stored):
    def kernel(ids, held_ref, out_ref):
        out_ref[...] = held_ref[0, 0]

    return pl.pallas_call(
        kernel,
        grid_spec=pltpu.PrefetchScalarGridSpec(
            num_scalar_prefetch=1,
            grid=(16,),
            in_specs=[held_block(0)],
            out_specs=pl.BlockSpec((QTR, D), lambda g, ids: (g, 0)),
        ),
        out_shape=jax.ShapeDtypeStruct((N_MICRO * ROWS, D), BF),
        compiler_params=PARAMS,
        name="held_rows",
    )(ids, stored)


def boundary_rows(ids, limits, sources, stored):
    def held_at(quarter):
        def index(micro, ids, limits):
            sample, half = sample_of(micro * 4 + quarter)
            return (12 + ids[sample], half, 0, 0)

        return pl.BlockSpec((1, 1, QTR, D), index)

    def source_at(which):
        def index(micro, ids, limits):
            return (jnp.where(limits[13] == which, micro, 0), 0, 0)

        return pl.BlockSpec((1, ROWS, D), index)

    def kernel(ids, limits, s0, s1, s2, h0, h1, h2, h3, out_ref):
        for quarter, held_ref in enumerate((h0, h1, h2, h3)):
            sample, half = sample_of(pl.program_id(0) * 4 + quarter)
            row = lax.broadcasted_iota(jnp.int32, (QTR, 1), 0) + half * QTR
            live = (row < limits[sample]) | (limits[12] == 1)
            rows = slice(quarter * QTR, (quarter + 1) * QTR)
            held = held_ref[0, 0].astype(F32)

            for which, source in enumerate((s0, s1, s2)):

                @pl.when(limits[13] == which)
                def _():
                    value = source[0, rows, :].astype(F32)
                    out_ref[0, rows, :] = jnp.where(live, value, held).astype(BF)

    return pl.pallas_call(
        kernel,
        grid_spec=pltpu.PrefetchScalarGridSpec(
            num_scalar_prefetch=2,
            grid=(N_MICRO,),
            in_specs=[source_at(which) for which in range(3)]
            + [held_at(quarter) for quarter in range(4)],
            out_specs=pl.BlockSpec((1, ROWS, D), lambda m, *tables: (0, m, 0)),
        ),
        out_shape=jax.ShapeDtypeStruct((1, N_MICRO * ROWS, D), BF),
        compiler_params=PARAMS,
        name="boundary_rows",
    )(ids, limits, *sources, stored, stored, stored, stored)


def product_kernel(has, place, *refs):
    rows = N_MICRO * ROWS
    out = refs[-1]

    total = jnp.zeros((CHUNK, QUARTER), F32)
    for source in range(2):
        low, high, early, late = refs[4 * source : 4 * source + 4]
        normed = jnp.concatenate(
            [low[...].reshape(rows, 128), high[...].reshape(rows, 128)], axis=1
        )
        slope = jnp.concatenate(
            [early[...].reshape(rows // 2, QUARTER), late[...].reshape(rows // 2, QUARTER)], axis=0
        )
        total = total + lax.dot_general(
            normed, slope, (((0,), (0,)), ((), ())), preferred_element_type=F32
        )
    for ref in refs[8 : 8 + has]:
        total = total + ref[...].astype(F32)
    out[...] = total.astype(BF)


def product(place, sums, k, part, arrived, wait_for=()):
    piece = pl.BlockSpec((CHUNK, QUARTER), lambda i, place: (0, 0))

    def columns(xh):
        return pl.BlockSpec(
            (N_MICRO, ROWS, 128), lambda i, place: (0, 0, xh * N_Z + lax.rem(place[3] + k, N_Z))
        )

    specs, arrays = [], []
    for normed, early, late in sums:
        specs += [columns(0), columns(1)]
        specs += [pl.BlockSpec((2, ROWS, QUARTER), lambda i, place: (0, 0, part))] * 2
        arrays += [normed, normed, early, late]
    return pl.pallas_call(
        functools.partial(product_kernel, len(arrived)),
        grid_spec=pltpu.PrefetchScalarGridSpec(
            num_scalar_prefetch=1,
            grid=(1,),
            in_specs=specs + [piece] * len(arrived) + [ANY] * len(wait_for),
            out_specs=piece,
        ),
        out_shape=jax.ShapeDtypeStruct((CHUNK, QUARTER), BF),
        compiler_params=PARAMS,
        cost_estimate=COST,
        name=f"product_{k}_{part}",
    )(place, *arrays, *arrived, *wait_for)


def split_x_kernel(place, q0, q1, mine, other):
    for out, xh in ((mine, place[0]), (other, 1 - place[0])):
        rows = part_rows(xh, 128)
        out[:, :QUARTER] = q0[rows, :]
        out[:, QUARTER:] = q1[rows, :]


def split_core_kernel(place, mine, arrived, _, own, other, total):
    total[...] = mine[...].astype(F32) + arrived[...].astype(F32)
    own[...] = total[part_rows(place[2], 64), :]
    other[...] = total[part_rows(1 - place[2], 64), :].astype(BF)


def scatter_grad(place, sums, core, wait_for):
    to_right = [send(product(place, sums, 4, 0, []), RIGHT), None]
    to_left = [None, send(product(place, sums, 4, 1, []), LEFT)]
    for step in range(3, 0, -1):
        for part in (1, 0):
            held = to_right[part]
            to_right[part] = send(
                product(place, sums, step, part, [] if held is None else [held]), RIGHT
            )
            held = to_left[1 - part]
            to_left[1 - part] = send(
                product(place, sums, N_Z - step, 1 - part, [] if held is None else [held]), LEFT
            )
    quarters = [
        product(place, sums, 0, part, [to_right[part], to_left[part]]) for part in range(2)
    ]
    block = ((128, HALF), BF)
    mine, other = placed(split_x_kernel, "split_x", place, quarters, [block, block])
    arrived = send(other, FAR_X)
    own, other, _ = placed(
        split_core_kernel, "split_core", place, [mine, arrived],
        [((64, HALF), F32), ((64, HALF), BF), ((128, HALF), F32)], [wait_for],
    )
    arrived = send(other, CORES).astype(F32)
    return jnp.where(
        core == 0,
        jnp.concatenate([own, arrived], axis=1),
        jnp.concatenate([arrived, own], axis=1),
    )


def live_mask(tab, micro):
    row = lax.broadcasted_iota(jnp.int32, (ROWS, 1), 0)
    if micro < 2:
        limit = jnp.where(row < 64, tab[4 + 2 * micro], tab[5 + 2 * micro])
        return row % 64 < limit
    limit = jnp.zeros((ROWS, 1), jnp.int32)
    for q in range(4):
        limit = jnp.where(row // QTR == q, tab[4 * micro + q], limit)
    return row % QTR < limit


def slot_block(micro):
    return jnp.where((micro >= 0) & (micro < N_MICRO), micro, N_MICRO)


def forward_kernel(tick, names, tab, *refs):
    ref = dict(zip(names, refs))
    micro = tick - tab[1]
    block = tab[0]
    active = (micro >= 0) & (micro < N_MICRO)
    x_ref, normed_ref = ref["x"], ref["normed"]

    if "first" in ref:

        for a, name in ((0, "first"), (1, "first_other")):

            @pl.when(active & (block == 0) & (tab[3] == a))
            def _():
                x_ref[0] = ref[name][...]

    if "core" in ref:

        @pl.when(active & (block % 2 == 1))
        def _():
            x_ref[0] = ref["core"][...]

    if "chip" in ref:

        @pl.when(active & (block % 2 == 0) & (block > 0))
        def _():
            x_ref[0] = ref["chip"][...]

    if "held" in ref:

        for name, mine in (("held", True), ("held_other", False)):

            @pl.when((block == N_SEC - 1) & ((tab[2] == tab[3]) == mine))
            def _():
                live = live_mask(tab, tick - LAST)
                x = jnp.where(live, x_ref[0].astype(F32), ref[name][...].astype(F32))
                x_ref[0] = x.astype(BF)

    @pl.when(active)
    def _():
        values = x_ref[0].astype(F32)
        inverse = lax.rsqrt(jnp.mean(values * values, axis=1, keepdims=True) + EPS)
        normed_ref[0] = (values * inverse * ref["gain"][...].astype(F32)).astype(BF)
        for at in range(0, D, QUARTER):
            cols = slice(at, at + QUARTER)
            mixed = jnp.dot(normed_ref[0], ref["weight"][:, cols], preferred_element_type=F32)
            ref["mixed"][0, :, cols] = mixed.astype(BF)
            output = (x_ref[0, :, cols].astype(F32) + mixed / (1.0 + jnp.exp(-mixed))).astype(BF)
            ref["msg"][:, cols] = output


STASH = {"x": BF, "mixed": BF, "normed": BF}


def forward_tick(tick, tab, blocks, weight, gain, stash, wait_for):
    slot = pl.BlockSpec((1, ROWS, D), lambda i, tab: (slot_block(tick - tab[1]), 0, 0))
    names = [*blocks, "weight", "gain"]
    arrays = [array for array, _ in blocks.values()] + [weight, gain]
    specs = [pl.BlockSpec((ROWS, D), lambda i, tab, at=at: (at, 0)) for _, at in blocks.values()]
    specs += [whole((D, D)), whole((1, D))]
    old = [] if stash is None else list(stash)
    aliases = {1 + len(arrays) + i: 1 + i for i in range(len(old))}
    names += [None] * (len(old) + len(wait_for)) + ["msg", *STASH]
    return pl.pallas_call(
        functools.partial(forward_kernel, tick, names),
        grid_spec=pltpu.PrefetchScalarGridSpec(
            num_scalar_prefetch=1,
            grid=(1,),
            in_specs=specs + [ANY] * (len(old) + len(wait_for)),
            out_specs=[WHOLE] + [slot] * 3,
        ),
        out_shape=[jax.ShapeDtypeStruct((ROWS, D), BF)]
        + [jax.ShapeDtypeStruct((N_MICRO + 1, ROWS, D), kind) for kind in STASH.values()],
        input_output_aliases=aliases,
        compiler_params=PARAMS,
        cost_estimate=COST,
        name=f"forward_{tick}",
    )(tab, *arrays, *old, *wait_for)


def backward_kernel(tick, names, tab, *refs):
    ref = dict(zip(names, refs))
    up_ref, slope_ref, weighted_ref = refs[-3:]
    x_ref, msg_ref = ref["x"], ref["msg"]
    micro = tick - (LAST - tab[1])
    block = tab[0]
    active = (micro >= 0) & (micro < N_MICRO)

    if "given" in ref:
        for a, name in ((1, "given"), (0, "given_other")):

            @pl.when(active & (block == N_SEC - 1) & (tab[3] == a))
            def _():
                given = ref[name][...].astype(F32)
                up_ref[...] = jnp.where(live_mask(tab, tick), given, 0.0).astype(BF)

    if "core" in ref:

        @pl.when(active & (block % 2 == 0))
        def _():
            up_ref[...] = ref["core"][...]

    if "chip" in ref:

        @pl.when(active & (block % 2 == 1) & (block < N_SEC - 1))
        def _():
            up_ref[...] = ref["chip"][...]

    @pl.when(active)
    def _():
        mixed = ref["mixed"][0].astype(F32)
        gated = 1.0 / (1.0 + jnp.exp(-mixed))
        up = up_ref[...].astype(F32)
        slope_ref[...] = (up * gated * (1.0 + mixed * (1.0 - gated))).astype(BF)
        for j, name in enumerate(("slope_0", "slope_1")):
            ref[name][0] = slope_ref[:, half_columns(tab[3] ^ (1 - j))]

    if tick in (LAST + 1, LAST + 3):
        for j in "01":
            leave, old = ref["leave_" + j], ref["old_" + j]
            leave[0] = old[tick - LAST - 1]

            @pl.when(block == 0)
            def _():
                leave[1] = ref["slope_" + j][0]

            @pl.when(block != 0)
            def _():
                leave[1] = old[tick - LAST]

    @pl.when(active & (block > 0))
    def _():
        values = x_ref[0].astype(F32)
        inverse = lax.rsqrt(jnp.mean(values * values, axis=1, keepdims=True) + EPS)
        total = jnp.zeros((ROWS, 128), F32)
        for at in range(0, D, QUARTER):
            cols = slice(at, at + QUARTER)
            back = lax.dot_general(
                slope_ref[...],
                ref["weight"][cols, :],
                (((1,), (1,)), ((), ())),
                preferred_element_type=F32,
            )
            weighted = back * ref["gain"][:, cols].astype(F32)
            weighted_ref[:, cols] = weighted
            terms = weighted * x_ref[0, :, cols].astype(F32)
            for part in range(0, QUARTER, 128):
                total = total + terms[:, part : part + 128]
        centre = jnp.sum(total, axis=1, keepdims=True) * (1.0 / D)
        factor = inverse * inverse * inverse * centre
        grad = up_ref[...].astype(F32) + inverse * weighted_ref[...]
        msg_ref[...] = (grad - x_ref[0].astype(F32) * factor).astype(BF)


def backward_tick(tick, tab, blocks, weight, gain, stash, slopes, wait_for):
    def micro_of(tab):
        return tick - (LAST - tab[1])

    read = pl.BlockSpec(
        (1, ROWS, D), lambda i, tab: (jnp.clip(micro_of(tab), 0, N_MICRO - 1), 0, 0)
    )
    slot = pl.BlockSpec((1, ROWS, HALF), lambda i, tab: (slot_block(micro_of(tab)), 0, 0))
    leaving = tick in (LAST + 1, LAST + 3)
    hold = tick < N_MICRO
    names = [*blocks, "weight", "gain", "x", "mixed"]
    arrays = [array for array, _ in blocks.values()] + [weight, gain, *stash]
    specs = [pl.BlockSpec((ROWS, D), lambda i, tab, at=at: (at, 0)) for _, at in blocks.values()]
    specs += [whole((D, D)), whole((1, D)), read, read]
    aliases = {len(arrays) - 1: 3, len(arrays): 4} if hold else {}
    if slopes is not None:
        aliases |= {len(arrays) + 1: 1, len(arrays) + 2: 2}
        arrays += slopes
        names += ["old_0", "old_1"]
        specs += [whole((N_MICRO + 1, ROWS, HALF)) if leaving else ANY] * 2
    names += [None] * len(wait_for) + ["msg", "slope_0", "slope_1"] + [None] * (2 * hold)
    names += ["leave_0", "leave_1"] if leaving else []
    leave = (2, ROWS, HALF)
    kept = jax.ShapeDtypeStruct((N_MICRO + 1, ROWS, HALF), BF)
    out = pl.pallas_call(
        functools.partial(backward_kernel, tick, names),
        grid_spec=pltpu.PrefetchScalarGridSpec(
            num_scalar_prefetch=1,
            grid=(1,),
            in_specs=specs + [ANY] * len(wait_for),
            out_specs=[WHOLE, slot, slot] + [ANY] * (2 * hold) + [whole(leave)] * (2 * leaving),
            scratch_shapes=[pltpu.VMEM((ROWS, D), BF)] * 2 + [pltpu.VMEM((ROWS, D), F32)],
        ),
        out_shape=[jax.ShapeDtypeStruct((ROWS, D), BF), kept, kept]
        + [jax.ShapeDtypeStruct(s.shape, s.dtype) for s in stash if hold]
        + [jax.ShapeDtypeStruct(leave, BF)] * (2 * leaving),
        input_output_aliases=aliases,
        compiler_params=PARAMS,
        cost_estimate=COST,
        name=f"backward_{tick}",
    )(tab, *arrays, *wait_for)
    return out[0], out[3:5] if hold else stash, out[1:3], out[3:] if leaving else []


def hand_on(array, wait_for):
    def kernel(*refs):
        pass

    return pl.pallas_call(
        kernel,
        in_specs=[ANY] * (1 + len(wait_for)),
        out_specs=ANY,
        out_shape=jax.ShapeDtypeStruct(array.shape, array.dtype),
        input_output_aliases={0: 0},
        compiler_params=PARAMS,
        name="hand_on",
    )(array, *wait_for)


def join(pieces):
    def kernel(*refs):
        for i, piece in enumerate(refs[:-1]):
            refs[-1][i] = piece[...]

    return pl.pallas_call(
        kernel,
        grid=(1,),
        in_specs=[pl.BlockSpec((ROWS, D), lambda i: (0, 0))] * len(pieces),
        out_specs=pl.BlockSpec((len(pieces), ROWS, D), lambda i: (0, 0, 0)),
        out_shape=jax.ShapeDtypeStruct((len(pieces), ROWS, D), BF),
        compiler_params=PARAMS,
        name="join",
    )(*pieces)


def body(embedded, out_grad, stored, sample_ids, lengths, weight, gain):
    section = lax.axis_index("section")
    data = lax.axis_index("dp")
    y, a = section // 2, section % 2
    xh, c = data // 16, data % 2
    z = (data // 2) % N_Z
    place = jnp.stack([xh, a, c, z])
    table = jnp.stack([2 * y + c, 3 * y + c, c, a])
    stored = stored.reshape(24, 2, QTR, D)

    first_other = send(embedded, CORES)
    gain_row = jnp.where(a == c, gain, send(gain, TURN))

    limits = jnp.where(a == c, lengths, send(lengths, CORES))
    late_table = jnp.concatenate([table, limits])
    held = held_rows(sample_ids, stored)
    full = gather_weight(place, weight[0], [held], [late_table, gain_row, first_other])
    held_other = send(held, TURN)
    given_other = send(out_grad, CORES)

    stash = slopes = None
    normed, terms, slopes_there, finals = [], [], [], []
    up_core, up_chip, down_core, down_chip = {}, {}, {}, {}
    for tick in range(LAST + TICKS):
        if tick < TICKS:
            blocks = {}
            if tick < N_MICRO:
                blocks["first"] = (embedded, tick)
                blocks["first_other"] = (first_other, tick)
            if tick in up_core:
                blocks["core"] = (up_core[tick], 0)
            if tick in up_chip:
                blocks["chip"] = (up_chip[tick], 0)
            if tick >= LAST:
                blocks["held"] = (held, tick - LAST)
                blocks["held_other"] = (held_other, tick - LAST)
            msg, *stash = forward_tick(
                tick,
                late_table if tick >= LAST else table,
                blocks,
                full,
                gain_row,
                stash,
                [held_other, given_other] if tick == LAST - 1 else [],
            )
            if tick >= LAST:
                finals.append(msg)
            if tick < TICKS - 1:
                up_core[tick + 1] = send(msg, UP_CORE)
            if 1 <= tick <= LAST:
                up_chip[tick + 2] = send(msg, UP_CHIP)
            if tick == TICKS - 1:
                normed = [stash[2], send(stash[2], FIRST), send(stash[2], SECOND)]
        if tick >= LAST:
            step = tick - LAST
            blocks = {}
            if step < N_MICRO:
                blocks["given"] = (out_grad, step)
                blocks["given_other"] = (given_other, step)
            if step in down_core:
                blocks["core"] = (down_core[step], 0)
            if step in down_chip:
                blocks["chip"] = (down_chip[step], 0)
            msg, stash[:2], slopes, halves = backward_tick(
                step,
                late_table if step < N_MICRO else table,
                blocks,
                full,
                gain_row,
                stash[:2],
                slopes,
                normed[1:] if step == 8 else [*terms[0], normed[1]] if step == LAST + 3 else [],
            )
            if step < TICKS - 1:
                down_core[step + 1] = send(msg, DOWN_CORE)
            if 1 <= step <= LAST:
                down_chip[step + 2] = send(msg, DOWN_CHIP)
            if halves:
                came, second = send(halves[0], FIRST), send(halves[1], SECOND)
                slopes_there += [came, second]
                terms.append((came, jnp.where(a == c, halves[1], second)))
            if step == LAST:
                normed = [normed[1], jnp.where(a == c, normed[0], normed[2])]

    following = send(hand_on(stash[0], slopes_there), TO_BEFORE)
    finals = join(finals)
    finals_other = send(finals, TURN_LAST)
    last = section == N_SEC - 1
    flags = jnp.stack([last, jnp.where(last, jnp.where(a == c, 1, 2), 0)]).astype(jnp.int32)
    boundary = boundary_rows(sample_ids, jnp.concatenate([lengths, flags]), [following, finals, finals_other], stored)
    shard = scatter_grad(place, list(zip(normed, *terms)), c, boundary)
    return (boundary, shard[None])


def solution(mesh):
    in_specs = (
        P("dp", None),
        P("dp", None),
        P("section", None, "dp", None, None),
        P("dp"),
        P("dp"),
        P("section", "dp", None),
        P("section", None),
    )
    out_specs = (P("section", "dp", None), P("section", "dp", None))
    return jax.shard_map(body, mesh=mesh, in_specs=in_specs, out_specs=out_specs, check_vma=False)
```

```python
import functools

import jax
import jax.numpy as jnp
from jax import lax
from jax.experimental import pallas as pl
from jax.experimental.pallas import tpu as pltpu
from jax.sharding import PartitionSpec as P

D = 2048
QTR = 32
N_MICRO = 4
ROWS = 128
N_SEC = 8
N_Z = 8
LAST = 10
TICKS = LAST + N_MICRO
EPS = 1e-6
BF = jnp.bfloat16
F32 = jnp.float32
BOTH = ("section", "dp")


def device(y, a, xh, z, c):
    return (2 * y + a) * 32 + 16 * xh + 2 * z + c


def pairs_of(target):
    out = []
    for y in range(4):
        for a in range(2):
            for xh in range(2):
                for z in range(N_Z):
                    for c in range(2):
                        to = target(y, a, xh, z, c)
                        if to is not None:
                            out.append((device(y, a, xh, z, c), device(*to)))
    return out


TURN = pairs_of(lambda y, a, xh, z, c: (y, c, xh, z, a) if a != c else None)
TO_BEFORE = pairs_of(
    lambda y, a, xh, z, c: (y, 0, xh, z, a) if c == 1 else (y - 1, 1, xh, z, a) if y > 0 else None
)
TURN_LAST = pairs_of(lambda y, a, xh, z, c: (y, 1, xh, z, a) if y == 3 and c == 1 and a == 0 else None)
CORES = pairs_of(lambda y, a, xh, z, c: (y, a, xh, z, 1 - c))
RIGHT = pairs_of(lambda y, a, xh, z, c: (y, a, xh, (z + 1) % N_Z, c))
LEFT = pairs_of(lambda y, a, xh, z, c: (y, a, xh, (z - 1) % N_Z, c))
UP_CORE = pairs_of(lambda y, a, xh, z, c: (y, a, xh, z, 1) if c == 0 else None)
UP_CHIP = pairs_of(lambda y, a, xh, z, c: (y + 1, a, xh, z, 0) if c == 1 and y < 3 else None)
DOWN_CORE = pairs_of(lambda y, a, xh, z, c: (y, a, xh, z, 0) if c == 1 else None)
DOWN_CHIP = pairs_of(lambda y, a, xh, z, c: (y - 1, a, xh, z, 1) if c == 0 and y > 0 else None)
FAR_X = pairs_of(lambda y, a, xh, z, c: (y, a, 1 - xh, z, c))
FAR_X_CORE = pairs_of(lambda y, a, xh, z, c: (y, a, 1 - xh, z, 1 - c))


def beside(y, a, xh, z, step, core):
    x = (2 * xh + a + step) % 4
    return (y, x % 2, x // 2, z, core)


TO_NEXT = pairs_of(
    lambda y, a, xh, z, c: beside(y, a, xh, z, 1, a) if c == 0 else (y, a, xh, z, 0) if a == 0 else None
)
TO_PREVIOUS = pairs_of(
    lambda y, a, xh, z, c: beside(y, a, xh, z, -1, a) if c == 1 else (y, a, xh, z, 1) if a == 1 else None
)

FIRST = pairs_of(
    lambda y, a, xh, z, c: (y, a, xh, z, 1 - a)
    if c == a
    else beside(y, a, xh, z, -1, 0)
    if a == 1
    else beside(y, a, xh, z, 1, 1)
)
SECOND = pairs_of(
    lambda y, a, xh, z, c: None
    if c == a
    else beside(y, a, xh, z, 1, 1)
    if a == 1
    else beside(y, a, xh, z, -1, 0)
)

CHUNK = 256
HALF = 1024
QUARTER = 512


def send(array, pairs):
    return lax.ppermute(array, BOTH, pairs)


ANY = pl.BlockSpec(memory_space=pl.ANY)
WHOLE = pl.BlockSpec((ROWS, D), lambda i, tab: (0, 0))
COST = pl.CostEstimate(flops=2**20, bytes_accessed=2**18, transcendentals=0)
PARAMS = pltpu.CompilerParams(vmem_limit_bytes=12 * 2**20)


def whole(shape):
    return pl.BlockSpec(shape, lambda i, place: (0,) * len(shape))


def placed(kernel, name, place, arrays, outs, wait_for=()):
    return pl.pallas_call(
        kernel,
        grid_spec=pltpu.PrefetchScalarGridSpec(
            num_scalar_prefetch=1,
            grid=(1,),
            in_specs=[whole(r.shape) for r in arrays] + [ANY] * len(wait_for),
            out_specs=[whole(shape) for shape, _ in outs],
        ),
        out_shape=[jax.ShapeDtypeStruct(shape, dtype) for shape, dtype in outs],
        compiler_params=PARAMS,
        name=name,
    )(place, *arrays, *wait_for)


def half_columns(index):
    return pl.ds(pl.multiple_of(index * HALF, HALF), HALF)


def part_rows(index, rows):
    return pl.ds(pl.multiple_of(index * rows, rows), rows)


def divide_kernel(place, shard, mine, other):
    mine[...] = shard[:, half_columns(place[2])]
    other[...] = shard[:, half_columns(1 - place[2])]


def arrange_kernel(place, p00, p01, p10, p11, out):
    for dx, dt, part in ((0, 0, p00), (0, 1, p01), (1, 0, p10), (1, 1, p11)):
        out[part_rows((place[0] ^ dx) * 2 + (place[2] ^ dt), 64), :] = part[...]


def pack(pieces, wait_for):
    rows = sum(piece.shape[0] for piece in pieces)

    def kernel(*refs):
        out, at = refs[len(pieces) + len(wait_for)], 0
        for piece in refs[: len(pieces)]:
            out[at : at + piece.shape[0], :] = piece[...]
            at += piece.shape[0]

    return pl.pallas_call(
        kernel,
        grid=(1,),
        in_specs=[pl.BlockSpec(p.shape, lambda i: (0, 0)) for p in pieces] + [ANY] * len(wait_for),
        out_specs=[pl.BlockSpec((rows, HALF), lambda i: (0, 0))] + [ANY] * len(pieces),
        out_shape=[jax.ShapeDtypeStruct((rows, HALF), BF)]
        + [jax.ShapeDtypeStruct(p.shape, BF) for p in pieces],
        input_output_aliases={i: 1 + i for i in range(len(pieces))},
        compiler_params=PARAMS,
        name="pack",
    )(*pieces, *wait_for)


def place_chunk(place, k, full, own, following, previous, at, wait_for):
    count = len(own)
    skip = 0 if full is None else 1

    def kernel(place, *refs):
        pieces, arrived, out = refs[:count], refs[count : count + 2], refs[count + 2 + skip + len(wait_for)]
        same = place[1] == place[2]
        for c in range(2):

            @pl.when(same & (place[2] == c))
            def _():
                row = 0
                for piece in pieces:
                    for at in range(0, piece.shape[0], 128):
                        out[(row + at) // 128, :, c * HALF : (c + 1) * HALF] = piece[at : at + 128, :]
                    row += piece.shape[0]
                for xh in range(2):
                    rows = slice(xh * 128, xh * 128 + 128)
                    out[xh, :, (1 - c) * HALF : (2 - c) * HALF] = arrived[c][rows, :]

        @pl.when(jnp.logical_not(same))
        def _():
            for c in range(2):
                for xh in range(2):
                    rows = slice(xh * 128, xh * 128 + 128)
                    out[xh, :, c * HALF : (c + 1) * HALF] = arrived[c][rows, :]

    block = pl.BlockSpec((CHUNK, HALF), lambda i, place: (at, 0))
    old = [] if full is None else [full]
    return pl.pallas_call(
        kernel,
        grid_spec=pltpu.PrefetchScalarGridSpec(
            num_scalar_prefetch=1,
            grid=(1,),
            in_specs=[whole(p.shape) for p in own] + [block] * 2 + [ANY] * (skip + len(wait_for)),
            out_specs=pl.BlockSpec(
                (2, 128, D), lambda i, place: (0, lax.rem(place[3] + k, N_Z), 0)
            ),
        ),
        out_shape=jax.ShapeDtypeStruct((2, HALF, D), BF),
        input_output_aliases={} if full is None else {count + 3: 0},
        compiler_params=PARAMS,
        name=f"place_{k}",
    )(place, *own, following, previous, *old, *wait_for)


def gather_weight(place, shard, early, ready):
    quarter, chunk = ((64, HALF), BF), ((CHUNK, HALF), BF)
    mine, other = placed(divide_kernel, "divide", place, [shard], [quarter, quarter])
    parts = [mine, send(other, CORES), send(mine, FAR_X), send(other, FAR_X_CORE)]
    first = placed(arrange_kernel, "arrange", place, parts, [chunk])[0]
    right, left, rows = first, first, first
    order = [(0, 0)]
    own = {0: [first]}
    full, before = None, early[:1]
    for step in range(1, 6):
        if step < 4:
            right, left = send(right, RIGHT), send(left, LEFT)
        elif step == 4:
            right, left = send(right[:128], RIGHT), send(left[128:], LEFT)
        moved = [send(rows, TO_NEXT), send(rows, TO_PREVIOUS)]
        if step < 5:
            rows, right, left = pack([right, left], before)
        before = moved + early[step : step + 1]
        for k, at in order:
            full = place_chunk(place, k, full, own[k], *moved, at, ready if k == 4 else [])
        order = [(-step % N_Z, 0), (step, 1)] if step < 4 else [(4, 0)]
        if step < 4:
            own[-step % N_Z], own[step] = [right], [left]
        else:
            own[4] = [right, left]
    return full.reshape(D, D)


def sample_of(group):
    early = group < 8
    return jnp.where(early, group // 2, group - 4), jnp.where(early, lax.rem(group, 2), 0)


def held_block(side):
    def index(group, ids, *rest):
        sample, half = sample_of(group)
        return (side * 12 + ids[sample], half, 0, 0)

    return pl.BlockSpec((1, 1, QTR, D), index)


def held_rows(ids, stored):
    def kernel(ids, held_ref, out_ref):
        out_ref[...] = held_ref[0, 0]

    return pl.pallas_call(
        kernel,
        grid_spec=pltpu.PrefetchScalarGridSpec(
            num_scalar_prefetch=1,
            grid=(16,),
            in_specs=[held_block(0)],
            out_specs=pl.BlockSpec((QTR, D), lambda g, ids: (g, 0)),
        ),
        out_shape=jax.ShapeDtypeStruct((N_MICRO * ROWS, D), BF),
        compiler_params=PARAMS,
        name="held_rows",
    )(ids, stored)


def boundary_rows(ids, limits, sources, stored):
    def held_at(quarter):
        def index(micro, ids, limits):
            sample, half = sample_of(micro * 4 + quarter)
            return (12 + ids[sample], half, 0, 0)

        return pl.BlockSpec((1, 1, QTR, D), index)

    def source_at(which):
        def index(micro, ids, limits):
            return (jnp.where(limits[13] == which, micro, 0), 0, 0)

        return pl.BlockSpec((1, ROWS, D), index)

    def kernel(ids, limits, s0, s1, s2, h0, h1, h2, h3, out_ref):
        for quarter, held_ref in enumerate((h0, h1, h2, h3)):
            sample, half = sample_of(pl.program_id(0) * 4 + quarter)
            row = lax.broadcasted_iota(jnp.int32, (QTR, 1), 0) + half * QTR
            live = (row < limits[sample]) | (limits[12] == 1)
            rows = slice(quarter * QTR, (quarter + 1) * QTR)
            held = held_ref[0, 0].astype(F32)

            for which, source in enumerate((s0, s1, s2)):

                @pl.when(limits[13] == which)
                def _():
                    value = source[0, rows, :].astype(F32)
                    out_ref[0, rows, :] = jnp.where(live, value, held).astype(BF)

    return pl.pallas_call(
        kernel,
        grid_spec=pltpu.PrefetchScalarGridSpec(
            num_scalar_prefetch=2,
            grid=(N_MICRO,),
            in_specs=[source_at(which) for which in range(3)]
            + [held_at(quarter) for quarter in range(4)],
            out_specs=pl.BlockSpec((1, ROWS, D), lambda m, *tables: (0, m, 0)),
        ),
        out_shape=jax.ShapeDtypeStruct((1, N_MICRO * ROWS, D), BF),
        compiler_params=PARAMS,
        name="boundary_rows",
    )(ids, limits, *sources, stored, stored, stored, stored)


def product_kernel(has, place, *refs):
    rows = N_MICRO * ROWS
    out = refs[-1]

    total = jnp.zeros((CHUNK, QUARTER), F32)
    for source in range(2):
        low, high, early, late = refs[4 * source : 4 * source + 4]
        normed = jnp.concatenate(
            [low[...].reshape(rows, 128), high[...].reshape(rows, 128)], axis=1
        )
        slope = jnp.concatenate(
            [early[...].reshape(rows // 2, QUARTER), late[...].reshape(rows // 2, QUARTER)], axis=0
        )
        total = total + lax.dot_general(
            normed, slope, (((0,), (0,)), ((), ())), preferred_element_type=F32
        )
    for ref in refs[8 : 8 + has]:
        total = total + ref[...].astype(F32)
    out[...] = total.astype(BF)


def product(place, sums, k, part, arrived, wait_for=()):
    piece = pl.BlockSpec((CHUNK, QUARTER), lambda i, place: (0, 0))

    def columns(xh):
        return pl.BlockSpec(
            (N_MICRO, ROWS, 128), lambda i, place: (0, 0, xh * N_Z + lax.rem(place[3] + k, N_Z))
        )

    specs, arrays = [], []
    for normed, early, late in sums:
        specs += [columns(0), columns(1)]
        specs += [pl.BlockSpec((2, ROWS, QUARTER), lambda i, place: (0, 0, part))] * 2
        arrays += [normed, normed, early, late]
    return pl.pallas_call(
        functools.partial(product_kernel, len(arrived)),
        grid_spec=pltpu.PrefetchScalarGridSpec(
            num_scalar_prefetch=1,
            grid=(1,),
            in_specs=specs + [piece] * len(arrived) + [ANY] * len(wait_for),
            out_specs=piece,
        ),
        out_shape=jax.ShapeDtypeStruct((CHUNK, QUARTER), BF),
        compiler_params=PARAMS,
        cost_estimate=COST,
        name=f"product_{k}_{part}",
    )(place, *arrays, *arrived, *wait_for)


def split_x_kernel(place, q0, q1, mine, other):
    for out, xh in ((mine, place[0]), (other, 1 - place[0])):
        rows = part_rows(xh, 128)
        out[:, :QUARTER] = q0[rows, :]
        out[:, QUARTER:] = q1[rows, :]


def split_core_kernel(place, mine, arrived, _, own, other, total):
    total[...] = mine[...].astype(F32) + arrived[...].astype(F32)
    own[...] = total[part_rows(place[2], 64), :]
    other[...] = total[part_rows(1 - place[2], 64), :].astype(BF)


def scatter_grad(place, sums, core, wait_for):
    to_right = [send(product(place, sums, 4, 0, []), RIGHT), None]
    to_left = [None, send(product(place, sums, 4, 1, []), LEFT)]
    for step in range(3, 0, -1):
        for part in (1, 0):
            held = to_right[part]
            to_right[part] = send(
                product(place, sums, step, part, [] if held is None else [held]), RIGHT
            )
            held = to_left[1 - part]
            to_left[1 - part] = send(
                product(place, sums, N_Z - step, 1 - part, [] if held is None else [held]), LEFT
            )
    quarters = [
        product(place, sums, 0, part, [to_right[part], to_left[part]]) for part in range(2)
    ]
    block = ((128, HALF), BF)
    mine, other = placed(split_x_kernel, "split_x", place, quarters, [block, block])
    arrived = send(other, FAR_X)
    own, other, _ = placed(
        split_core_kernel, "split_core", place, [mine, arrived],
        [((64, HALF), F32), ((64, HALF), BF), ((128, HALF), F32)], [wait_for],
    )
    arrived = send(other, CORES).astype(F32)
    return jnp.where(
        core == 0,
        jnp.concatenate([own, arrived], axis=1),
        jnp.concatenate([arrived, own], axis=1),
    )


def live_mask(tab, micro):
    row = lax.broadcasted_iota(jnp.int32, (ROWS, 1), 0)
    if micro < 2:
        limit = jnp.where(row < 64, tab[4 + 2 * micro], tab[5 + 2 * micro])
        return row % 64 < limit
    limit = jnp.zeros((ROWS, 1), jnp.int32)
    for q in range(4):
        limit = jnp.where(row // QTR == q, tab[4 * micro + q], limit)
    return row % QTR < limit


def slot_block(micro):
    return jnp.where((micro >= 0) & (micro < N_MICRO), micro, N_MICRO)


def forward_kernel(tick, names, tab, *refs):
    ref = dict(zip(names, refs))
    micro = tick - tab[1]
    block = tab[0]
    active = (micro >= 0) & (micro < N_MICRO)
    x_ref, normed_ref = ref["x"], ref["normed"]

    if "first" in ref:

        for a, name in ((0, "first"), (1, "first_other")):

            @pl.when(active & (block == 0) & (tab[3] == a))
            def _():
                x_ref[0] = ref[name][...]

    if "core" in ref:

        @pl.when(active & (block % 2 == 1))
        def _():
            x_ref[0] = ref["core"][...]

    if "chip" in ref:

        @pl.when(active & (block % 2 == 0) & (block > 0))
        def _():
            x_ref[0] = ref["chip"][...]

    if "held" in ref:

        for name, mine in (("held", True), ("held_other", False)):

            @pl.when((block == N_SEC - 1) & ((tab[2] == tab[3]) == mine))
            def _():
                live = live_mask(tab, tick - LAST)
                x = jnp.where(live, x_ref[0].astype(F32), ref[name][...].astype(F32))
                x_ref[0] = x.astype(BF)

    @pl.when(active)
    def _():
        values = x_ref[0].astype(F32)
        inverse = lax.rsqrt(jnp.mean(values * values, axis=1, keepdims=True) + EPS)
        normed_ref[0] = (values * inverse * ref["gain"][...].astype(F32)).astype(BF)
        for at in range(0, D, QUARTER):
            cols = slice(at, at + QUARTER)
            mixed = jnp.dot(normed_ref[0], ref["weight"][:, cols], preferred_element_type=F32)
            ref["mixed"][0, :, cols] = mixed.astype(BF)
            output = (x_ref[0, :, cols].astype(F32) + mixed / (1.0 + jnp.exp(-mixed))).astype(BF)
            ref["msg"][:, cols] = output


STASH = {"x": BF, "mixed": BF, "normed": BF}


def forward_tick(tick, tab, blocks, weight, gain, stash, wait_for):
    slot = pl.BlockSpec((1, ROWS, D), lambda i, tab: (slot_block(tick - tab[1]), 0, 0))
    names = [*blocks, "weight", "gain"]
    arrays = [array for array, _ in blocks.values()] + [weight, gain]
    specs = [pl.BlockSpec((ROWS, D), lambda i, tab, at=at: (at, 0)) for _, at in blocks.values()]
    specs += [whole((D, D)), whole((1, D))]
    old = [] if stash is None else list(stash)
    aliases = {1 + len(arrays) + i: 1 + i for i in range(len(old))}
    names += [None] * (len(old) + len(wait_for)) + ["msg", *STASH]
    return pl.pallas_call(
        functools.partial(forward_kernel, tick, names),
        grid_spec=pltpu.PrefetchScalarGridSpec(
            num_scalar_prefetch=1,
            grid=(1,),
            in_specs=specs + [ANY] * (len(old) + len(wait_for)),
            out_specs=[WHOLE] + [slot] * 3,
        ),
        out_shape=[jax.ShapeDtypeStruct((ROWS, D), BF)]
        + [jax.ShapeDtypeStruct((N_MICRO + 1, ROWS, D), kind) for kind in STASH.values()],
        input_output_aliases=aliases,
        compiler_params=PARAMS,
        cost_estimate=COST,
        name=f"forward_{tick}",
    )(tab, *arrays, *old, *wait_for)


def backward_kernel(tick, names, tab, *refs):
    ref = dict(zip(names, refs))
    up_ref, slope_ref, weighted_ref = refs[-3:]
    x_ref, msg_ref = ref["x"], ref["msg"]
    micro = tick - (LAST - tab[1])
    block = tab[0]
    active = (micro >= 0) & (micro < N_MICRO)

    if "given" in ref:
        for a, name in ((1, "given"), (0, "given_other")):

            @pl.when(active & (block == N_SEC - 1) & (tab[3] == a))
            def _():
                given = ref[name][...].astype(F32)
                up_ref[...] = jnp.where(live_mask(tab, tick), given, 0.0).astype(BF)

    if "core" in ref:

        @pl.when(active & (block % 2 == 0))
        def _():
            up_ref[...] = ref["core"][...]

    if "chip" in ref:

        @pl.when(active & (block % 2 == 1) & (block < N_SEC - 1))
        def _():
            up_ref[...] = ref["chip"][...]

    @pl.when(active)
    def _():
        mixed = ref["mixed"][0].astype(F32)
        gated = 1.0 / (1.0 + jnp.exp(-mixed))
        up = up_ref[...].astype(F32)
        slope_ref[...] = (up * gated * (1.0 + mixed * (1.0 - gated))).astype(BF)
        for j, name in enumerate(("slope_0", "slope_1")):
            ref[name][0] = slope_ref[:, half_columns(tab[3] ^ (1 - j))]

    if tick in (LAST + 1, LAST + 3):
        for j in "01":
            leave, old = ref["leave_" + j], ref["old_" + j]
            leave[0] = old[tick - LAST - 1]

            @pl.when(block == 0)
            def _():
                leave[1] = ref["slope_" + j][0]

            @pl.when(block != 0)
            def _():
                leave[1] = old[tick - LAST]

    @pl.when(active & (block > 0))
    def _():
        values = x_ref[0].astype(F32)
        inverse = lax.rsqrt(jnp.mean(values * values, axis=1, keepdims=True) + EPS)
        total = jnp.zeros((ROWS, 128), F32)
        for at in range(0, D, CHUNK):
            cols = slice(at, at + CHUNK)
            back = lax.dot_general(
                ref["weight"][cols, :],
                slope_ref[...],
                (((1,), (1,)), ((), ())),
                preferred_element_type=F32,
            ).T
            weighted = back * ref["gain"][:, cols].astype(F32)
            weighted_ref[:, cols] = weighted
            terms = weighted * x_ref[0, :, cols].astype(F32)
            for part in range(0, CHUNK, 128):
                total = total + terms[:, part : part + 128]
        centre = jnp.sum(total, axis=1, keepdims=True) * (1.0 / D)
        factor = inverse * inverse * inverse * centre
        grad = up_ref[...].astype(F32) + inverse * weighted_ref[...]
        msg_ref[...] = (grad - x_ref[0].astype(F32) * factor).astype(BF)


def backward_tick(tick, tab, blocks, weight, gain, stash, slopes, wait_for):
    def micro_of(tab):
        return tick - (LAST - tab[1])

    read = pl.BlockSpec(
        (1, ROWS, D), lambda i, tab: (jnp.clip(micro_of(tab), 0, N_MICRO - 1), 0, 0)
    )
    slot = pl.BlockSpec((1, ROWS, HALF), lambda i, tab: (slot_block(micro_of(tab)), 0, 0))
    leaving = tick in (LAST + 1, LAST + 3)
    hold = tick < N_MICRO
    names = [*blocks, "weight", "gain", "x", "mixed"]
    arrays = [array for array, _ in blocks.values()] + [weight, gain, *stash]
    specs = [pl.BlockSpec((ROWS, D), lambda i, tab, at=at: (at, 0)) for _, at in blocks.values()]
    specs += [whole((D, D)), whole((1, D)), read, read]
    aliases = {len(arrays) - 1: 3, len(arrays): 4} if hold else {}
    if slopes is not None:
        aliases |= {len(arrays) + 1: 1, len(arrays) + 2: 2}
        arrays += slopes
        names += ["old_0", "old_1"]
        specs += [whole((N_MICRO + 1, ROWS, HALF)) if leaving else ANY] * 2
    names += [None] * len(wait_for) + ["msg", "slope_0", "slope_1"] + [None] * (2 * hold)
    names += ["leave_0", "leave_1"] if leaving else []
    leave = (2, ROWS, HALF)
    kept = jax.ShapeDtypeStruct((N_MICRO + 1, ROWS, HALF), BF)
    out = pl.pallas_call(
        functools.partial(backward_kernel, tick, names),
        grid_spec=pltpu.PrefetchScalarGridSpec(
            num_scalar_prefetch=1,
            grid=(1,),
            in_specs=specs + [ANY] * len(wait_for),
            out_specs=[WHOLE, slot, slot] + [ANY] * (2 * hold) + [whole(leave)] * (2 * leaving),
            scratch_shapes=[pltpu.VMEM((ROWS, D), BF)] * 2 + [pltpu.VMEM((ROWS, D), F32)],
        ),
        out_shape=[jax.ShapeDtypeStruct((ROWS, D), BF), kept, kept]
        + [jax.ShapeDtypeStruct(s.shape, s.dtype) for s in stash if hold]
        + [jax.ShapeDtypeStruct(leave, BF)] * (2 * leaving),
        input_output_aliases=aliases,
        compiler_params=PARAMS,
        cost_estimate=COST,
        name=f"backward_{tick}",
    )(tab, *arrays, *wait_for)
    return out[0], out[3:5] if hold else stash, out[1:3], out[3:] if leaving else []


def hand_on(array, wait_for):
    def kernel(*refs):
        pass

    return pl.pallas_call(
        kernel,
        in_specs=[ANY] * (1 + len(wait_for)),
        out_specs=ANY,
        out_shape=jax.ShapeDtypeStruct(array.shape, array.dtype),
        input_output_aliases={0: 0},
        compiler_params=PARAMS,
        name="hand_on",
    )(array, *wait_for)


def join(pieces):
    def kernel(*refs):
        for i, piece in enumerate(refs[:-1]):
            refs[-1][i] = piece[...]

    return pl.pallas_call(
        kernel,
        grid=(1,),
        in_specs=[pl.BlockSpec((ROWS, D), lambda i: (0, 0))] * len(pieces),
        out_specs=pl.BlockSpec((len(pieces), ROWS, D), lambda i: (0, 0, 0)),
        out_shape=jax.ShapeDtypeStruct((len(pieces), ROWS, D), BF),
        compiler_params=PARAMS,
        name="join",
    )(*pieces)


def body(embedded, out_grad, stored, sample_ids, lengths, weight, gain):
    section = lax.axis_index("section")
    data = lax.axis_index("dp")
    y, a = section // 2, section % 2
    xh, c = data // 16, data % 2
    z = (data // 2) % N_Z
    place = jnp.stack([xh, a, c, z])
    table = jnp.stack([2 * y + c, 3 * y + c, c, a])
    stored = stored.reshape(24, 2, QTR, D)

    first_other = send(embedded, CORES)
    gain_row = jnp.where(a == c, gain, send(gain, TURN))

    limits = jnp.where(a == c, lengths, send(lengths, CORES))
    late_table = jnp.concatenate([table, limits])
    held = held_rows(sample_ids, stored)
    full = gather_weight(place, weight[0], [held], [late_table, gain_row, first_other])
    held_other = send(held, TURN)
    given_other = send(out_grad, CORES)

    stash = slopes = None
    normed, leaving, finals = [], [], []
    up_core, up_chip, down_core, down_chip = {}, {}, {}, {}
    for tick in range(LAST + TICKS):
        if tick < TICKS:
            blocks = {}
            if tick < N_MICRO:
                blocks["first"] = (embedded, tick)
                blocks["first_other"] = (first_other, tick)
            if tick in up_core:
                blocks["core"] = (up_core[tick], 0)
            if tick in up_chip:
                blocks["chip"] = (up_chip[tick], 0)
            if tick >= LAST:
                blocks["held"] = (held, tick - LAST)
                blocks["held_other"] = (held_other, tick - LAST)
            msg, *stash = forward_tick(
                tick,
                late_table if tick >= LAST else table,
                blocks,
                full,
                gain_row,
                stash,
                [held_other, given_other] if tick == LAST - 1 else [],
            )
            if tick >= LAST:
                finals.append(msg)
            if tick < TICKS - 1:
                up_core[tick + 1] = send(msg, UP_CORE)
            if 1 <= tick <= LAST:
                up_chip[tick + 2] = send(msg, UP_CHIP)
            if tick == TICKS - 1:
                normed = [stash[2], send(stash[2], FIRST), send(stash[2], SECOND)]
        if tick >= LAST:
            step = tick - LAST
            blocks = {}
            if step < N_MICRO:
                blocks["given"] = (out_grad, step)
                blocks["given_other"] = (given_other, step)
            if step in down_core:
                blocks["core"] = (down_core[step], 0)
            if step in down_chip:
                blocks["chip"] = (down_chip[step], 0)
            msg, stash[:2], slopes, halves = backward_tick(
                step,
                late_table if step < N_MICRO else table,
                blocks,
                full,
                gain_row,
                stash[:2],
                slopes,
                normed[1:] if step == 8 else list(leaving[0][1:]) if step == LAST + 3 else [],
            )
            if step < TICKS - 1:
                down_core[step + 1] = send(msg, DOWN_CORE)
            if 1 <= step <= LAST:
                down_chip[step + 2] = send(msg, DOWN_CHIP)
            if halves:
                leaving.append((halves[1], send(halves[0], FIRST), send(halves[1], SECOND)))
            if step == LAST:
                normed = [normed[1], jnp.where(a == c, normed[0], normed[2])]

    slopes_there = [*leaving[1][1:], *leaving[0][1:]]
    following = send(hand_on(stash[0], slopes_there), TO_BEFORE)
    finals = join(finals)
    finals_other = send(finals, TURN_LAST)
    last = section == N_SEC - 1
    slopes_of = [(came, jnp.where(a == c, own, second)) for own, came, second in leaving]
    flags = jnp.stack([last, jnp.where(last, jnp.where(a == c, 1, 2), 0)]).astype(jnp.int32)
    boundary = boundary_rows(sample_ids, jnp.concatenate([lengths, flags]), [following, finals, finals_other], stored)
    shard = scatter_grad(place, list(zip(normed, *slopes_of)), c, boundary)
    return (boundary, shard[None])


def solution(mesh):
    in_specs = (
        P("dp", None),
        P("dp", None),
        P("section", None, "dp", None, None),
        P("dp"),
        P("dp"),
        P("section", "dp", None),
        P("section", None),
    )
    out_specs = (P("section", "dp", None), P("section", "dp", None))
    return jax.shard_map(body, mesh=mesh, in_specs=in_specs, out_specs=out_specs, check_vma=False)
```
